32 devices in a mesh: row: 4 (over z), col: 8 (over y, x, core).
Axes of the slice: x: 2, y: 2, z: 4, core: 2. Of those that a mesh axis runs over, the one named last changes fastest.
Arguments:
- compound_pos: float32 [8192, 128], P(('row', 'col')), may hold values from -1.75 to 1.75
- compound_mom: float32 [8192, 128], P(('row', 'col')), may hold values from -6 to 6
- target_pos: float32 [8192, 128], P(('row', 'col')), may hold values from -1.75 to 1.75
- target_mom: float32 [8192, 128], P(('row', 'col')), may hold values from -6 to 6
- tile_rows: int32 [32, 256], P(('row', 'col')), may hold values from 0 to 63, as said below
- tile_cols: int32 [32, 256], P(('row', 'col')), may hold values from 0 to 63, as said below
- tile_count: int32 [32], P(('row', 'col')), may hold values from 32 to 256, as said below
- tile_values: bfloat16 [32, 256, 128, 128], P(('row', 'col')), may hold values from -6 to 6
- tile_weight: bfloat16 [32, 256, 128, 128], P(('row', 'col')), may hold values from 0 to 2, as said below
Outputs:
- compound_out: float32 [8192, 128], P(('row', 'col'))
- compound_mom_out: float32 [8192, 128], P(('row', 'col'))
- target_out: float32 [8192, 128], P(('row', 'col'))
- target_mom_out: float32 [8192, 128], P(('row', 'col'))
The draws below stay inside these ranges and needn't reach their ends.
Inputs may be any that keep to these rules, and one draw needn't show every extreme that they name: `tile_rows`: slots of device d = i * 8 + j name compound blocks from i * 8 * 2 to (i + 1) * 8 * 2 - 1. `tile_cols`: slots of device d = i * 8 + j name target blocks (a * 8 + j) * 2 + c with a < 4 and c < 2. `tile_count`: some device has all 256 slots live in every draw. `tile_weight`: unobserved entries are 0; observed ones are positive.
All inputs are finite; a program needn't handle non-finite values.
Results may differ from the reference program's by a relative error of at most 0.0095.
Values may be sent and summed in bfloat16 or wider, within the bound.
No kernel may reach another device: no remote copies, remote signals or barrier semaphores. Data moves between devices by JAX's collectives and lax.ppermute only.
A program may use at most 128 MiB of HBM per device.

```python
import jax
import jax.numpy as jnp
from jax import lax

BS = 128
K = 128
UB_DEV = 2
VB_DEV = 2
TCAP = 256
LEAPS = 2
ROW_DEVS = 4
COL_DEVS = 8
NUB = 64
NVB = 64
COMPOUNDS = 8192
TARGETS = 8192
DEVICES = 32


def draw_tile_rows(key, part):
    device_ids = jnp.arange(DEVICES, dtype=jnp.int32)[:, None]
    row_group = device_ids // COL_DEVS
    local_pick = jax.random.randint(key, (DEVICES, TCAP), 0, COL_DEVS * UB_DEV, dtype=jnp.int32)
    return (row_group * (COL_DEVS * UB_DEV) + local_pick).astype(jnp.int32)


def draw_tile_cols(key, part):
    device_ids = jnp.arange(DEVICES, dtype=jnp.int32)[:, None]
    col_group = device_ids % COL_DEVS
    local_pick = jax.random.randint(key, (DEVICES, TCAP), 0, ROW_DEVS * VB_DEV, dtype=jnp.int32)
    holder_row = local_pick // VB_DEV
    within = local_pick % VB_DEV
    return ((holder_row * COL_DEVS + col_group) * VB_DEV + within).astype(jnp.int32)


def draw_tile_count(key, part):
    lowest = max(1, TCAP // 8)
    counts = jax.random.randint(key, (DEVICES,), lowest, 7 * TCAP // 8 + 1, dtype=jnp.int32)
    busiest = jax.random.randint(jax.random.fold_in(key, 7), (), 0, DEVICES, dtype=jnp.int32)
    return jnp.where(jnp.arange(DEVICES, dtype=jnp.int32) == busiest, TCAP, counts).astype(jnp.int32)


def draw_tile_weight(key, part):
    shape = (DEVICES, TCAP, BS, BS)
    seen = jax.random.bernoulli(jax.random.fold_in(key, 11), 0.5, shape).astype(jnp.float32)
    spread = jax.random.uniform(jax.random.fold_in(key, 13), shape, jnp.float32, 0.0, 1.0)
    level = jnp.exp(jnp.log(0.5) + spread * (jnp.log(2.0) - jnp.log(0.5)))
    return (seen * level).astype(jnp.bfloat16)


def shard_levels(stream_key, dims, shards, least, top_value):
    def one(position, parts):
        draws = jax.random.uniform(jax.random.fold_in(jax.random.fold_in(stream_key, 6), position), (parts,), jnp.float32, least / len(shards), top_value / len(shards))
        return jnp.repeat(jnp.exp(draws), dims[position] // parts).reshape((-1,) + (1,) * (len(dims) - position - 1))

    factor_of = one(*shards[0])
    for cut in shards[1:]:
        factor_of = factor_of * one(*cut)
    return factor_of


def centred(stream_key, dims, width, bound, split=(), kind=jnp.bfloat16):
    values = width * jax.random.normal(stream_key, dims, jnp.float32)
    if split:
        values = values * shard_levels(stream_key, dims, split, -0.22, 0.18)
    return jnp.clip(values, -bound, bound).astype(kind)


def setup_inputs(seed: int = 0) -> dict:
    streams_of = jax.random.split(jax.random.key(seed), 10)
    return {
        "compound_pos": centred(streams_of[0], (COMPOUNDS, K), 0.3, 1.75, ((0, 32),), jnp.float32),
        "compound_mom": centred(streams_of[1], (COMPOUNDS, K), 1.0, 6.0, ((0, 32),), jnp.float32),
        "target_pos": centred(streams_of[2], (TARGETS, K), 0.3, 1.75, ((0, 32),), jnp.float32),
        "target_mom": centred(streams_of[3], (TARGETS, K), 1.0, 6.0, ((0, 32),), jnp.float32),
        "tile_rows": draw_tile_rows(jax.random.fold_in(streams_of[9], 71), 0),
        "tile_cols": draw_tile_cols(jax.random.fold_in(streams_of[9], 71), 0),
        "tile_count": draw_tile_count(jax.random.fold_in(streams_of[9], 71), 0),
        "tile_values": centred(streams_of[7], (DEVICES, TCAP, BS, BS), 1.0, 6.0, ((0, 32),)),
        "tile_weight": draw_tile_weight(jax.random.fold_in(streams_of[9], 71), 0),
    }


degrees_free = 4.0
noise_scale = 0.5
prior_weight = 1.0
step_size = 0.01


def all_forces(compound_now, target_now, tile_rows, tile_cols, tile_count, tile_values, tile_weight):
    comp_low = lax.optimization_barrier(compound_now.astype(jnp.bfloat16)).astype(jnp.float32).reshape(NUB, BS, K)
    targ_low = lax.optimization_barrier(target_now.astype(jnp.bfloat16)).astype(jnp.float32).reshape(NVB, BS, K)

    def visit(carry, pieces):
        row_ids, col_ids, live_count, values, entry_weight = pieces
        comp_rows = comp_low[row_ids]
        targ_rows = targ_low[col_ids]
        predicted = jnp.einsum("tik,tjk->tij", comp_rows, targ_rows, precision=lax.Precision.HIGHEST)
        resid_tile = values.astype(jnp.float32) - predicted
        weights = (degrees_free + 1.0) * resid_tile / (degrees_free * noise_scale * noise_scale + resid_tile * resid_tile)
        alive_mask = (jnp.arange(TCAP, dtype=jnp.int32) < live_count).astype(jnp.float32)
        kept_mask = entry_weight.astype(jnp.float32) * alive_mask[:, None, None]
        scaled = lax.optimization_barrier((weights * kept_mask).astype(jnp.bfloat16)).astype(jnp.float32)
        comp_part = jnp.einsum("tij,tjk->tik", scaled, targ_rows, precision=lax.Precision.HIGHEST)
        targ_part = jnp.einsum("tij,tik->tjk", scaled, comp_rows, precision=lax.Precision.HIGHEST)
        return (carry[0].at[row_ids].add(comp_part), carry[1].at[col_ids].add(targ_part)), None

    start = (jnp.zeros((NUB, BS, K), jnp.float32), jnp.zeros((NVB, BS, K), jnp.float32))
    (comp_grad, targ_grad), unused = lax.scan(visit, start, (tile_rows, tile_cols, tile_count, tile_values, tile_weight))
    comp_force = comp_grad.reshape(COMPOUNDS, K) - prior_weight * compound_now
    targ_force = targ_grad.reshape(TARGETS, K) - prior_weight * target_now
    return comp_force, targ_force


def reference(compound_pos, compound_mom, target_pos, target_mom, tile_rows, tile_cols, tile_count, tile_values, tile_weight):
    def forces(comp_now, targ_now):
        return all_forces(comp_now, targ_now, tile_rows, tile_cols, tile_count, tile_values, tile_weight)

    comp_place, targ_place = compound_pos, target_pos
    comp_speed, targ_speed = compound_mom, target_mom
    comp_force, targ_force = forces(comp_place, targ_place)
    for leap_index in range(LEAPS):
        comp_speed = comp_speed + 0.5 * step_size * comp_force
        targ_speed = targ_speed + 0.5 * step_size * targ_force
        comp_place = comp_place + step_size * comp_speed
        targ_place = targ_place + step_size * targ_speed
        comp_force, targ_force = forces(comp_place, targ_place)
        comp_speed = comp_speed + 0.5 * step_size * comp_force
        targ_speed = targ_speed + 0.5 * step_size * targ_force
    return (comp_place, comp_speed, targ_place, targ_speed)
```

```python
import functools
import math

import jax
import jax.numpy as jnp
from jax import lax
from jax.experimental import pallas as pl
from jax.experimental.pallas import tpu as pltpu
from jax.sharding import PartitionSpec as P

LEAPS = 2


degrees_free = 4.0
noise_scale = 0.5
prior_weight = 1.0
step_size = 0.01

VMEM_BYTES = 58 * 2**20


def force_kernel(cols, rows, chunk, depth, slot_ref, live_ref, *refs):
    comp_refs, refs = refs[:cols], refs[cols:]
    targ_refs, refs = refs[:rows], refs[rows:]
    values_hbm, weight_hbm, refs = refs[0], refs[1], refs[2:]
    comp_outs, refs = refs[:cols], refs[cols:]
    targ_outs, refs = refs[:rows], refs[rows:]
    values_buf, weight_buf, pred, total, targ_acc, sems = refs
    side = values_buf.shape[2]
    comp_per = comp_refs[0].shape[0] // side
    targ_per = targ_refs[0].shape[0] // side
    targ_group = rows * targ_per
    chunks = (live_ref[0] + chunk - 1) // chunk

    def copies(index):
        spot = lax.rem(index, depth)
        source = pl.ds(index * chunk, chunk)
        return (
            pltpu.make_async_copy(values_hbm.at[source], values_buf.at[spot], sems.at[0, spot]),
            pltpu.make_async_copy(weight_hbm.at[source], weight_buf.at[spot], sems.at[1, spot]),
        )

    def fetch(index):
        @pl.when(index < chunks)
        def _():
            for copy in copies(index):
                copy.start()

    lax.fori_loop(0, depth, lambda index, unused: (fetch(index), unused)[1], 0)

    zeros = jnp.zeros((side, side), jnp.float32)
    for col in range(cols):
        comp = comp_refs[col][...]
        for row in range(rows):
            block = lax.dot_general(
                comp,
                targ_refs[row][...],
                (((1,), (1,)), ((), ())),
                preferred_element_type=jnp.float32,
            ).astype(pred.dtype)
            for i in range(comp_per):
                for j in range(targ_per):
                    pair = (col * comp_per + i) * targ_group + row * targ_per + j
                    pred[pair] = block[i * side : (i + 1) * side, j * side : (j + 1) * side]
                    total[pair] = zeros

    one = jnp.asarray(degrees_free * noise_scale * noise_scale, pred.dtype)

    def visit_chunk(index, unused):
        spot = lax.rem(index, depth)
        for copy in copies(index):
            copy.wait()

        def visit(slot, unused):
            pair = slot_ref[index * chunk + slot]
            resid = values_buf[spot, slot] - pred[pair]
            scaled = resid / (one + resid * resid) * weight_buf[spot, slot]
            total[pair] += scaled.astype(jnp.float32)
            return unused

        lax.fori_loop(0, chunk, visit, 0, unroll=4)
        fetch(index + depth)
        return unused

    lax.fori_loop(0, chunks, visit_chunk, 0)

    gain = degrees_free + 1.0
    for col in range(cols):
        comp = comp_refs[col][...]
        comp_sum = None
        for row in range(rows):
            first = (col * comp_per) * targ_group + row * targ_per
            tiles = [
                jnp.concatenate(
                    [total[first + i * targ_group + j] for j in range(targ_per)], axis=1
                )
                for i in range(comp_per)
            ]
            weights = jnp.concatenate(tiles, axis=0).astype(jnp.bfloat16)
            part = jnp.dot(weights, targ_refs[row][...], preferred_element_type=jnp.float32)
            comp_sum = part if comp_sum is None else comp_sum + part
            targ_part = lax.dot_general(
                comp, weights, (((0,), (0,)), ((), ())), preferred_element_type=jnp.float32
            )
            if col == 0:
                targ_acc[row] = targ_part
            elif col < cols - 1:
                targ_acc[row] += targ_part
            else:
                whole = (targ_acc[row] + targ_part) * gain
                targ_outs[row][...] = whole.T.astype(targ_outs[row].dtype)
        comp_outs[col][...] = (comp_sum * gain).astype(comp_outs[col].dtype)


def local_grads(slots, live, comp_blocks, targ_blocks, values, weight):
    cols, rows = len(comp_blocks), len(targ_blocks)
    slot_count, side, rank = values.shape
    comp_rows, rank = comp_blocks[0].shape
    targ_rows = targ_blocks[0].shape[0]
    pairs = cols * (comp_rows // side) * rows * (targ_rows // side)
    chunk = math.gcd(slot_count, 16)
    room = VMEM_BYTES - 8 * 2**20 - (pairs + 1) * side * side * 6
    depth = max(2, min(slot_count // chunk, room // (chunk * side * side * 4)))
    smem = pl.BlockSpec(memory_space=pltpu.SMEM)
    vmem = pl.BlockSpec(memory_space=pltpu.VMEM)
    hbm = pl.BlockSpec(memory_space=pl.ANY)

    def shapes(count, shape):
        return [
            jax.ShapeDtypeStruct(shape, jnp.float32 if n == 0 else jnp.bfloat16)
            for n in range(count)
        ]

    outs = pl.pallas_call(
        functools.partial(force_kernel, cols, rows, chunk, depth),
        out_shape=shapes(cols, (comp_rows, rank)) + shapes(rows, (targ_rows, rank)),
        in_specs=[smem, smem] + [vmem] * (cols + rows) + [hbm, hbm],
        out_specs=[vmem] * (cols + rows),
        scratch_shapes=[
            pltpu.VMEM((depth, chunk, side, side), values.dtype),
            pltpu.VMEM((depth, chunk, side, side), weight.dtype),
            pltpu.VMEM((pairs + 1, side, side), jnp.bfloat16),
            pltpu.VMEM((pairs + 1, side, side), jnp.float32),
            pltpu.VMEM((rows, rank, targ_rows), jnp.float32),
            pltpu.SemaphoreType.DMA((2, depth)),
        ],
        compiler_params=pltpu.CompilerParams(vmem_limit_bytes=VMEM_BYTES),
        name="tile_force",
    )(slots, live, *comp_blocks, *targ_blocks, values, weight)
    return outs[:cols], outs[cols:]


def swap(block, axis, offset):
    size = lax.axis_size(axis)
    return lax.ppermute(block, axis, [(i, i ^ offset) for i in range(size)])


def spread(block, axis):
    return [block] + [swap(block, axis, offset) for offset in range(1, lax.axis_size(axis))]


def collect(blocks, axis):
    got = [swap(block, axis, offset) for offset, block in enumerate(blocks) if offset]
    whole = blocks[0]
    for block in got:
        whole = whole + block.astype(jnp.float32)
    return whole


def body(
    compound_pos,
    compound_mom,
    target_pos,
    target_mom,
    tile_rows,
    tile_cols,
    tile_count,
    tile_values,
    tile_weight,
):
    side = tile_values.shape[2]
    comp_per = compound_pos.shape[0] // side
    targ_per = target_pos.shape[0] // side
    cols, rows = lax.axis_size("col"), lax.axis_size("row")
    col_index, row_index = lax.axis_index("col"), lax.axis_index("row")
    assert cols & (cols - 1) == 0 and rows & (rows - 1) == 0
    comp_local = tile_rows[0] - row_index * (cols * comp_per)
    comp_place = ((comp_local // comp_per) ^ col_index) * comp_per + comp_local % comp_per
    holder = tile_cols[0] // targ_per // cols
    targ_place = (holder ^ row_index) * targ_per + tile_cols[0] % targ_per
    targ_group = rows * targ_per
    alive = jnp.arange(tile_values.shape[1], dtype=jnp.int32) < tile_count[0]
    spare = cols * comp_per * targ_group
    slots = jnp.where(alive, comp_place * targ_group + targ_place, spare)

    def forces(comp, targ):
        comp_blocks = spread(comp.astype(jnp.bfloat16), "col")
        targ_blocks = spread(targ.astype(jnp.bfloat16), "row")
        comp_parts, targ_parts = local_grads(
            slots, tile_count, comp_blocks, targ_blocks, tile_values[0], tile_weight[0]
        )
        comp_sum = collect(comp_parts, "col")
        targ_sum = collect(targ_parts, "row")
        return comp_sum - prior_weight * comp, targ_sum - prior_weight * targ

    places = (compound_pos, target_pos)
    speeds = (compound_mom, target_mom)
    push = forces(*places)
    for leap in range(LEAPS):
        scale = (0.5 if leap == 0 else 1.0) * step_size
        speeds = tuple(p + scale * f for p, f in zip(speeds, push))
        places = tuple(q + step_size * p for q, p in zip(places, speeds))
        push = forces(*places)
    speeds = tuple(p + 0.5 * step_size * f for p, f in zip(speeds, push))
    return (places[0], speeds[0], places[1], speeds[1])


def solution(mesh):
    split = P(("row", "col"), None)
    tiles = P(("row", "col"), None, None, None)
    return jax.shard_map(
        body,
        mesh=mesh,
        in_specs=(split,) * 6 + (P(("row", "col")), tiles, tiles),
        out_specs=(split,) * 4,
        check_vma=False,
    )
```

```python
import functools
import math

import jax
import jax.numpy as jnp
from jax import lax
from jax.experimental import pallas as pl
from jax.experimental.pallas import tpu as pltpu
from jax.sharding import PartitionSpec as P

LEAPS = 2


degrees_free = 4.0
noise_scale = 0.5
prior_weight = 1.0
step_size = 0.01

VMEM_BYTES = 58 * 2**20


def force_kernel(cols, rows, chunk, depth, slot_ref, live_ref, place_ref, *refs):
    comp_refs, refs = refs[:cols], refs[cols:]
    targ_refs, refs = refs[:rows], refs[rows:]
    values_hbm, weight_hbm, refs = refs[0], refs[1], refs[2:]
    comp_out, targ_out, refs = refs[0], refs[1], refs[2:]
    values_buf, weight_buf, pred, total, targ_acc, sems = refs
    side = values_buf.shape[2]
    comp_per = comp_refs[0].shape[0] // side
    targ_per = targ_refs[0].shape[0] // side
    targ_group = rows * targ_per
    chunks = (live_ref[0] + chunk - 1) // chunk

    def copies(index):
        spot = lax.rem(index, depth)
        source = pl.ds(index * chunk, chunk)
        return (
            pltpu.make_async_copy(values_hbm.at[source], values_buf.at[spot], sems.at[0, spot]),
            pltpu.make_async_copy(weight_hbm.at[source], weight_buf.at[spot], sems.at[1, spot]),
        )

    def fetch(index):
        @pl.when(index < chunks)
        def _():
            for copy in copies(index):
                copy.start()

    lax.fori_loop(0, depth, lambda index, unused: (fetch(index), unused)[1], 0)

    zeros = jnp.zeros((side, side), jnp.float32)
    for col in range(cols):
        comp = comp_refs[col][...]
        for row in range(rows):
            block = lax.dot_general(
                comp,
                targ_refs[row][...],
                (((1,), (1,)), ((), ())),
                preferred_element_type=jnp.float32,
            ).astype(pred.dtype)
            for i in range(comp_per):
                for j in range(targ_per):
                    pair = (col * comp_per + i) * targ_group + row * targ_per + j
                    pred[pair] = block[i * side : (i + 1) * side, j * side : (j + 1) * side]
                    total[pair] = zeros

    one = jnp.asarray(degrees_free * noise_scale * noise_scale, pred.dtype)

    def visit_chunk(index, unused):
        spot = lax.rem(index, depth)
        for copy in copies(index):
            copy.wait()

        def visit(slot, unused):
            pair = slot_ref[index * chunk + slot]
            resid = values_buf[spot, slot] - pred[pair]
            scaled = resid / (one + resid * resid) * weight_buf[spot, slot]
            total[pair] += scaled.astype(jnp.float32)
            return unused

        lax.fori_loop(0, chunk, visit, 0, unroll=4)
        fetch(index + depth)
        return unused

    lax.fori_loop(0, chunks, visit_chunk, 0)

    gain = degrees_free + 1.0
    for col in range(cols):
        comp = comp_refs[col][...]
        comp_sum = None
        for row in range(rows):
            first = (col * comp_per) * targ_group + row * targ_per
            tiles = [
                jnp.concatenate(
                    [total[first + i * targ_group + j] for j in range(targ_per)], axis=1
                )
                for i in range(comp_per)
            ]
            weights = jnp.concatenate(tiles, axis=0).astype(jnp.bfloat16)
            part = jnp.dot(weights, targ_refs[row][...], preferred_element_type=jnp.float32)
            comp_sum = part if comp_sum is None else comp_sum + part
            targ_part = lax.dot_general(
                comp, weights, (((0,), (0,)), ((), ())), preferred_element_type=jnp.float32
            )
            if col == 0:
                targ_acc[row] = targ_part
            elif col < cols - 1:
                targ_acc[row] += targ_part
            else:
                whole = (targ_acc[row] + targ_part) * gain
                targ_out[place_ref[1] ^ row] = whole.T.astype(targ_out.dtype)
        comp_out[place_ref[0] ^ col] = (comp_sum * gain).astype(comp_out.dtype)


def local_grads(slots, live, place, comp_blocks, targ_blocks, values, weight):
    cols, rows = len(comp_blocks), len(targ_blocks)
    slot_count, side, rank = values.shape
    comp_rows, rank = comp_blocks[0].shape
    targ_rows = targ_blocks[0].shape[0]
    pairs = cols * (comp_rows // side) * rows * (targ_rows // side)
    chunk = math.gcd(slot_count, 16)
    room = VMEM_BYTES - 8 * 2**20 - (pairs + 1) * side * side * 6
    depth = max(2, min(slot_count // chunk, room // (chunk * side * side * 4)))
    smem = pl.BlockSpec(memory_space=pltpu.SMEM)
    vmem = pl.BlockSpec(memory_space=pltpu.VMEM)
    hbm = pl.BlockSpec(memory_space=pl.ANY)

    return pl.pallas_call(
        functools.partial(force_kernel, cols, rows, chunk, depth),
        out_shape=(
            jax.ShapeDtypeStruct((cols, comp_rows, rank), jnp.bfloat16),
            jax.ShapeDtypeStruct((rows, targ_rows, rank), jnp.bfloat16),
        ),
        in_specs=[smem] * 3 + [vmem] * (cols + rows) + [hbm, hbm],
        out_specs=(vmem, vmem),
        scratch_shapes=[
            pltpu.VMEM((depth, chunk, side, side), values.dtype),
            pltpu.VMEM((depth, chunk, side, side), weight.dtype),
            pltpu.VMEM((pairs + 1, side, side), jnp.bfloat16),
            pltpu.VMEM((pairs + 1, side, side), jnp.float32),
            pltpu.VMEM((rows, rank, targ_rows), jnp.float32),
            pltpu.SemaphoreType.DMA((2, depth)),
        ],
        compiler_params=pltpu.CompilerParams(vmem_limit_bytes=VMEM_BYTES),
        name="tile_force",
    )(slots, live, place, *comp_blocks, *targ_blocks, values, weight)


def swap(block, axis, offset):
    size = lax.axis_size(axis)
    return lax.ppermute(block, axis, [(i, i ^ offset) for i in range(size)])


def spread(block, axis):
    return [block] + [swap(block, axis, offset) for offset in range(1, lax.axis_size(axis))]


def collect(blocks, axis):
    got = lax.all_to_all(blocks, axis, 0, 0)
    return jnp.sum(got.astype(jnp.float32), axis=0)


def body(
    compound_pos,
    compound_mom,
    target_pos,
    target_mom,
    tile_rows,
    tile_cols,
    tile_count,
    tile_values,
    tile_weight,
):
    side = tile_values.shape[2]
    comp_per = compound_pos.shape[0] // side
    targ_per = target_pos.shape[0] // side
    cols, rows = lax.axis_size("col"), lax.axis_size("row")
    col_index, row_index = lax.axis_index("col"), lax.axis_index("row")
    assert cols & (cols - 1) == 0 and rows & (rows - 1) == 0
    comp_local = tile_rows[0] - row_index * (cols * comp_per)
    comp_place = ((comp_local // comp_per) ^ col_index) * comp_per + comp_local % comp_per
    holder = tile_cols[0] // targ_per // cols
    targ_place = (holder ^ row_index) * targ_per + tile_cols[0] % targ_per
    targ_group = rows * targ_per
    alive = jnp.arange(tile_values.shape[1], dtype=jnp.int32) < tile_count[0]
    spare = cols * comp_per * targ_group
    slots = jnp.where(alive, comp_place * targ_group + targ_place, spare)

    place = jnp.stack([col_index, row_index]).astype(jnp.int32)

    def forces(comp, targ):
        comp_blocks = spread(comp.astype(jnp.bfloat16), "col")
        targ_blocks = spread(targ.astype(jnp.bfloat16), "row")
        comp_parts, targ_parts = local_grads(
            slots, tile_count, place, comp_blocks, targ_blocks, tile_values[0], tile_weight[0]
        )
        comp_sum = collect(comp_parts, "col")
        targ_sum = collect(targ_parts, "row")
        return comp_sum - prior_weight * comp, targ_sum - prior_weight * targ

    places = (compound_pos, target_pos)
    speeds = (compound_mom, target_mom)
    push = forces(*places)
    for leap in range(LEAPS):
        scale = (0.5 if leap == 0 else 1.0) * step_size
        speeds = tuple(p + scale * f for p, f in zip(speeds, push))
        places = tuple(q + step_size * p for q, p in zip(places, speeds))
        push = forces(*places)
    speeds = tuple(p + 0.5 * step_size * f for p, f in zip(speeds, push))
    return (places[0], speeds[0], places[1], speeds[1])


def solution(mesh):
    split = P(("row", "col"), None)
    tiles = P(("row", "col"), None, None, None)
    return jax.shard_map(
        body,
        mesh=mesh,
        in_specs=(split,) * 6 + (P(("row", "col")), tiles, tiles),
        out_specs=(split,) * 4,
        check_vma=False,
    )
```

```python
import functools
import math

import jax
import jax.numpy as jnp
from jax import lax
from jax.experimental import pallas as pl
from jax.experimental.pallas import tpu as pltpu
from jax.sharding import PartitionSpec as P

LEAPS = 2


degrees_free = 4.0
noise_scale = 0.5
prior_weight = 1.0
step_size = 0.01


def force_kernel(cols, rows, chunk, depth, slot_ref, live_ref, *refs):
    comp_refs, refs = refs[:cols], refs[cols:]
    targ_refs, refs = refs[:rows], refs[rows:]
    values_hbm, weight_hbm, refs = refs[0], refs[1], refs[2:]
    comp_keep, comp_send, refs = refs[0], refs[1], refs[2:]
    targ_outs, refs = refs[:rows], refs[rows:]
    values_buf, weight_buf, pred, total, comp_flip, targ_flip, targ_acc, sems = refs
    side = values_buf.shape[2]
    comp_per = comp_refs[0].shape[0] // side
    targ_per = targ_refs[0].shape[0] // side
    targ_group = rows * targ_per
    chunks = (live_ref[0] + chunk - 1) // chunk

    def copies(index):
        spot = lax.rem(index, depth)
        source = pl.ds(index * chunk, chunk)
        return (
            pltpu.make_async_copy(values_hbm.at[source], values_buf.at[spot], sems.at[0, spot]),
            pltpu.make_async_copy(weight_hbm.at[source], weight_buf.at[spot], sems.at[1, spot]),
        )

    def fetch(index):
        @pl.when(index < chunks)
        def _():
            for copy in copies(index):
                copy.start()

    lax.fori_loop(0, depth, lambda index, unused: (fetch(index), unused)[1], 0)

    comp_rows, targ_rows = comp_per * side, targ_per * side
    zeros = jnp.zeros((side, side), jnp.float32)
    for row in range(rows):
        targ_flip[:, row * targ_rows : (row + 1) * targ_rows] = targ_refs[row][...].T
    for col in range(cols):
        comp = comp_refs[col][...]
        comp_flip[:, col * comp_rows : (col + 1) * comp_rows] = comp.T
        for row in range(rows):
            block = jnp.dot(
                comp,
                targ_flip[:, row * targ_rows : (row + 1) * targ_rows],
                preferred_element_type=jnp.float32,
            ).astype(pred.dtype)
            for i in range(comp_per):
                for j in range(targ_per):
                    pair = (col * comp_per + i) * targ_group + row * targ_per + j
                    pred[pair] = block[i * side : (i + 1) * side, j * side : (j + 1) * side]
                    total[pair] = zeros

    one = jnp.asarray(degrees_free * noise_scale * noise_scale, pred.dtype)

    def visit_chunk(index, unused):
        spot = lax.rem(index, depth)
        for copy in copies(index):
            copy.wait()

        def visit(slot, unused):
            pair = slot_ref[index * chunk + slot]
            resid = values_buf[spot, slot] - pred[pair]
            inverse = pl.reciprocal(one + resid * resid, approx=True)
            scaled = resid * weight_buf[spot, slot] * inverse
            total[pair] += scaled.astype(jnp.float32)
            return unused

        lax.fori_loop(0, chunk, visit, 0, unroll=4)
        fetch(index + depth)
        return unused

    lax.fori_loop(0, chunks, visit_chunk, 0)

    gain = degrees_free + 1.0
    for col in range(cols):
        comp = comp_flip[:, col * comp_rows : (col + 1) * comp_rows]
        comp_sum = None
        for row in range(rows):
            first = (col * comp_per) * targ_group + row * targ_per
            tiles = [
                jnp.concatenate(
                    [total[first + i * targ_group + j] for j in range(targ_per)], axis=1
                )
                for i in range(comp_per)
            ]
            weights = jnp.concatenate(tiles, axis=0).astype(jnp.bfloat16)
            part = jnp.dot(weights, targ_refs[row][...], preferred_element_type=jnp.float32)
            comp_sum = part if comp_sum is None else comp_sum + part
            targ_part = jnp.dot(comp, weights, preferred_element_type=jnp.float32)
            if col == 0:
                targ_acc[row] = targ_part
            elif col < cols - 1:
                targ_acc[row] += targ_part
            else:
                whole = (targ_acc[row] + targ_part) * gain
                targ_outs[row][...] = whole.T.astype(targ_outs[row].dtype)
        comp_out = comp_send if col % 2 else comp_keep
        comp_out[col // 2] = (comp_sum * gain).astype(comp_out.dtype)


def local_grads(slots, live, comp_blocks, targ_blocks, values, weight):
    cols, rows = len(comp_blocks), len(targ_blocks)
    slot_count, side, rank = values.shape
    comp_rows, rank = comp_blocks[0].shape
    targ_rows = targ_blocks[0].shape[0]
    pairs = cols * (comp_rows // side) * rows * (targ_rows // side)
    chunk = math.gcd(slot_count, 16)
    tile = side * side
    depth = min(slot_count // chunk, 4)
    held = (pairs + 1) * tile * 6 + depth * chunk * tile * 4
    held += (cols * comp_rows + rows * targ_rows) * rank * 8
    smem = pl.BlockSpec(memory_space=pltpu.SMEM)
    vmem = pl.BlockSpec(memory_space=pltpu.VMEM)
    hbm = pl.BlockSpec(memory_space=pl.ANY)

    comp_shape = jax.ShapeDtypeStruct((cols // 2, comp_rows, rank), jnp.bfloat16)
    targ_shapes = [
        jax.ShapeDtypeStruct((targ_rows, rank), jnp.bfloat16 if row else jnp.float32)
        for row in range(rows)
    ]
    outs = pl.pallas_call(
        functools.partial(force_kernel, cols, rows, chunk, depth),
        out_shape=[comp_shape, comp_shape] + targ_shapes,
        in_specs=[smem, smem] + [vmem] * (cols + rows) + [hbm, hbm],
        out_specs=[vmem] * (2 + rows),
        scratch_shapes=[
            pltpu.VMEM((depth, chunk, side, side), values.dtype),
            pltpu.VMEM((depth, chunk, side, side), weight.dtype),
            pltpu.VMEM((pairs + 1, side, side), jnp.bfloat16),
            pltpu.VMEM((pairs + 1, side, side), jnp.float32),
            pltpu.VMEM((rank, cols * comp_rows), jnp.bfloat16),
            pltpu.VMEM((rank, rows * targ_rows), jnp.bfloat16),
            pltpu.VMEM((rows, rank, targ_rows), jnp.float32),
            pltpu.SemaphoreType.DMA((2, depth)),
        ],
        compiler_params=pltpu.CompilerParams(vmem_limit_bytes=held + 4 * 2**20),
        name="tile_force",
    )(slots, live, *comp_blocks, *targ_blocks, values, weight)
    return outs[0], outs[1], outs[2:]


def swap(block, axis, offset):
    size = lax.axis_size(axis)
    return lax.ppermute(block, axis, [(i, i ^ offset) for i in range(size)])


def spread(block, axis):
    return [block] + [swap(block, axis, offset) for offset in range(1, lax.axis_size(axis))]


def spread_pairs(block, axis):
    firsts = [block]
    firsts += [swap(block, axis, offset) for offset in range(2, lax.axis_size(axis), 2)]
    return [each for first in firsts for each in (first, swap(first, axis, 1))]


def collect(blocks, axis):
    got = [swap(block, axis, offset) for offset, block in enumerate(blocks) if offset]
    whole = blocks[0].astype(jnp.float32)
    for block in got:
        whole = whole + block.astype(jnp.float32)
    return whole


def collect_pairs(keep, send, axis):
    got = swap(send, axis, 1)
    both = [
        keep[n].astype(jnp.float32) + got[n].astype(jnp.float32) for n in range(keep.shape[0])
    ]
    whole = both[0]
    for n, block in enumerate(both[1:]):
        whole = whole + swap(block.astype(keep.dtype), axis, 2 * n + 2).astype(jnp.float32)
    return whole


def body(
    compound_pos,
    compound_mom,
    target_pos,
    target_mom,
    tile_rows,
    tile_cols,
    tile_count,
    tile_values,
    tile_weight,
):
    side = tile_values.shape[2]
    comp_per = compound_pos.shape[0] // side
    targ_per = target_pos.shape[0] // side
    cols, rows = lax.axis_size("col"), lax.axis_size("row")
    col_index, row_index = lax.axis_index("col"), lax.axis_index("row")
    assert cols & (cols - 1) == 0 and rows & (rows - 1) == 0
    comp_local = tile_rows[0] - row_index * (cols * comp_per)
    comp_place = ((comp_local // comp_per) ^ col_index) * comp_per + comp_local % comp_per
    holder = tile_cols[0] // targ_per // cols
    targ_place = (holder ^ row_index) * targ_per + tile_cols[0] % targ_per
    targ_group = rows * targ_per
    alive = jnp.arange(tile_values.shape[1], dtype=jnp.int32) < tile_count[0]
    spare = cols * comp_per * targ_group
    slots = jnp.where(alive, comp_place * targ_group + targ_place, spare)

    def forces(comp, targ):
        comp_blocks = spread_pairs(comp.astype(jnp.bfloat16), "col")
        targ_blocks = spread(targ.astype(jnp.bfloat16), "row")
        comp_keep, comp_send, targ_parts = local_grads(
            slots, tile_count, comp_blocks, targ_blocks, tile_values[0], tile_weight[0]
        )
        comp_sum = collect_pairs(comp_keep, comp_send, "col")
        targ_sum = collect(targ_parts, "row")
        return comp_sum - prior_weight * comp, targ_sum - prior_weight * targ

    places = (compound_pos, target_pos)
    speeds = (compound_mom, target_mom)
    push = forces(*places)
    for leap in range(LEAPS):
        scale = (0.5 if leap == 0 else 1.0) * step_size
        speeds = tuple(p + scale * f for p, f in zip(speeds, push))
        places = tuple(q + step_size * p for q, p in zip(places, speeds))
        push = forces(*places)
    speeds = tuple(p + 0.5 * step_size * f for p, f in zip(speeds, push))
    return (places[0], speeds[0], places[1], speeds[1])


def solution(mesh):
    split = P(("row", "col"), None)
    tiles = P(("row", "col"), None, None, None)
    return jax.shard_map(
        body,
        mesh=mesh,
        in_specs=(split,) * 6 + (P(("row", "col")), tiles, tiles),
        out_specs=(split,) * 4,
        check_vma=False,
    )
```

```python
import functools
import math

import jax
import jax.numpy as jnp
from jax import lax
from jax.experimental import pallas as pl
from jax.experimental.pallas import tpu as pltpu
from jax.sharding import PartitionSpec as P

LEAPS = 2
GROUP = 4


degrees_free = 4.0
noise_scale = 0.5
prior_weight = 1.0
step_size = 0.01


def force_kernel(cols, rows, chunk, depth, slot_ref, live_ref, *refs):
    comp_firsts, comp_seconds, refs = refs[: cols // 2], refs[cols // 2], refs[cols // 2 + 1 :]
    targ_refs, refs = refs[:rows], refs[rows:]
    values_hbm, weight_hbm, refs = refs[0], refs[1], refs[2:]
    comp_keep, comp_send, refs = refs[0], refs[1], refs[2:]
    targ_outs, refs = refs[:rows], refs[rows:]
    values_buf, weight_buf, pred, total, comp_flip, targ_flip, targ_acc, sems = refs
    side = values_buf.shape[2]
    comp_per = comp_firsts[0].shape[0] // side
    targ_per = targ_refs[0].shape[0] // side
    targ_group = rows * targ_per
    chunks = (live_ref[0] + chunk - 1) // chunk

    def copies(index):
        spot = lax.rem(index, depth)
        source = pl.ds(index * chunk, chunk)
        return (
            pltpu.make_async_copy(values_hbm.at[source], values_buf.at[spot], sems.at[0, spot]),
            pltpu.make_async_copy(weight_hbm.at[source], weight_buf.at[spot], sems.at[1, spot]),
        )

    def fetch(index):
        @pl.when(index < chunks)
        def _():
            for copy in copies(index):
                copy.start()

    lax.fori_loop(0, depth, lambda index, unused: (fetch(index), unused)[1], 0)

    comp_rows, targ_rows = comp_per * side, targ_per * side
    zeros = jnp.zeros((side, side), jnp.float32)
    for row in range(rows):
        targ_flip[:, row * targ_rows : (row + 1) * targ_rows] = targ_refs[row][...].T
    for col in range(cols):
        if col % 2:
            comp = comp_seconds[col // 2 * comp_rows : (col // 2 + 1) * comp_rows]
        else:
            comp = comp_firsts[col // 2][...]
        comp_flip[:, col * comp_rows : (col + 1) * comp_rows] = comp.T
        for row in range(rows):
            block = jnp.dot(
                comp,
                targ_flip[:, row * targ_rows : (row + 1) * targ_rows],
                preferred_element_type=jnp.float32,
            ).astype(pred.dtype)
            for i in range(comp_per):
                for j in range(targ_per):
                    pair = (col * comp_per + i) * targ_group + row * targ_per + j
                    pred[pair] = block[i * side : (i + 1) * side, j * side : (j + 1) * side]
                    total[pair] = zeros

    one = jnp.asarray(degrees_free * noise_scale * noise_scale, pred.dtype)

    def visit_chunk(index, unused):
        spot = lax.rem(index, depth)
        for copy in copies(index):
            copy.wait()

        def visit(step, unused):
            slots = [step * GROUP + n for n in range(GROUP)]
            pairs = [slot_ref[index * chunk + slot] for slot in slots]
            scaled = []
            for slot, pair in zip(slots, pairs):
                resid = values_buf[spot, slot] - pred[pair]
                inverse = pl.reciprocal(one + resid * resid, approx=True)
                scaled.append(resid * weight_buf[spot, slot] * inverse)
            for each, pair in zip(scaled, pairs):
                total[pair] += each.astype(jnp.float32)
            return unused

        lax.fori_loop(0, chunk // GROUP, visit, 0, unroll=2)
        fetch(index + depth)
        return unused

    lax.fori_loop(0, chunks, visit_chunk, 0)

    gain = degrees_free + 1.0
    for col in range(cols):
        comp = comp_flip[:, col * comp_rows : (col + 1) * comp_rows]
        comp_sum = None
        for row in range(rows):
            first = (col * comp_per) * targ_group + row * targ_per
            tiles = [
                jnp.concatenate(
                    [total[first + i * targ_group + j] for j in range(targ_per)], axis=1
                )
                for i in range(comp_per)
            ]
            weights = jnp.concatenate(tiles, axis=0).astype(jnp.bfloat16)
            part = jnp.dot(weights, targ_refs[row][...], preferred_element_type=jnp.float32)
            comp_sum = part if comp_sum is None else comp_sum + part
            targ_part = jnp.dot(comp, weights, preferred_element_type=jnp.float32)
            if col == 0:
                targ_acc[row] = targ_part
            elif col < cols - 1:
                targ_acc[row] += targ_part
            else:
                whole = (targ_acc[row] + targ_part) * gain
                targ_outs[row][...] = whole.T.astype(targ_outs[row].dtype)
        comp_out = comp_send if col % 2 else comp_keep
        comp_out[col // 2] = (comp_sum * gain).astype(comp_out.dtype)


def local_grads(slots, live, comp_firsts, comp_seconds, targ_blocks, values, weight):
    cols, rows = 2 * len(comp_firsts), len(targ_blocks)
    slot_count, side, rank = values.shape
    comp_rows, rank = comp_firsts[0].shape
    targ_rows = targ_blocks[0].shape[0]
    pairs = cols * (comp_rows // side) * rows * (targ_rows // side)
    chunk = math.gcd(slot_count, 16)
    tile = side * side
    held = (pairs + 1) * tile * 6 + (cols * comp_rows + rows * targ_rows) * rank * 8
    depth = max(2, min(slot_count // chunk, (36 * 2**20 - held) // (chunk * tile * 4)))
    held += depth * chunk * tile * 4
    smem = pl.BlockSpec(memory_space=pltpu.SMEM)
    vmem = pl.BlockSpec(memory_space=pltpu.VMEM)
    hbm = pl.BlockSpec(memory_space=pltpu.HBM)

    comp_shape = jax.ShapeDtypeStruct((cols // 2, comp_rows, rank), jnp.bfloat16)
    targ_shapes = [
        jax.ShapeDtypeStruct((targ_rows, rank), jnp.bfloat16 if row else jnp.float32)
        for row in range(rows)
    ]
    outs = pl.pallas_call(
        functools.partial(force_kernel, cols, rows, chunk, depth),
        out_shape=[comp_shape, comp_shape] + targ_shapes,
        in_specs=[smem, smem] + [vmem] * (cols // 2 + 1 + rows) + [hbm, hbm],
        out_specs=[vmem] * (2 + rows),
        scratch_shapes=[
            pltpu.VMEM((depth, chunk, side, side), values.dtype),
            pltpu.VMEM((depth, chunk, side, side), weight.dtype),
            pltpu.VMEM((pairs + 1, side, side), jnp.bfloat16),
            pltpu.VMEM((pairs + 1, side, side), jnp.float32),
            pltpu.VMEM((rank, cols * comp_rows), jnp.bfloat16),
            pltpu.VMEM((rank, rows * targ_rows), jnp.bfloat16),
            pltpu.VMEM((rows, rank, targ_rows), jnp.float32),
            pltpu.SemaphoreType.DMA((2, depth)),
        ],
        compiler_params=pltpu.CompilerParams(vmem_limit_bytes=max(held + 4 * 2**20, 57 * 2**20)),
        name="tile_force",
    )(slots, live, *comp_firsts, comp_seconds, *targ_blocks, values, weight)
    return outs[0], outs[1], outs[2:]


def swap(block, axis, offset):
    size = lax.axis_size(axis)
    return lax.ppermute(block, axis, [(i, i ^ offset) for i in range(size)])


def spread(block, axis):
    return [block] + [swap(block, axis, offset) for offset in range(1, lax.axis_size(axis))]


def spread_pairs(block, axis):
    firsts = [block]
    firsts += [swap(block, axis, offset) for offset in range(2, lax.axis_size(axis), 2)]
    seconds = swap(jnp.concatenate(firsts), axis, 1)
    return firsts, seconds


def collect(blocks, axis):
    got = [swap(block, axis, offset) for offset, block in enumerate(blocks) if offset]
    whole = blocks[0].astype(jnp.float32)
    for block in got:
        whole = whole + block.astype(jnp.float32)
    return whole


def collect_pairs(keep, send, axis):
    got = swap(send, axis, 1)
    both = [
        keep[n].astype(jnp.float32) + got[n].astype(jnp.float32) for n in range(keep.shape[0])
    ]
    whole = both[0]
    for n, block in enumerate(both[1:]):
        whole = whole + swap(block.astype(keep.dtype), axis, 2 * n + 2).astype(jnp.float32)
    return whole


def body(
    compound_pos,
    compound_mom,
    target_pos,
    target_mom,
    tile_rows,
    tile_cols,
    tile_count,
    tile_values,
    tile_weight,
):
    side = tile_values.shape[2]
    comp_per = compound_pos.shape[0] // side
    targ_per = target_pos.shape[0] // side
    cols, rows = lax.axis_size("col"), lax.axis_size("row")
    col_index, row_index = lax.axis_index("col"), lax.axis_index("row")
    assert cols & (cols - 1) == 0 and rows & (rows - 1) == 0
    comp_local = tile_rows[0] - row_index * (cols * comp_per)
    comp_place = ((comp_local // comp_per) ^ col_index) * comp_per + comp_local % comp_per
    holder = tile_cols[0] // targ_per // cols
    targ_place = (holder ^ row_index) * targ_per + tile_cols[0] % targ_per
    targ_group = rows * targ_per
    alive = jnp.arange(tile_values.shape[1], dtype=jnp.int32) < tile_count[0]
    spare = cols * comp_per * targ_group
    slots = jnp.where(alive, comp_place * targ_group + targ_place, spare)

    def forces(comp, targ):
        comp_firsts, comp_seconds = spread_pairs(comp.astype(jnp.bfloat16), "col")
        targ_blocks = spread(targ.astype(jnp.bfloat16), "row")
        comp_keep, comp_send, targ_parts = local_grads(
            slots, tile_count, comp_firsts, comp_seconds, targ_blocks, tile_values[0], tile_weight[0]
        )
        comp_sum = collect_pairs(comp_keep, comp_send, "col")
        targ_sum = collect(targ_parts, "row")
        return comp_sum - prior_weight * comp, targ_sum - prior_weight * targ

    places = (compound_pos, target_pos)
    speeds = (compound_mom, target_mom)
    push = forces(*places)
    for leap in range(LEAPS):
        scale = (0.5 if leap == 0 else 1.0) * step_size
        speeds = tuple(p + scale * f for p, f in zip(speeds, push))
        places = tuple(q + step_size * p for q, p in zip(places, speeds))
        push = forces(*places)
    speeds = tuple(p + 0.5 * step_size * f for p, f in zip(speeds, push))
    return (places[0], speeds[0], places[1], speeds[1])


def solution(mesh):
    split = P(("row", "col"), None)
    tiles = P(("row", "col"), None, None, None)
    return jax.shard_map(
        body,
        mesh=mesh,
        in_specs=(split,) * 6 + (P(("row", "col")), tiles, tiles),
        out_specs=(split,) * 4,
        check_vma=False,
    )
```

```python
import functools
import math

import jax
import jax.numpy as jnp
from jax import lax
from jax.experimental import pallas as pl
from jax.experimental.pallas import tpu as pltpu
from jax.sharding import PartitionSpec as P

LEAPS = 2
GROUP = 4
CROWD = 12
VMEM_BYTES = 48 * 2**20


degrees_free = 4.0
noise_scale = 0.5
prior_weight = 1.0
step_size = 0.01


def force_kernel(cols, rows, chunk, depth, slot_ref, live_ref, crowd_ref, *refs):
    comp_firsts, comp_seconds, refs = refs[: cols // 2], refs[cols // 2], refs[cols // 2 + 1 :]
    targ_firsts, targ_seconds, refs = refs[: rows // 2], refs[rows // 2], refs[rows // 2 + 1 :]
    values_hbm, weight_hbm, refs = refs[0], refs[1], refs[2:]
    comp_keep, comp_send, targ_keep, targ_send, refs = *refs[:4], refs[4:]
    values_buf, weight_buf, pred, total, comp_flip, targ_flip, comp_acc, targ_acc, sems = refs
    side = values_buf.shape[2]
    comp_rows, targ_rows = comp_firsts[0].shape[0], targ_firsts[0].shape[0]
    comp_per, targ_per = comp_rows // side, targ_rows // side
    targ_group = rows * targ_per
    chunks = (live_ref[0] + chunk - 1) // chunk
    crowded = crowd_ref[0] > CROWD

    def comp_block(col):
        if col % 2:
            return comp_seconds[col // 2 * comp_rows : (col // 2 + 1) * comp_rows]
        return comp_firsts[col // 2][...]

    def targ_block(row):
        if row % 2:
            return targ_seconds[row // 2 * targ_rows : (row // 2 + 1) * targ_rows]
        return targ_firsts[row // 2][...]

    def copies(index):
        spot = lax.rem(index, depth)
        source = pl.ds(index * chunk, chunk)
        return (
            pltpu.make_async_copy(values_hbm.at[source], values_buf.at[spot], sems.at[0, spot]),
            pltpu.make_async_copy(weight_hbm.at[source], weight_buf.at[spot], sems.at[1, spot]),
        )

    def fetch(index):
        @pl.when(index < chunks)
        def _():
            for copy in copies(index):
                copy.start()

    def each_chunk(visit, steps):
        def visit_chunk(index, unused):
            spot = lax.rem(index, depth)
            for copy in copies(index):
                copy.wait()
            lax.fori_loop(0, steps, functools.partial(visit, index, spot), 0, unroll=2)
            fetch(index + depth)
            return unused

        lax.fori_loop(0, chunks, visit_chunk, 0)

    lax.fori_loop(0, depth, lambda index, unused: (fetch(index), unused)[1], 0)

    zeros = jnp.zeros((side, side), total.dtype)
    for row in range(rows):
        targ_flip[:, row * targ_rows : (row + 1) * targ_rows] = targ_block(row).T
    for col in range(cols):
        comp = comp_block(col)
        comp_flip[:, col * comp_rows : (col + 1) * comp_rows] = comp.T
        for row in range(rows):
            block = jnp.dot(
                comp,
                targ_flip[:, row * targ_rows : (row + 1) * targ_rows],
                preferred_element_type=jnp.float32,
            ).astype(pred.dtype)
            for i in range(comp_per):
                for j in range(targ_per):
                    pair = (col * comp_per + i) * targ_group + row * targ_per + j
                    pred[pair] = block[i * side : (i + 1) * side, j * side : (j + 1) * side]
                    total[pair] = zeros

    one = jnp.asarray(degrees_free * noise_scale * noise_scale, pred.dtype)

    def weigh(spot, slot, pair):
        resid = values_buf[spot, slot] - pred[pair]
        inverse = pl.reciprocal(one + resid * resid, approx=True)
        return resid * weight_buf[spot, slot] * inverse

    @pl.when(jnp.logical_not(crowded))
    def _():
        def visit(index, spot, step, unused):
            slots = [step * GROUP + n for n in range(GROUP)]
            pairs = [slot_ref[index * chunk + slot] for slot in slots]
            scaled = [weigh(spot, slot, pair) for slot, pair in zip(slots, pairs)]
            for each, pair in zip(scaled, pairs):
                total[pair] += each
            return unused

        each_chunk(visit, chunk // GROUP)

    @pl.when(crowded)
    def _():
        comp_acc[...] = jnp.zeros_like(comp_acc)
        targ_acc[...] = jnp.zeros_like(targ_acc)

        def visit(index, spot, slot, unused):
            pair = slot_ref[index * chunk + slot]

            @pl.when(pair < pred.shape[0] - 1)
            def _():
                scaled = weigh(spot, slot, pair)
                comp_at = pl.ds(pl.multiple_of(pair // targ_group * side, side), side)
                targ_at = pl.ds(pl.multiple_of(pair % targ_group * side, side), side)
                comp_acc[:, comp_at] += lax.dot_general(
                    targ_flip[:, targ_at],
                    scaled,
                    (((1,), (1,)), ((), ())),
                    preferred_element_type=jnp.float32,
                )
                targ_acc[:, targ_at] += jnp.dot(
                    comp_flip[:, comp_at], scaled, preferred_element_type=jnp.float32
                )

            return unused

        each_chunk(visit, chunk)

    gain = degrees_free + 1.0
    targ_all = jnp.concatenate([targ_block(row) for row in range(rows)])
    for col in range(cols):
        weights = jnp.concatenate(
            [
                jnp.concatenate([total[i * targ_group + j] for j in range(targ_group)], axis=1)
                for i in range(col * comp_per, (col + 1) * comp_per)
            ]
        )
        part = jnp.dot(weights, targ_all, preferred_element_type=jnp.float32) * gain
        comp_out = comp_send if col % 2 else comp_keep
        comp_out[col // 2] = part.astype(comp_out.dtype)
    for row in range(rows):
        weights = jnp.concatenate(
            [
                jnp.concatenate(
                    [total[i * targ_group + row * targ_per + j] for j in range(targ_per)], axis=1
                )
                for i in range(cols * comp_per)
            ]
        )
        part = jnp.dot(comp_flip[...], weights, preferred_element_type=jnp.float32) * gain
        targ_out = targ_send if row % 2 else targ_keep
        targ_out[row // 2] = part.T.astype(targ_out.dtype)

    @pl.when(crowded)
    def _():
        for col in range(cols):
            comp_out = comp_send if col % 2 else comp_keep
            part = comp_acc[:, col * comp_rows : (col + 1) * comp_rows] * gain
            comp_out[col // 2] = part.T.astype(comp_out.dtype)
        for row in range(rows):
            targ_out = targ_send if row % 2 else targ_keep
            part = targ_acc[:, row * targ_rows : (row + 1) * targ_rows] * gain
            targ_out[row // 2] = part.T.astype(targ_out.dtype)


def local_grads(slots, live, crowd, comp_firsts, comp_seconds, targ_firsts, targ_seconds, values, weight):
    cols, rows = 2 * len(comp_firsts), 2 * len(targ_firsts)
    slot_count, side, rank = values.shape
    comp_rows, rank = comp_firsts[0].shape
    targ_rows = targ_firsts[0].shape[0]
    pairs = cols * (comp_rows // side) * rows * (targ_rows // side)
    chunk = math.gcd(slot_count, 16)
    tile = side * side
    held = (pairs + 1) * tile * 4 + (cols * comp_rows + rows * targ_rows) * rank * 8
    depth = max(2, min(slot_count // chunk, (36 * 2**20 - held) // (chunk * tile * 4)))
    held += depth * chunk * tile * 4
    smem = pl.BlockSpec(memory_space=pltpu.SMEM)
    vmem = pl.BlockSpec(memory_space=pltpu.VMEM)
    hbm = pl.BlockSpec(memory_space=pltpu.HBM)
    comp_shape = jax.ShapeDtypeStruct((cols // 2, comp_rows, rank), jnp.bfloat16)
    targ_shape = jax.ShapeDtypeStruct((rows // 2, targ_rows, rank), jnp.bfloat16)
    return pl.pallas_call(
        functools.partial(force_kernel, cols, rows, chunk, depth),
        out_shape=[comp_shape, comp_shape, targ_shape, targ_shape],
        in_specs=[smem] * 3 + [vmem] * (cols // 2 + 1 + rows // 2 + 1) + [hbm, hbm],
        out_specs=[vmem] * 4,
        scratch_shapes=[
            pltpu.VMEM((depth, chunk, side, side), values.dtype),
            pltpu.VMEM((depth, chunk, side, side), weight.dtype),
            pltpu.VMEM((pairs + 1, side, side), jnp.bfloat16),
            pltpu.VMEM((pairs + 1, side, side), jnp.bfloat16),
            pltpu.VMEM((rank, cols * comp_rows), jnp.bfloat16),
            pltpu.VMEM((rank, rows * targ_rows), jnp.bfloat16),
            pltpu.VMEM((rank, cols * comp_rows), jnp.float32),
            pltpu.VMEM((rank, rows * targ_rows), jnp.float32),
            pltpu.SemaphoreType.DMA((2, depth)),
        ],
        compiler_params=pltpu.CompilerParams(
            vmem_limit_bytes=max(held + 4 * 2**20, VMEM_BYTES)
        ),
        name="tile_force",
    )(slots, live, crowd, *comp_firsts, comp_seconds, *targ_firsts, targ_seconds, values, weight)


def swap(block, axis, offset):
    size = lax.axis_size(axis)
    return lax.ppermute(block, axis, [(i, i ^ offset) for i in range(size)])


def spread_pairs(block, axis):
    firsts = [block]
    firsts += [swap(block, axis, offset) for offset in range(2, lax.axis_size(axis), 2)]
    seconds = swap(jnp.concatenate(firsts), axis, 1)
    return firsts, seconds


def collect_pairs(keep, send, axis):
    got = swap(send, axis, 1)
    both = [
        keep[n].astype(jnp.float32) + got[n].astype(jnp.float32) for n in range(keep.shape[0])
    ]
    whole = both[0]
    for n, block in enumerate(both[1:]):
        whole = whole + swap(block.astype(keep.dtype), axis, 2 * n + 2).astype(jnp.float32)
    return whole


def body(
    compound_pos,
    compound_mom,
    target_pos,
    target_mom,
    tile_rows,
    tile_cols,
    tile_count,
    tile_values,
    tile_weight,
):
    side = tile_values.shape[2]
    comp_per = compound_pos.shape[0] // side
    targ_per = target_pos.shape[0] // side
    cols, rows = lax.axis_size("col"), lax.axis_size("row")
    col_index, row_index = lax.axis_index("col"), lax.axis_index("row")
    assert cols & (cols - 1) == 0 and rows & (rows - 1) == 0
    comp_local = tile_rows[0] - row_index * (cols * comp_per)
    comp_place = ((comp_local // comp_per) ^ col_index) * comp_per + comp_local % comp_per
    holder = tile_cols[0] // targ_per // cols
    targ_place = (holder ^ row_index) * targ_per + tile_cols[0] % targ_per
    targ_group = rows * targ_per
    alive = jnp.arange(tile_values.shape[1], dtype=jnp.int32) < tile_count[0]
    spare = cols * comp_per * targ_group
    slots = jnp.where(alive, comp_place * targ_group + targ_place, spare)

    same = jnp.logical_and(slots[:, None] == slots[None, :], alive[None, :])
    crowd = jnp.max(jnp.sum(same.astype(jnp.int32), axis=1)).reshape(1)

    def forces(comp, targ):
        comp_keep, comp_send, targ_keep, targ_send = local_grads(
            slots,
            tile_count,
            crowd,
            *spread_pairs(comp.astype(jnp.bfloat16), "col"),
            *spread_pairs(targ.astype(jnp.bfloat16), "row"),
            tile_values[0],
            tile_weight[0],
        )
        comp_sum = collect_pairs(comp_keep, comp_send, "col")
        targ_sum = collect_pairs(targ_keep, targ_send, "row")
        return comp_sum - prior_weight * comp, targ_sum - prior_weight * targ

    places = (compound_pos, target_pos)
    speeds = (compound_mom, target_mom)
    push = forces(*places)
    for leap in range(LEAPS):
        scale = (0.5 if leap == 0 else 1.0) * step_size
        speeds = tuple(p + scale * f for p, f in zip(speeds, push))
        places = tuple(q + step_size * p for q, p in zip(places, speeds))
        push = forces(*places)
    speeds = tuple(p + 0.5 * step_size * f for p, f in zip(speeds, push))
    return (places[0], speeds[0], places[1], speeds[1])


def solution(mesh):
    split = P(("row", "col"), None)
    tiles = P(("row", "col"), None, None, None)
    return jax.shard_map(
        body,
        mesh=mesh,
        in_specs=(split,) * 6 + (P(("row", "col")), tiles, tiles),
        out_specs=(split,) * 4,
        check_vma=False,
    )
```

```python
import functools
import math

import jax
import jax.numpy as jnp
from jax import lax
from jax.experimental import pallas as pl
from jax.experimental.pallas import tpu as pltpu
from jax.sharding import PartitionSpec as P

LEAPS = 2
GROUP = 4
UNROLL = 4


degrees_free = 4.0
noise_scale = 0.5
prior_weight = 1.0
step_size = 0.01


def load_kernel(targ_group, shape, pair_ref, live_ref, values_hbm, weight_hbm, *refs):
    values_out, weight_out, lists_ref, sems = refs
    pairs, comp_tiles, targ_tiles = shape
    slots = values_hbm.shape[0]
    chunks = sems.shape[1]
    chunk = slots // chunks

    def copies(index):
        part = pl.ds(index * chunk, chunk)
        return (
            pltpu.make_async_copy(values_hbm.at[part], values_out.at[part], sems.at[0, index]),
            pltpu.make_async_copy(weight_hbm.at[part], weight_out.at[part], sems.at[1, index]),
        )

    for index in range(chunks):

        @pl.when(index * chunk < live_ref[0])
        def _():
            for copy in copies(index):
                copy.start()

    values_out[slots] = jnp.zeros_like(values_out[slots])
    weight_out[slots] = jnp.zeros_like(weight_out[slots])

    across = jnp.broadcast_to(pair_ref[...].astype(jnp.float32), (slots, slots))
    down = across.T
    at = lax.broadcasted_iota(jnp.int32, (slots, slots), 1).astype(jnp.float32)
    mine = lax.broadcasted_iota(jnp.int32, (slots, slots), 0).astype(jnp.float32)
    spare = float(comp_tiles * targ_group)
    same = down == across

    def count(mask, axis):
        return jnp.sum(jnp.where(mask, 1.0, 0.0), axis=axis, keepdims=True)

    earlier = count(same & (mine < at), 0)
    groups = jnp.floor((count(same, 0) + (GROUP - 1.0)) * (1.0 / GROUP))
    opens = (earlier == 0.0) & (across[:1] < spare)
    before = across < down
    rank = jnp.sum(jnp.where(before & opens, 1.0, 0.0), axis=1, keepdims=True)
    first = jnp.sum(jnp.where(before & opens, groups, 0.0), axis=1, keepdims=True)
    pair = down[:, :1]
    earlier = count(same & (at < mine), 1)
    alive = pair < spare
    opens = (earlier == 0.0) & alive
    step = jnp.floor(earlier * (1.0 / GROUP))
    place = jnp.where(alive, first + step, -1.0)
    member = earlier - GROUP * step
    groups = jnp.floor((count(same, 1) + (GROUP - 1.0)) * (1.0 / GROUP))

    def pick(mask, value, rest):
        return jnp.sum(jnp.where(mask, value - rest, 0.0), axis=0, keepdims=True) + rest

    here = place == at
    comp_tile = jnp.floor((pair + 0.5) * (1.0 / targ_group))
    rows = [pick(here & (member == n), mine[:, :1], float(slots)) for n in range(GROUP)]
    rows.append(pick(here & (member == 0.0), rank, float(pairs)))
    here = (rank == at) & opens
    rows.append(pick(here, comp_tile, float(comp_tiles)))
    rows.append(pick(here, pair - targ_group * comp_tile, float(targ_tiles)))
    totals = [jnp.sum(jnp.where(opens, n, 0.0), axis=0, keepdims=True) for n in (groups, 1.0)]
    rows.append(jnp.where(at[:1] == 0.0, totals[0], totals[1]))
    lists_ref[...] = jnp.concatenate(rows, axis=0).astype(jnp.int32)

    for index in range(chunks):

        @pl.when(index * chunk < live_ref[0])
        def _():
            for copy in copies(index):
                copy.wait()


def force_kernel(cols, rows, lists_ref, *refs):
    comp_firsts, comp_seconds, refs = refs[: cols // 2], refs[cols // 2], refs[cols // 2 + 1 :]
    targ_firsts, targ_seconds, refs = refs[: rows // 2], refs[rows // 2], refs[rows // 2 + 1 :]
    values_ref, weight_ref, refs = refs[0], refs[1], refs[2:]
    comp_keep, comp_send, targ_keep, targ_send, refs = *refs[:4], refs[4:]
    pred, total, comp_tiles, comp_flip, targ_tiles, targ_flip, comp_acc, targ_acc = refs
    side = values_ref.shape[1]
    comp_rows, targ_rows = comp_firsts[0].shape[0], targ_firsts[0].shape[0]
    comp_per, targ_per = comp_rows // side, targ_rows // side

    def fill(count, per, firsts, seconds, tiles, flip, acc):
        for n in range(count):
            for i in range(per):
                if n % 2:
                    start = (n // 2 * per + i) * side
                    tile = seconds[start : start + side]
                else:
                    tile = firsts[n // 2][i * side : (i + 1) * side]
                tiles[n * per + i] = tile
                flip[n * per + i] = tile.T
                acc[n * per + i] = jnp.zeros(acc.shape[1:], acc.dtype)

    fill(cols, comp_per, comp_firsts, comp_seconds, comp_tiles, comp_flip, comp_acc)
    fill(rows, targ_per, targ_firsts, targ_seconds, targ_tiles, targ_flip, targ_acc)

    def steps(count):
        return lax.div(count + (UNROLL - 1), UNROLL)

    def pair_at(step):
        spots = [step * UNROLL + n for n in range(UNROLL)]
        return [(spot, lists_ref[GROUP + 1, spot], lists_ref[GROUP + 2, spot]) for spot in spots]

    last = pred.shape[0] - 1
    pairs, groups = lists_ref[GROUP + 3, 1], lists_ref[GROUP + 3, 0]

    def predict(step, unused):
        blocks = [
            (spot, jnp.dot(comp_tiles[i], targ_flip[j], preferred_element_type=jnp.float32))
            for spot, i, j in pair_at(step)
        ]
        for spot, block in blocks:
            spot = jnp.minimum(spot, last)
            pred[spot] = block.astype(pred.dtype)
            total[spot] = jnp.zeros(total.shape[1:], total.dtype)
        return unused

    lax.fori_loop(0, steps(pairs), predict, 0)

    one = jnp.asarray(degrees_free * noise_scale * noise_scale, pred.dtype)

    def weigh(step, unused):
        sums = []
        for n in range(UNROLL):
            group = step * UNROLL + n
            spot = lists_ref[GROUP, group]
            guess = pred[spot]
            whole = None
            for m in range(GROUP):
                slot = lists_ref[m, group]
                resid = values_ref[slot] - guess
                inverse = pl.reciprocal(one + resid * resid, approx=True)
                scaled = resid * weight_ref[slot] * inverse
                whole = scaled if whole is None else whole + scaled
            sums.append((spot, whole))
        for spot, whole in sums:
            total[spot] += whole.astype(total.dtype)
        return unused

    lax.fori_loop(0, steps(groups), weigh, 0)

    def gather(step, unused):
        parts = []
        for spot, i, j in pair_at(step):
            weights = total[jnp.minimum(spot, last)].astype(jnp.bfloat16)
            comp_part = jnp.dot(weights, targ_tiles[j], preferred_element_type=jnp.float32)
            targ_part = jnp.dot(comp_flip[i], weights, preferred_element_type=jnp.float32)
            parts.append((i, comp_part, j, targ_part))
        for i, comp_part, j, targ_part in parts:
            comp_acc[i] += comp_part
            targ_acc[j] += targ_part
        return unused

    lax.fori_loop(0, steps(pairs), gather, 0)

    gain = degrees_free + 1.0
    for n in range(cols):
        out = comp_send if n % 2 else comp_keep
        for i in range(comp_per):
            part = comp_acc[n * comp_per + i] * gain
            out[n // 2, i * side : (i + 1) * side] = part.astype(out.dtype)
    for n in range(rows):
        out = targ_send if n % 2 else targ_keep
        for i in range(targ_per):
            part = targ_acc[n * targ_per + i] * gain
            out[n // 2, i * side : (i + 1) * side] = part.T.astype(out.dtype)


smem = pl.BlockSpec(memory_space=pltpu.SMEM)
vmem = pl.BlockSpec(memory_space=pltpu.VMEM)
hbm = pl.BlockSpec(memory_space=pltpu.HBM)


def load_tiles(pairs, live, targ_group, shape, values, weight):
    slots, side, width = values.shape
    chunks = slots // math.gcd(slots, 16)
    held = pltpu.VMEM((slots + 1, side, width), values.dtype)
    values, weight = (pltpu.with_memory_space_constraint(x, pltpu.HBM) for x in (values, weight))
    return pl.pallas_call(
        functools.partial(load_kernel, targ_group, shape),
        out_shape=[held, held, jax.ShapeDtypeStruct((GROUP + 4, slots), jnp.int32)],
        in_specs=[vmem, smem, hbm, hbm],
        out_specs=[vmem] * 3,
        scratch_shapes=[pltpu.SemaphoreType.DMA((2, chunks))],
        compiler_params=pltpu.CompilerParams(vmem_limit_bytes=24 * 2**20),
        name="tile_load",
    )(pairs, live, values, weight)


def local_grads(lists, comp_firsts, comp_seconds, targ_firsts, targ_seconds, values, weight, pairs):
    cols, rows = 2 * len(comp_firsts), 2 * len(targ_firsts)
    comp_rows, rank = comp_firsts[0].shape
    targ_rows = targ_firsts[0].shape[0]
    side = values.shape[1]
    comp_tiles, targ_tiles = cols * comp_rows // side, rows * targ_rows // side
    comp_shape = jax.ShapeDtypeStruct((cols // 2, comp_rows, rank), jnp.bfloat16)
    targ_shape = jax.ShapeDtypeStruct((rows // 2, targ_rows, rank), jnp.bfloat16)
    held = (pairs + 1) * side * side * 6 + (comp_tiles + targ_tiles + 2) * side * rank * 8
    held += 4 * values.size
    return pl.pallas_call(
        functools.partial(force_kernel, cols, rows),
        out_shape=[comp_shape, comp_shape, targ_shape, targ_shape],
        in_specs=[smem] + [vmem] * (cols // 2 + 1 + rows // 2 + 1 + 2),
        out_specs=[vmem] * 4,
        scratch_shapes=[
            pltpu.VMEM((pairs + 1, side, side), jnp.bfloat16),
            pltpu.VMEM((pairs + 1, side, side), jnp.float32),
            pltpu.VMEM((comp_tiles + 1, side, rank), jnp.bfloat16),
            pltpu.VMEM((comp_tiles + 1, rank, side), jnp.bfloat16),
            pltpu.VMEM((targ_tiles + 1, side, rank), jnp.bfloat16),
            pltpu.VMEM((targ_tiles + 1, rank, side), jnp.bfloat16),
            pltpu.VMEM((comp_tiles + 1, side, rank), jnp.float32),
            pltpu.VMEM((targ_tiles + 1, rank, side), jnp.float32),
        ],
        compiler_params=pltpu.CompilerParams(vmem_limit_bytes=held + 4 * 2**20),
        name="tile_force",
    )(lists, *comp_firsts, comp_seconds, *targ_firsts, targ_seconds, values, weight)


def swap(block, axis, offset):
    size = lax.axis_size(axis)
    return lax.ppermute(block, axis, [(i, i ^ offset) for i in range(size)])


def spread_pairs(block, axis):
    firsts = [block]
    firsts += [swap(block, axis, offset) for offset in range(2, lax.axis_size(axis), 2)]
    seconds = swap(jnp.concatenate(firsts), axis, 1)
    return firsts, seconds


def collect_pairs(keep, send, axis):
    got = swap(send, axis, 1)
    both = [
        keep[n].astype(jnp.float32) + got[n].astype(jnp.float32) for n in range(keep.shape[0])
    ]
    whole = both[0]
    for n, block in enumerate(both[1:]):
        whole = whole + swap(block.astype(keep.dtype), axis, 2 * n + 2).astype(jnp.float32)
    return whole


def body(
    compound_pos,
    compound_mom,
    target_pos,
    target_mom,
    tile_rows,
    tile_cols,
    tile_count,
    tile_values,
    tile_weight,
):
    side = tile_values.shape[2]
    comp_per = compound_pos.shape[0] // side
    targ_per = target_pos.shape[0] // side
    cols, rows = lax.axis_size("col"), lax.axis_size("row")
    col_index, row_index = lax.axis_index("col"), lax.axis_index("row")
    assert cols & (cols - 1) == 0 and rows & (rows - 1) == 0
    comp_local = tile_rows[0] - row_index * (cols * comp_per)
    comp_place = ((comp_local // comp_per) ^ col_index) * comp_per + comp_local % comp_per
    holder = tile_cols[0] // targ_per // cols
    targ_place = (holder ^ row_index) * targ_per + tile_cols[0] % targ_per
    targ_group = rows * targ_per
    alive = jnp.arange(tile_values.shape[1], dtype=jnp.int32) < tile_count[0]
    spare = cols * comp_per * targ_group
    slots = jnp.where(alive, comp_place * targ_group + targ_place, spare)

    shape = (min(spare, slots.shape[0]), cols * comp_per, targ_group)
    values, weight, lists = load_tiles(
        slots[None], tile_count, targ_group, shape, tile_values[0], tile_weight[0]
    )

    def forces(comp, targ):
        comp_keep, comp_send, targ_keep, targ_send = local_grads(
            lists,
            *spread_pairs(comp.astype(jnp.bfloat16), "col"),
            *spread_pairs(targ.astype(jnp.bfloat16), "row"),
            values,
            weight,
            shape[0],
        )
        comp_sum = collect_pairs(comp_keep, comp_send, "col")
        targ_sum = collect_pairs(targ_keep, targ_send, "row")
        return comp_sum - prior_weight * comp, targ_sum - prior_weight * targ

    places = (compound_pos, target_pos)
    speeds = (compound_mom, target_mom)
    push = forces(*places)
    for leap in range(LEAPS):
        scale = (0.5 if leap == 0 else 1.0) * step_size
        speeds = tuple(p + scale * f for p, f in zip(speeds, push))
        places = tuple(q + step_size * p for q, p in zip(places, speeds))
        push = forces(*places)
    speeds = tuple(p + 0.5 * step_size * f for p, f in zip(speeds, push))
    return (places[0], speeds[0], places[1], speeds[1])


def solution(mesh):
    split = P(("row", "col"), None)
    tiles = P(("row", "col"), None, None, None)
    return jax.shard_map(
        body,
        mesh=mesh,
        in_specs=(split,) * 6 + (P(("row", "col")), tiles, tiles),
        out_specs=(split,) * 4,
        check_vma=False,
    )
```

```python
import functools
import math

import jax
import jax.numpy as jnp
from jax import lax
from jax.experimental import pallas as pl
from jax.experimental.pallas import tpu as pltpu
from jax.sharding import PartitionSpec as P

LEAPS = 2
GROUP = 4
UNROLL = 4


degrees_free = 4.0
noise_scale = 0.5
prior_weight = 1.0
step_size = 0.01


def load_kernel(targ_group, shape, pair_ref, live_ref, values_hbm, weight_hbm, *refs):
    values_out, weight_out, lists_ref, sems = refs
    pairs, comp_tiles, targ_tiles = shape
    slots = values_hbm.shape[0]
    chunks = sems.shape[1]
    chunk = slots // chunks

    def copies(index):
        part = pl.ds(index * chunk, chunk)
        return (
            pltpu.make_async_copy(values_hbm.at[part], values_out.at[part], sems.at[0, index]),
            pltpu.make_async_copy(weight_hbm.at[part], weight_out.at[part], sems.at[1, index]),
        )

    for index in range(chunks):

        @pl.when(index * chunk < live_ref[0])
        def _():
            for copy in copies(index):
                copy.start()

    values_out[slots] = jnp.zeros_like(values_out[slots])
    weight_out[slots] = jnp.zeros_like(weight_out[slots])

    across = jnp.broadcast_to(pair_ref[...].astype(jnp.float32), (slots, slots))
    down = across.T
    at = lax.broadcasted_iota(jnp.int32, (slots, slots), 1).astype(jnp.float32)
    mine = lax.broadcasted_iota(jnp.int32, (slots, slots), 0).astype(jnp.float32)
    spare = float(comp_tiles * targ_group)
    same = down == across

    def count(mask, axis):
        return jnp.sum(jnp.where(mask, 1.0, 0.0), axis=axis, keepdims=True)

    earlier = count(same & (mine < at), 0)
    groups = jnp.floor((count(same, 0) + (GROUP - 1.0)) * (1.0 / GROUP))
    opens = (earlier == 0.0) & (across[:1] < spare)
    before = across < down
    rank = jnp.sum(jnp.where(before & opens, 1.0, 0.0), axis=1, keepdims=True)
    first = jnp.sum(jnp.where(before & opens, groups, 0.0), axis=1, keepdims=True)
    pair = down[:, :1]
    earlier = count(same & (at < mine), 1)
    alive = pair < spare
    opens = (earlier == 0.0) & alive
    step = jnp.floor(earlier * (1.0 / GROUP))
    place = jnp.where(alive, first + step, -1.0)
    member = earlier - GROUP * step
    groups = jnp.floor((count(same, 1) + (GROUP - 1.0)) * (1.0 / GROUP))

    def pick(mask, value, rest):
        return jnp.sum(jnp.where(mask, value - rest, 0.0), axis=0, keepdims=True) + rest

    here = place == at
    comp_tile = jnp.floor((pair + 0.5) * (1.0 / targ_group))
    rows = [pick(here & (member == n), mine[:, :1], float(slots)) for n in range(GROUP)]
    rows.append(pick(here & (member == 0.0), rank, float(pairs)))
    here = (rank == at) & opens
    rows.append(pick(here, comp_tile, float(comp_tiles)))
    rows.append(pick(here, pair - targ_group * comp_tile, float(targ_tiles)))
    totals = [jnp.sum(jnp.where(opens, n, 0.0), axis=0, keepdims=True) for n in (groups, 1.0)]
    rows.append(jnp.where(at[:1] == 0.0, totals[0], totals[1]))
    lists_ref[...] = jnp.concatenate(rows, axis=0).astype(jnp.int32)

    for index in range(chunks):

        @pl.when(index * chunk < live_ref[0])
        def _():
            for copy in copies(index):
                copy.wait()


def force_kernel(cols, rows, lists_ref, *refs):
    comp_firsts, comp_seconds, refs = refs[: cols // 2], refs[cols // 2], refs[cols // 2 + 1 :]
    targ_blocks, refs = refs[:rows], refs[rows:]
    values_ref, weight_ref, refs = refs[0], refs[1], refs[2:]
    comp_keep, comp_send, refs = refs[0], refs[1], refs[2:]
    targ_outs, refs = refs[:rows], refs[rows:]
    pred, total, comp_tiles, comp_flip, targ_tiles, targ_flip, comp_acc, targ_acc = refs
    side = values_ref.shape[1]
    comp_rows, targ_rows = comp_firsts[0].shape[0], targ_blocks[0].shape[0]
    comp_per, targ_per = comp_rows // side, targ_rows // side

    def fill(spot, tile, tiles, flip, acc):
        tiles[spot] = tile
        flip[spot] = tile.T
        acc[spot] = jnp.zeros(acc.shape[1:], acc.dtype)

    for n in range(rows):
        for i in range(targ_per):
            tile = targ_blocks[n][i * side : (i + 1) * side]
            fill(n * targ_per + i, tile, targ_tiles, targ_flip, targ_acc)
    for n in range(cols):
        for i in range(comp_per):
            start = (n // 2 * comp_per * (n % 2) + i) * side
            tile = (comp_seconds if n % 2 else comp_firsts[n // 2])[start : start + side]
            fill(n * comp_per + i, tile, comp_tiles, comp_flip, comp_acc)

    def steps(count):
        return lax.div(count + (UNROLL - 1), UNROLL)

    def pair_at(step):
        spots = [step * UNROLL + n for n in range(UNROLL)]
        return [(spot, lists_ref[GROUP + 1, spot], lists_ref[GROUP + 2, spot]) for spot in spots]

    last = pred.shape[0] - 1
    pairs, groups = lists_ref[GROUP + 3, 1], lists_ref[GROUP + 3, 0]

    def predict(step, unused):
        blocks = [
            (spot, jnp.dot(comp_tiles[i], targ_flip[j], preferred_element_type=jnp.float32))
            for spot, i, j in pair_at(step)
        ]
        for spot, block in blocks:
            spot = jnp.minimum(spot, last)
            pred[spot] = block.astype(pred.dtype)
            total[spot] = jnp.zeros(total.shape[1:], total.dtype)
        return unused

    lax.fori_loop(0, steps(pairs), predict, 0)

    one = degrees_free * noise_scale * noise_scale

    def weigh(step, unused):
        sums = []
        for n in range(UNROLL):
            group = step * UNROLL + n
            spot = lists_ref[GROUP, group]
            guess = pred[spot].astype(jnp.float32)
            whole = None
            for m in range(GROUP):
                slot = lists_ref[m, group]
                resid = values_ref[slot].astype(jnp.float32) - guess
                inverse = pl.reciprocal(one + resid * resid, approx=True)
                scaled = resid * weight_ref[slot].astype(jnp.float32) * inverse
                whole = scaled if whole is None else whole + scaled
            sums.append((spot, whole))
        for spot, whole in sums:
            total[spot] += whole
        return unused

    lax.fori_loop(0, steps(groups), weigh, 0)

    def gather(step, unused):
        parts = []
        for spot, i, j in pair_at(step):
            weights = total[jnp.minimum(spot, last)].astype(jnp.bfloat16)
            comp_part = jnp.dot(weights, targ_tiles[j], preferred_element_type=jnp.float32)
            targ_part = jnp.dot(comp_flip[i], weights, preferred_element_type=jnp.float32)
            parts.append((i, comp_part, j, targ_part))
        for i, comp_part, j, targ_part in parts:
            comp_acc[i] += comp_part
            targ_acc[j] += targ_part
        return unused

    lax.fori_loop(0, steps(pairs), gather, 0)

    gain = degrees_free + 1.0
    for n in range(cols):
        out = comp_send if n % 2 else comp_keep
        for i in range(comp_per):
            part = comp_acc[n * comp_per + i] * gain
            out[n // 2, i * side : (i + 1) * side] = part.astype(out.dtype)
    for n in range(rows):
        out = targ_outs[n]
        for i in range(targ_per):
            part = targ_acc[n * targ_per + i] * gain
            out[i * side : (i + 1) * side] = part.T.astype(out.dtype)


smem = pl.BlockSpec(memory_space=pltpu.SMEM)
vmem = pl.BlockSpec(memory_space=pltpu.VMEM)
hbm = pl.BlockSpec(memory_space=pltpu.HBM)


def load_tiles(pairs, live, targ_group, shape, values, weight):
    slots, side, width = values.shape
    chunks = slots // math.gcd(slots, 16)
    held = pltpu.VMEM((slots + 1, side, width), values.dtype)
    values, weight = (pltpu.with_memory_space_constraint(x, pltpu.HBM) for x in (values, weight))
    return pl.pallas_call(
        functools.partial(load_kernel, targ_group, shape),
        out_shape=[held, held, jax.ShapeDtypeStruct((GROUP + 4, slots), jnp.int32)],
        in_specs=[vmem, smem, hbm, hbm],
        out_specs=[vmem] * 3,
        scratch_shapes=[pltpu.SemaphoreType.DMA((2, chunks))],
        compiler_params=pltpu.CompilerParams(vmem_limit_bytes=24 * 2**20),
        name="tile_load",
    )(pairs, live, values, weight)


def local_grads(lists, comp_firsts, comp_seconds, targ_blocks, values, weight, pairs):
    cols, rows = 2 * len(comp_firsts), len(targ_blocks)
    comp_rows, rank = comp_firsts[0].shape
    targ_rows = targ_blocks[0].shape[0]
    side = values.shape[1]
    comp_tiles, targ_tiles = cols * comp_rows // side, rows * targ_rows // side
    comp_shape = jax.ShapeDtypeStruct((cols // 2, comp_rows, rank), jnp.bfloat16)
    targ_shape = jax.ShapeDtypeStruct((targ_rows, rank), jnp.bfloat16)
    held = (pairs + 1) * side * side * 6 + (comp_tiles + targ_tiles + 2) * side * rank * 8
    held += 4 * values.size
    outs = pl.pallas_call(
        functools.partial(force_kernel, cols, rows),
        out_shape=[comp_shape] * 2 + [targ_shape] * rows,
        in_specs=[smem] + [vmem] * (cols // 2 + 1 + rows + 2),
        out_specs=[vmem] * (2 + rows),
        scratch_shapes=[
            pltpu.VMEM((pairs + 1, side, side), jnp.bfloat16),
            pltpu.VMEM((pairs + 1, side, side), jnp.float32),
            pltpu.VMEM((comp_tiles + 1, side, rank), jnp.bfloat16),
            pltpu.VMEM((comp_tiles + 1, rank, side), jnp.bfloat16),
            pltpu.VMEM((targ_tiles + 1, side, rank), jnp.bfloat16),
            pltpu.VMEM((targ_tiles + 1, rank, side), jnp.bfloat16),
            pltpu.VMEM((comp_tiles + 1, side, rank), jnp.float32),
            pltpu.VMEM((targ_tiles + 1, rank, side), jnp.float32),
        ],
        compiler_params=pltpu.CompilerParams(vmem_limit_bytes=held + 4 * 2**20),
        name="tile_force",
    )(lists, *comp_firsts, comp_seconds, *targ_blocks, values, weight)
    return outs[0], outs[1], outs[2:]


def swap(block, axis, offset):
    size = lax.axis_size(axis)
    return lax.ppermute(block, axis, [(i, i ^ offset) for i in range(size)])


def spread(block, axis):
    return [block] + [swap(block, axis, offset) for offset in range(1, lax.axis_size(axis))]


def collect(blocks, axis):
    whole = blocks[0].astype(jnp.float32)
    for offset, block in enumerate(blocks[1:]):
        whole = whole + swap(block, axis, offset + 1).astype(jnp.float32)
    return whole


def spread_pairs(block, axis):
    firsts = [block]
    firsts += [swap(block, axis, offset) for offset in range(2, lax.axis_size(axis), 2)]
    seconds = swap(jnp.concatenate(firsts), axis, 1)
    return firsts, seconds


def collect_pairs(keep, send, axis):
    got = swap(send, axis, 1)
    both = [
        keep[n].astype(jnp.float32) + got[n].astype(jnp.float32) for n in range(keep.shape[0])
    ]
    whole = both[0]
    for n, block in enumerate(both[1:]):
        whole = whole + swap(block.astype(keep.dtype), axis, 2 * n + 2).astype(jnp.float32)
    return whole


def body(
    compound_pos,
    compound_mom,
    target_pos,
    target_mom,
    tile_rows,
    tile_cols,
    tile_count,
    tile_values,
    tile_weight,
):
    side = tile_values.shape[2]
    comp_per = compound_pos.shape[0] // side
    targ_per = target_pos.shape[0] // side
    cols, rows = lax.axis_size("col"), lax.axis_size("row")
    col_index, row_index = lax.axis_index("col"), lax.axis_index("row")
    assert cols & (cols - 1) == 0 and rows & (rows - 1) == 0
    comp_local = tile_rows[0] - row_index * (cols * comp_per)
    comp_place = ((comp_local // comp_per) ^ col_index) * comp_per + comp_local % comp_per
    holder = tile_cols[0] // targ_per // cols
    targ_place = (holder ^ row_index) * targ_per + tile_cols[0] % targ_per
    targ_group = rows * targ_per
    alive = jnp.arange(tile_values.shape[1], dtype=jnp.int32) < tile_count[0]
    spare = cols * comp_per * targ_group
    slots = jnp.where(alive, comp_place * targ_group + targ_place, spare)

    shape = (min(spare, slots.shape[0]), cols * comp_per, targ_group)
    values, weight, lists = load_tiles(
        slots[None], tile_count, targ_group, shape, tile_values[0], tile_weight[0]
    )

    def forces(comp, targ):
        comp_keep, comp_send, targ_parts = local_grads(
            lists,
            *spread_pairs(comp.astype(jnp.bfloat16), "col"),
            spread(targ.astype(jnp.bfloat16), "row"),
            values,
            weight,
            shape[0],
        )
        comp_sum = collect_pairs(comp_keep, comp_send, "col")
        targ_sum = collect(targ_parts, "row")
        return comp_sum - prior_weight * comp, targ_sum - prior_weight * targ

    places = (compound_pos, target_pos)
    speeds = (compound_mom, target_mom)
    push = forces(*places)
    for leap in range(LEAPS):
        scale = (0.5 if leap == 0 else 1.0) * step_size
        speeds = tuple(p + scale * f for p, f in zip(speeds, push))
        places = tuple(q + step_size * p for q, p in zip(places, speeds))
        push = forces(*places)
    speeds = tuple(p + 0.5 * step_size * f for p, f in zip(speeds, push))
    return (places[0], speeds[0], places[1], speeds[1])


def solution(mesh):
    split = P(("row", "col"), None)
    tiles = P(("row", "col"), None, None, None)
    return jax.shard_map(
        body,
        mesh=mesh,
        in_specs=(split,) * 6 + (P(("row", "col")), tiles, tiles),
        out_specs=(split,) * 4,
        check_vma=False,
    )
```

```python
import functools
import math

import jax
import jax.numpy as jnp
from jax import lax
from jax.experimental import pallas as pl
from jax.experimental.pallas import tpu as pltpu
from jax.sharding import PartitionSpec as P

LEAPS = 2
GROUP = 4
UNROLL = 4


degrees_free = 4.0
noise_scale = 0.5
prior_weight = 1.0
step_size = 0.01


def load_kernel(targ_group, shape, pair_ref, live_ref, values_hbm, weight_hbm, *refs):
    values_out, weight_out, lists_ref, sems = refs
    pairs, comp_tiles, targ_tiles = shape
    slots = values_hbm.shape[0]
    chunks = sems.shape[1]
    chunk = slots // chunks

    def copies(index):
        part = pl.ds(index * chunk, chunk)
        return (
            pltpu.make_async_copy(values_hbm.at[part], values_out.at[part], sems.at[0, index]),
            pltpu.make_async_copy(weight_hbm.at[part], weight_out.at[part], sems.at[1, index]),
        )

    for index in range(chunks):

        @pl.when(index * chunk < live_ref[0])
        def _():
            for copy in copies(index):
                copy.start()

    values_out[slots] = jnp.zeros_like(values_out[slots])
    weight_out[slots] = jnp.zeros_like(weight_out[slots])

    across = jnp.broadcast_to(pair_ref[...].astype(jnp.float32), (slots, slots))
    down = across.T
    at = lax.broadcasted_iota(jnp.int32, (slots, slots), 1).astype(jnp.float32)
    mine = lax.broadcasted_iota(jnp.int32, (slots, slots), 0).astype(jnp.float32)
    spare = float(comp_tiles * targ_group)
    same = down == across

    def count(mask, axis):
        return jnp.sum(jnp.where(mask, 1.0, 0.0), axis=axis, keepdims=True)

    earlier = count(same & (mine < at), 0)
    groups = jnp.floor((count(same, 0) + (GROUP - 1.0)) * (1.0 / GROUP))
    opens = (earlier == 0.0) & (across[:1] < spare)
    before = across < down
    rank = jnp.sum(jnp.where(before & opens, 1.0, 0.0), axis=1, keepdims=True)
    first = jnp.sum(jnp.where(before & opens, groups, 0.0), axis=1, keepdims=True)
    pair = down[:, :1]
    earlier = count(same & (at < mine), 1)
    alive = pair < spare
    opens = (earlier == 0.0) & alive
    step = jnp.floor(earlier * (1.0 / GROUP))
    place = jnp.where(alive, first + step, -1.0)
    member = earlier - GROUP * step
    groups = jnp.floor((count(same, 1) + (GROUP - 1.0)) * (1.0 / GROUP))

    def pick(mask, value, rest):
        return jnp.sum(jnp.where(mask, value - rest, 0.0), axis=0, keepdims=True) + rest

    here = place == at
    comp_tile = jnp.floor((pair + 0.5) * (1.0 / targ_group))
    rows = [pick(here & (member == n), mine[:, :1], float(slots)) for n in range(GROUP)]
    rows.append(pick(here & (member == 0.0), rank, float(pairs)))
    here = (rank == at) & opens
    rows.append(pick(here, comp_tile, float(comp_tiles)))
    rows.append(pick(here, pair - targ_group * comp_tile, float(targ_tiles)))
    totals = [jnp.sum(jnp.where(opens, n, 0.0), axis=0, keepdims=True) for n in (groups, 1.0)]
    rows.append(jnp.where(at[:1] == 0.0, totals[0], totals[1]))
    lists_ref[...] = jnp.concatenate(rows, axis=0).astype(jnp.int32)

    for index in range(chunks):

        @pl.when(index * chunk < live_ref[0])
        def _():
            for copy in copies(index):
                copy.wait()


def force_kernel(cols, rows, lists_ref, *refs):
    comp_blocks, refs = refs[: cols // 2], refs[cols // 2 :]
    targ_blocks, refs = refs[:rows], refs[rows:]
    values_ref, weight_ref, refs = refs[0], refs[1], refs[2:]
    comp_outs, refs = refs[: cols // 2], refs[cols // 2 :]
    targ_outs, refs = refs[:rows], refs[rows:]
    pred, total, comp_tiles, comp_flip, targ_tiles, targ_flip, comp_acc, targ_acc = refs
    side = values_ref.shape[1]
    comp_rows, targ_rows = comp_blocks[0].shape[0] // 2, targ_blocks[0].shape[0]
    comp_per, targ_per = comp_rows // side, targ_rows // side

    def fill(spot, tile, tiles, flip, acc):
        tiles[spot] = tile
        flip[spot] = tile.T
        acc[spot] = jnp.zeros(acc.shape[1:], acc.dtype)

    for n in range(rows):
        for i in range(targ_per):
            tile = targ_blocks[n][i * side : (i + 1) * side]
            fill(n * targ_per + i, tile, targ_tiles, targ_flip, targ_acc)
    for n in range(cols):
        for i in range(comp_per):
            start = (n % 2 * comp_per + i) * side
            tile = comp_blocks[n // 2][start : start + side]
            fill(n * comp_per + i, tile, comp_tiles, comp_flip, comp_acc)

    def steps(count):
        return lax.div(count + (UNROLL - 1), UNROLL)

    def pair_at(step):
        spots = [step * UNROLL + n for n in range(UNROLL)]
        return [(spot, lists_ref[GROUP + 1, spot], lists_ref[GROUP + 2, spot]) for spot in spots]

    last = pred.shape[0] - 1
    pairs, groups = lists_ref[GROUP + 3, 1], lists_ref[GROUP + 3, 0]

    def predict(step, unused):
        blocks = [
            (spot, jnp.dot(comp_tiles[i], targ_flip[j], preferred_element_type=jnp.float32))
            for spot, i, j in pair_at(step)
        ]
        for spot, block in blocks:
            spot = jnp.minimum(spot, last)
            pred[spot] = block.astype(pred.dtype)
            total[spot] = jnp.zeros(total.shape[1:], total.dtype)
        return unused

    lax.fori_loop(0, steps(pairs), predict, 0)

    one = degrees_free * noise_scale * noise_scale

    def weigh(step, unused):
        sums = []
        for n in range(UNROLL):
            group = step * UNROLL + n
            spot = lists_ref[GROUP, group]
            guess = pred[spot].astype(jnp.float32)
            whole = None
            for m in range(GROUP):
                slot = lists_ref[m, group]
                resid = values_ref[slot].astype(jnp.float32) - guess
                inverse = pl.reciprocal(one + resid * resid, approx=True)
                scaled = resid * weight_ref[slot].astype(jnp.float32) * inverse
                whole = scaled if whole is None else whole + scaled
            sums.append((spot, whole))
        for spot, whole in sums:
            total[spot] += whole
        return unused

    lax.fori_loop(0, steps(groups), weigh, 0)

    def gather(step, unused):
        parts = []
        for spot, i, j in pair_at(step):
            weights = total[jnp.minimum(spot, last)].astype(jnp.bfloat16)
            comp_part = jnp.dot(weights, targ_tiles[j], preferred_element_type=jnp.float32)
            targ_part = jnp.dot(comp_flip[i], weights, preferred_element_type=jnp.float32)
            parts.append((i, comp_part, j, targ_part))
        for i, comp_part, j, targ_part in parts:
            comp_acc[i] += comp_part
            targ_acc[j] += targ_part
        return unused

    lax.fori_loop(0, steps(pairs), gather, 0)

    gain = degrees_free + 1.0
    for n in range(cols):
        out = comp_outs[n // 2]
        for i in range(comp_per):
            part = comp_acc[n * comp_per + i] * gain
            start = (n % 2 * comp_per + i) * side
            out[start : start + side] = part.astype(out.dtype)
    for n in range(rows):
        out = targ_outs[n]
        for i in range(targ_per):
            part = targ_acc[n * targ_per + i] * gain
            out[i * side : (i + 1) * side] = part.T.astype(out.dtype)


smem = pl.BlockSpec(memory_space=pltpu.SMEM)
vmem = pl.BlockSpec(memory_space=pltpu.VMEM)
hbm = pl.BlockSpec(memory_space=pltpu.HBM)


def load_tiles(pairs, live, targ_group, shape, values, weight):
    slots, side, width = values.shape
    chunks = slots // math.gcd(slots, 16)
    held = pltpu.VMEM((slots + 1, side, width), values.dtype)
    values, weight = (pltpu.with_memory_space_constraint(x, pltpu.HBM) for x in (values, weight))
    return pl.pallas_call(
        functools.partial(load_kernel, targ_group, shape),
        out_shape=[held, held, jax.ShapeDtypeStruct((GROUP + 4, slots), jnp.int32)],
        in_specs=[vmem, smem, hbm, hbm],
        out_specs=[vmem] * 3,
        scratch_shapes=[pltpu.SemaphoreType.DMA((2, chunks))],
        compiler_params=pltpu.CompilerParams(vmem_limit_bytes=24 * 2**20),
        name="tile_load",
    )(pairs, live, values, weight)


def local_grads(lists, comp_blocks, targ_blocks, values, weight, pairs):
    cols, rows = 2 * len(comp_blocks), len(targ_blocks)
    comp_rows, rank = comp_blocks[0].shape[0] // 2, comp_blocks[0].shape[1]
    targ_rows = targ_blocks[0].shape[0]
    side = values.shape[1]
    comp_tiles, targ_tiles = cols * comp_rows // side, rows * targ_rows // side
    comp_shape = jax.ShapeDtypeStruct((2 * comp_rows, rank), jnp.bfloat16)
    targ_shape = jax.ShapeDtypeStruct((targ_rows, rank), jnp.bfloat16)
    held = (pairs + 1) * side * side * 6 + (comp_tiles + targ_tiles + 2) * side * rank * 8
    held += 4 * values.size
    outs = pl.pallas_call(
        functools.partial(force_kernel, cols, rows),
        out_shape=[comp_shape] * (cols // 2) + [targ_shape] * rows,
        in_specs=[smem] + [vmem] * (cols // 2 + rows + 2),
        out_specs=[vmem] * (cols // 2 + rows),
        scratch_shapes=[
            pltpu.VMEM((pairs + 1, side, side), jnp.bfloat16),
            pltpu.VMEM((pairs + 1, side, side), jnp.float32),
            pltpu.VMEM((comp_tiles + 1, side, rank), jnp.bfloat16),
            pltpu.VMEM((comp_tiles + 1, rank, side), jnp.bfloat16),
            pltpu.VMEM((targ_tiles + 1, side, rank), jnp.bfloat16),
            pltpu.VMEM((targ_tiles + 1, rank, side), jnp.bfloat16),
            pltpu.VMEM((comp_tiles + 1, side, rank), jnp.float32),
            pltpu.VMEM((targ_tiles + 1, rank, side), jnp.float32),
        ],
        compiler_params=pltpu.CompilerParams(vmem_limit_bytes=held + 4 * 2**20),
        name="tile_force",
    )(lists, *comp_blocks, *targ_blocks, values, weight)
    return outs[: cols // 2], outs[cols // 2 :]


def swap(block, axis, offset):
    size = lax.axis_size(axis)
    return lax.ppermute(block, axis, [(i, i ^ offset) for i in range(size)])


def spread(block, axis):
    return [block] + [swap(block, axis, offset) for offset in range(1, lax.axis_size(axis))]


def collect(blocks, axis):
    whole = blocks[0].astype(jnp.float32)
    for offset, block in enumerate(blocks[1:]):
        whole = whole + swap(block, axis, offset + 1).astype(jnp.float32)
    return whole


def spread_pairs(both, axis):
    size = lax.axis_size(axis)
    return [both] + [swap(both, axis, offset) for offset in range(2, size, 2)]


def with_mate(block, axis):
    return jnp.concatenate([block, swap(block, axis, 1)])


def collect_pairs(blocks, axis, last):
    both = blocks[0].astype(jnp.float32)
    for n, block in enumerate(blocks[1:]):
        both = both + swap(block, axis, 2 * n + 2).astype(jnp.float32)
    low = both.astype(blocks[0].dtype)
    mine, other = jnp.split(low, 2)
    if last:
        return mine.astype(jnp.float32) + swap(other, axis, 1).astype(jnp.float32)
    got_other, got_mine = jnp.split(swap(low, axis, 1), 2)
    return low.astype(jnp.float32) + jnp.concatenate([got_mine, got_other]).astype(jnp.float32)


def body(
    compound_pos,
    compound_mom,
    target_pos,
    target_mom,
    tile_rows,
    tile_cols,
    tile_count,
    tile_values,
    tile_weight,
):
    side = tile_values.shape[2]
    comp_per = compound_pos.shape[0] // side
    targ_per = target_pos.shape[0] // side
    cols, rows = lax.axis_size("col"), lax.axis_size("row")
    col_index, row_index = lax.axis_index("col"), lax.axis_index("row")
    assert cols & (cols - 1) == 0 and rows & (rows - 1) == 0
    comp_local = tile_rows[0] - row_index * (cols * comp_per)
    comp_place = ((comp_local // comp_per) ^ col_index) * comp_per + comp_local % comp_per
    holder = tile_cols[0] // targ_per // cols
    targ_place = (holder ^ row_index) * targ_per + tile_cols[0] % targ_per
    targ_group = rows * targ_per
    alive = jnp.arange(tile_values.shape[1], dtype=jnp.int32) < tile_count[0]
    spare = cols * comp_per * targ_group
    slots = jnp.where(alive, comp_place * targ_group + targ_place, spare)

    shape = (min(spare, slots.shape[0]), cols * comp_per, targ_group)
    values, weight, lists = load_tiles(
        slots[None], tile_count, targ_group, shape, tile_values[0], tile_weight[0]
    )

    def forces(comp, targ, last=False):
        comp_parts, targ_parts = local_grads(
            lists,
            spread_pairs(comp.astype(jnp.bfloat16), "col"),
            spread(targ.astype(jnp.bfloat16), "row"),
            values,
            weight,
            shape[0],
        )
        comp_sum = collect_pairs(comp_parts, "col", last)
        targ_sum = collect(targ_parts, "row")
        return comp_sum - prior_weight * comp[: comp_sum.shape[0]], targ_sum - prior_weight * targ

    places = (with_mate(compound_pos, "col"), target_pos)
    speeds = (with_mate(compound_mom, "col"), target_mom)
    push = forces(*places)
    for leap in range(LEAPS):
        scale = (0.5 if leap == 0 else 1.0) * step_size
        speeds = tuple(p + scale * f for p, f in zip(speeds, push))
        places = tuple(q + step_size * p for q, p in zip(places, speeds))
        push = forces(*places, last=leap == LEAPS - 1)
    own = compound_pos.shape[0]
    places, speeds = ((comp[:own], targ) for comp, targ in (places, speeds))
    speeds = tuple(p + 0.5 * step_size * f for p, f in zip(speeds, push))
    return (places[0], speeds[0], places[1], speeds[1])


def solution(mesh):
    split = P(("row", "col"), None)
    tiles = P(("row", "col"), None, None, None)
    return jax.shard_map(
        body,
        mesh=mesh,
        in_specs=(split,) * 6 + (P(("row", "col")), tiles, tiles),
        out_specs=(split,) * 4,
        check_vma=False,
    )
```

```python
import functools
import math

import jax
import jax.numpy as jnp
from jax import lax
from jax.experimental import pallas as pl
from jax.experimental.pallas import tpu as pltpu
from jax.sharding import PartitionSpec as P

LEAPS = 2
GROUP = 4
UNROLL = 4
SCALE = 2.0**-20


degrees_free = 4.0
noise_scale = 0.5
prior_weight = 1.0
step_size = 0.01


def load_kernel(targ_group, shape, pair_ref, live_ref, values_hbm, weight_hbm, *refs):
    values_out, weight_out, lists_ref, sems = refs
    pairs, comp_tiles, targ_tiles = shape
    slots = values_hbm.shape[0]
    chunks = sems.shape[1]
    chunk = slots // chunks

    def copies(index):
        part = pl.ds(index * chunk, chunk)
        return (
            pltpu.make_async_copy(values_hbm.at[part], values_out.at[part], sems.at[0, index]),
            pltpu.make_async_copy(weight_hbm.at[part], weight_out.at[part], sems.at[1, index]),
        )

    for index in range(chunks):

        @pl.when(index * chunk < live_ref[0])
        def _():
            for copy in copies(index):
                copy.start()

    values_out[slots] = jnp.zeros_like(values_out[slots])
    weight_out[slots] = jnp.zeros_like(weight_out[slots])

    across = jnp.broadcast_to(pair_ref[...].astype(jnp.float32), (slots, slots))
    down = across.T
    at = lax.broadcasted_iota(jnp.int32, (slots, slots), 1).astype(jnp.float32)
    mine = lax.broadcasted_iota(jnp.int32, (slots, slots), 0).astype(jnp.float32)
    spare = float(comp_tiles * targ_group)
    same = down == across

    def count(mask, axis):
        return jnp.sum(jnp.where(mask, 1.0, 0.0), axis=axis, keepdims=True)

    earlier = count(same & (mine < at), 0)
    groups = jnp.floor((count(same, 0) + (GROUP - 1.0)) * (1.0 / GROUP))
    opens = (earlier == 0.0) & (across[:1] < spare)
    before = across < down
    rank = jnp.sum(jnp.where(before & opens, 1.0, 0.0), axis=1, keepdims=True)
    first = jnp.sum(jnp.where(before & opens, groups, 0.0), axis=1, keepdims=True)
    pair = down[:, :1]
    earlier = count(same & (at < mine), 1)
    alive = pair < spare
    opens = (earlier == 0.0) & alive
    step = jnp.floor(earlier * (1.0 / GROUP))
    place = jnp.where(alive, first + step, -1.0)
    member = earlier - GROUP * step
    groups = jnp.floor((count(same, 1) + (GROUP - 1.0)) * (1.0 / GROUP))

    def pick(mask, value, rest):
        return jnp.sum(jnp.where(mask, value - rest, 0.0), axis=0, keepdims=True) + rest

    here = place == at
    comp_tile = jnp.floor((pair + 0.5) * (1.0 / targ_group))
    rows = [pick(here & (member == n), mine[:, :1], float(slots)) for n in range(GROUP)]
    rows.append(pick(here & (member == 0.0), rank, float(pairs)))
    here = (rank == at) & opens
    rows.append(pick(here, comp_tile, float(comp_tiles)))
    rows.append(pick(here, pair - targ_group * comp_tile, float(targ_tiles)))
    totals = [jnp.sum(jnp.where(opens, n, 0.0), axis=0, keepdims=True) for n in (groups, 1.0)]
    rows.append(jnp.where(at[:1] == 0.0, totals[0], totals[1]))
    lists_ref[...] = jnp.concatenate(rows, axis=0).astype(jnp.int32)

    for index in range(chunks):

        @pl.when(index * chunk < live_ref[0])
        def _():
            for copy in copies(index):
                copy.wait()


def force_kernel(cols, rows, lists_ref, *refs):
    comp_firsts, refs = refs[: cols // 2], refs[cols // 2 :]
    comp_seconds, refs = refs[: cols // 2], refs[cols // 2 :]
    targ_blocks, refs = refs[:rows], refs[rows:]
    values_ref, weight_ref, refs = refs[0], refs[1], refs[2:]
    comp_keep, comp_send, refs = refs[0], refs[1], refs[2:]
    targ_outs, refs = refs[:rows], refs[rows:]
    pred, total, comp_tiles, comp_flip, targ_tiles, targ_flip, comp_acc, targ_acc = refs
    side = values_ref.shape[1]
    comp_rows, targ_rows = comp_firsts[0].shape[0], targ_blocks[0].shape[0]
    comp_per, targ_per = comp_rows // side, targ_rows // side

    def fill(spot, tile, tiles, flip, acc):
        tiles[spot] = tile
        flip[spot] = tile.T
        acc[spot] = jnp.zeros(acc.shape[1:], acc.dtype)

    for n in range(rows):
        for i in range(targ_per):
            tile = targ_blocks[n][i * side : (i + 1) * side]
            fill(n * targ_per + i, tile, targ_tiles, targ_flip, targ_acc)
    for n in range(cols):
        for i in range(comp_per):
            tile = (comp_seconds if n % 2 else comp_firsts)[n // 2][i * side : (i + 1) * side]
            fill(n * comp_per + i, tile, comp_tiles, comp_flip, comp_acc)

    def steps(count):
        return lax.div(count + (UNROLL - 1), UNROLL)

    def pair_at(step):
        spots = [step * UNROLL + n for n in range(UNROLL)]
        return [(spot, lists_ref[GROUP + 1, spot], lists_ref[GROUP + 2, spot]) for spot in spots]

    last = pred.shape[0] - 1
    pairs, groups = lists_ref[GROUP + 3, 1], lists_ref[GROUP + 3, 0]

    def predict(step, unused):
        blocks = [
            (spot, jnp.dot(comp_tiles[i], targ_flip[j], preferred_element_type=jnp.float32))
            for spot, i, j in pair_at(step)
        ]
        for spot, block in blocks:
            spot = jnp.minimum(spot, last)
            pred[spot] = block.astype(pred.dtype)
            total[spot] = jnp.zeros(total.shape[1:], total.dtype)
        return unused

    lax.fori_loop(0, steps(pairs), predict, 0)

    one = jnp.asarray(degrees_free * noise_scale * noise_scale, pred.dtype)

    def weigh(step, unused):
        sums = []
        for n in range(UNROLL):
            group = step * UNROLL + n
            spot = lists_ref[GROUP, group]
            guess = pred[spot]
            whole = None
            for m in range(0, GROUP, 2):
                slots = lists_ref[m, group], lists_ref[m + 1, group]
                left, right = (values_ref[slot] - guess for slot in slots)
                small = right * SCALE
                left_top, left_low = left * weight_ref[slots[0]], left * left + one
                right_top, right_low = small * weight_ref[slots[1]], small * right + one * SCALE
                top = left_top * right_low + right_top * left_low
                both = top * pl.reciprocal(left_low * right_low, approx=True)
                whole = both if whole is None else whole + both
            sums.append((spot, whole))
        for spot, whole in sums:
            total[spot] += whole.astype(total.dtype)
        return unused

    lax.fori_loop(0, steps(groups), weigh, 0)

    def gather(step, unused):
        parts = []
        for spot, i, j in pair_at(step):
            weights = total[jnp.minimum(spot, last)].astype(jnp.bfloat16)
            comp_part = jnp.dot(weights, targ_tiles[j], preferred_element_type=jnp.float32)
            targ_part = jnp.dot(comp_flip[i], weights, preferred_element_type=jnp.float32)
            parts.append((i, comp_part, j, targ_part))
        for i, comp_part, j, targ_part in parts:
            comp_acc[i] += comp_part
            targ_acc[j] += targ_part
        return unused

    lax.fori_loop(0, steps(pairs), gather, 0)

    gain = degrees_free + 1.0
    for n in range(cols):
        out = comp_send if n % 2 else comp_keep
        for i in range(comp_per):
            part = comp_acc[n * comp_per + i] * gain
            out[n // 2, i * side : (i + 1) * side] = part.astype(out.dtype)
    for n in range(rows):
        out = targ_outs[n]
        for i in range(targ_per):
            part = targ_acc[n * targ_per + i] * gain
            out[i * side : (i + 1) * side] = part.T.astype(out.dtype)


smem = pl.BlockSpec(memory_space=pltpu.SMEM)
vmem = pl.BlockSpec(memory_space=pltpu.VMEM)
hbm = pl.BlockSpec(memory_space=pltpu.HBM)


def load_tiles(pairs, live, targ_group, shape, values, weight):
    slots, side, width = values.shape
    chunks = slots // math.gcd(slots, 16)
    held = pltpu.VMEM((slots + 1, side, width), values.dtype)
    values, weight = (pltpu.with_memory_space_constraint(x, pltpu.HBM) for x in (values, weight))
    return pl.pallas_call(
        functools.partial(load_kernel, targ_group, shape),
        out_shape=[held, held, jax.ShapeDtypeStruct((GROUP + 4, slots), jnp.int32)],
        in_specs=[vmem, smem, hbm, hbm],
        out_specs=[vmem] * 3,
        scratch_shapes=[pltpu.SemaphoreType.DMA((2, chunks))],
        compiler_params=pltpu.CompilerParams(vmem_limit_bytes=24 * 2**20),
        name="tile_load",
    )(pairs, live, values, weight)


def local_grads(lists, comp_firsts, comp_seconds, targ_blocks, values, weight, pairs):
    cols, rows = 2 * len(comp_firsts), len(targ_blocks)
    comp_rows, rank = comp_firsts[0].shape
    targ_rows = targ_blocks[0].shape[0]
    side = values.shape[1]
    comp_tiles, targ_tiles = cols * comp_rows // side, rows * targ_rows // side
    comp_shape = jax.ShapeDtypeStruct((cols // 2, comp_rows, rank), jnp.bfloat16)
    targ_shape = jax.ShapeDtypeStruct((targ_rows, rank), jnp.bfloat16)
    held = (pairs + 1) * side * side * 6 + (comp_tiles + targ_tiles + 2) * side * rank * 8
    held += 4 * values.size
    outs = pl.pallas_call(
        functools.partial(force_kernel, cols, rows),
        out_shape=[comp_shape] * 2 + [targ_shape] * rows,
        in_specs=[smem] + [vmem] * (cols + rows + 2),
        out_specs=[vmem] * (2 + rows),
        scratch_shapes=[
            pltpu.VMEM((pairs + 1, side, side), jnp.bfloat16),
            pltpu.VMEM((pairs + 1, side, side), jnp.float32),
            pltpu.VMEM((comp_tiles + 1, side, rank), jnp.bfloat16),
            pltpu.VMEM((comp_tiles + 1, rank, side), jnp.bfloat16),
            pltpu.VMEM((targ_tiles + 1, side, rank), jnp.bfloat16),
            pltpu.VMEM((targ_tiles + 1, rank, side), jnp.bfloat16),
            pltpu.VMEM((comp_tiles + 1, side, rank), jnp.float32),
            pltpu.VMEM((targ_tiles + 1, rank, side), jnp.float32),
        ],
        compiler_params=pltpu.CompilerParams(vmem_limit_bytes=held + 4 * 2**20),
        name="tile_force",
    )(lists, *comp_firsts, *comp_seconds, *targ_blocks, values, weight)
    return outs[0], outs[1], outs[2:]


def swap(block, axis, offset):
    size = lax.axis_size(axis)
    return lax.ppermute(block, axis, [(i, i ^ offset) for i in range(size)])


def spread(block, axis):
    return [block] + [swap(block, axis, offset) for offset in range(1, lax.axis_size(axis))]


def collect(blocks, axis):
    whole = blocks[0].astype(jnp.float32)
    for offset, block in enumerate(blocks[1:]):
        whole = whole + swap(block, axis, offset + 1).astype(jnp.float32)
    return whole


def spread_pairs(block, axis):
    firsts = [block]
    firsts += [swap(block, axis, offset) for offset in range(2, lax.axis_size(axis), 2)]
    return firsts, [swap(block, axis, 1) for block in firsts]


def collect_pairs(keep, send, axis):
    got = swap(send, axis, 1)
    both = [
        keep[n].astype(jnp.float32) + got[n].astype(jnp.float32) for n in range(keep.shape[0])
    ]
    whole = both[0]
    for n, block in enumerate(both[1:]):
        whole = whole + swap(block.astype(keep.dtype), axis, 2 * n + 2).astype(jnp.float32)
    return whole


def body(
    compound_pos,
    compound_mom,
    target_pos,
    target_mom,
    tile_rows,
    tile_cols,
    tile_count,
    tile_values,
    tile_weight,
):
    side = tile_values.shape[2]
    comp_per = compound_pos.shape[0] // side
    targ_per = target_pos.shape[0] // side
    cols, rows = lax.axis_size("col"), lax.axis_size("row")
    col_index, row_index = lax.axis_index("col"), lax.axis_index("row")
    assert cols & (cols - 1) == 0 and rows & (rows - 1) == 0
    comp_local = tile_rows[0] - row_index * (cols * comp_per)
    comp_place = ((comp_local // comp_per) ^ col_index) * comp_per + comp_local % comp_per
    holder = tile_cols[0] // targ_per // cols
    targ_place = (holder ^ row_index) * targ_per + tile_cols[0] % targ_per
    targ_group = rows * targ_per
    alive = jnp.arange(tile_values.shape[1], dtype=jnp.int32) < tile_count[0]
    spare = cols * comp_per * targ_group
    slots = jnp.where(alive, comp_place * targ_group + targ_place, spare)

    shape = (min(spare, slots.shape[0]), cols * comp_per, targ_group)
    values, weight, lists = load_tiles(
        slots[None], tile_count, targ_group, shape, tile_values[0], tile_weight[0]
    )

    def forces(comp, targ):
        comp_keep, comp_send, targ_parts = local_grads(
            lists,
            *spread_pairs(comp.astype(jnp.bfloat16), "col"),
            spread(targ.astype(jnp.bfloat16), "row"),
            values,
            weight,
            shape[0],
        )
        comp_sum = collect_pairs(comp_keep, comp_send, "col")
        targ_sum = collect(targ_parts, "row")
        return comp_sum - prior_weight * comp, targ_sum - prior_weight * targ

    places = (compound_pos, target_pos)
    speeds = (compound_mom, target_mom)
    push = forces(*places)
    for leap in range(LEAPS):
        scale = (0.5 if leap == 0 else 1.0) * step_size
        speeds = tuple(p + scale * f for p, f in zip(speeds, push))
        places = tuple(q + step_size * p for q, p in zip(places, speeds))
        push = forces(*places)
    speeds = tuple(p + 0.5 * step_size * f for p, f in zip(speeds, push))
    return (places[0], speeds[0], places[1], speeds[1])


def solution(mesh):
    split = P(("row", "col"), None)
    tiles = P(("row", "col"), None, None, None)
    return jax.shard_map(
        body,
        mesh=mesh,
        in_specs=(split,) * 6 + (P(("row", "col")), tiles, tiles),
        out_specs=(split,) * 4,
        check_vma=False,
    )
```

```python
import functools
import math

import jax
import jax.numpy as jnp
from jax import lax
from jax.experimental import pallas as pl
from jax.experimental.pallas import tpu as pltpu
from jax.sharding import PartitionSpec as P

LEAPS = 2
GROUP = 4
UNROLL = 4


degrees_free = 4.0
noise_scale = 0.5
prior_weight = 1.0
step_size = 0.01


def load_kernel(targ_group, shape, pair_ref, live_ref, values_hbm, weight_hbm, *refs):
    values_out, weight_out, lists_ref, sems = refs
    pairs, comp_tiles, targ_tiles = shape
    slots = values_hbm.shape[0]
    chunks = sems.shape[1]
    chunk = slots // chunks

    def copies(index):
        part = pl.ds(index * chunk, chunk)
        return (
            pltpu.make_async_copy(values_hbm.at[part], values_out.at[part], sems.at[0, index]),
            pltpu.make_async_copy(weight_hbm.at[part], weight_out.at[part], sems.at[1, index]),
        )

    for index in range(chunks):

        @pl.when(index * chunk < live_ref[0])
        def _():
            for copy in copies(index):
                copy.start()

    values_out[slots] = jnp.zeros_like(values_out[slots])
    weight_out[slots] = jnp.zeros_like(weight_out[slots])

    across = jnp.broadcast_to(pair_ref[...].astype(jnp.float32), (slots, slots))
    down = across.T
    at = lax.broadcasted_iota(jnp.int32, (slots, slots), 1).astype(jnp.float32)
    mine = lax.broadcasted_iota(jnp.int32, (slots, slots), 0).astype(jnp.float32)
    spare = float(comp_tiles * targ_group)
    same = down == across

    def count(mask, axis):
        return jnp.sum(jnp.where(mask, 1.0, 0.0), axis=axis, keepdims=True)

    earlier = count(same & (mine < at), 0)
    groups = jnp.floor((count(same, 0) + (GROUP - 1.0)) * (1.0 / GROUP))
    opens = (earlier == 0.0) & (across[:1] < spare)
    before = across < down
    rank = jnp.sum(jnp.where(before & opens, 1.0, 0.0), axis=1, keepdims=True)
    first = jnp.sum(jnp.where(before & opens, groups, 0.0), axis=1, keepdims=True)
    pair = down[:, :1]
    earlier = count(same & (at < mine), 1)
    alive = pair < spare
    opens = (earlier == 0.0) & alive
    step = jnp.floor(earlier * (1.0 / GROUP))
    place = jnp.where(alive, first + step, -1.0)
    member = earlier - GROUP * step
    groups = jnp.floor((count(same, 1) + (GROUP - 1.0)) * (1.0 / GROUP))

    def pick(mask, value, rest):
        return jnp.sum(jnp.where(mask, value - rest, 0.0), axis=0, keepdims=True) + rest

    here = place == at
    comp_tile = jnp.floor((pair + 0.5) * (1.0 / targ_group))
    rows = [pick(here & (member == n), mine[:, :1], float(slots)) for n in range(GROUP)]
    rows.append(pick(here & (member == 0.0), rank, float(pairs)))
    here = (rank == at) & opens
    rows.append(pick(here, comp_tile, float(comp_tiles)))
    rows.append(pick(here, pair - targ_group * comp_tile, float(targ_tiles)))
    totals = [jnp.sum(jnp.where(opens, n, 0.0), axis=0, keepdims=True) for n in (groups, 1.0)]
    rows.append(jnp.where(at[:1] == 0.0, totals[0], totals[1]))
    lists_ref[...] = jnp.concatenate(rows, axis=0).astype(jnp.int32)

    for index in range(chunks):

        @pl.when(index * chunk < live_ref[0])
        def _():
            for copy in copies(index):
                copy.wait()


def force_kernel(cols, rows, lists_ref, *refs):
    comp_firsts, refs = refs[: cols // 2], refs[cols // 2 :]
    comp_seconds, refs = refs[: cols // 2], refs[cols // 2 :]
    targ_blocks, refs = refs[:rows], refs[rows:]
    values_ref, weight_ref, refs = refs[0], refs[1], refs[2:]
    comp_keep, comp_send, refs = refs[0], refs[1], refs[2:]
    targ_outs, refs = refs[:rows], refs[rows:]
    pred, total, comp_tiles, comp_flip, targ_tiles, targ_flip, comp_acc, targ_acc = refs
    side = values_ref.shape[1]
    comp_rows, targ_rows = comp_firsts[0].shape[0], targ_blocks[0].shape[0]
    comp_per, targ_per = comp_rows // side, targ_rows // side

    def fill(spot, tile, tiles, flip, acc):
        tiles[spot] = tile
        flip[spot] = tile.T
        acc[spot] = jnp.zeros(acc.shape[1:], acc.dtype)

    for n in range(rows):
        for i in range(targ_per):
            tile = targ_blocks[n][i * side : (i + 1) * side]
            fill(n * targ_per + i, tile, targ_tiles, targ_flip, targ_acc)
    for n in range(cols):
        for i in range(comp_per):
            tile = (comp_seconds if n % 2 else comp_firsts)[n // 2][i * side : (i + 1) * side]
            fill(n * comp_per + i, tile, comp_tiles, comp_flip, comp_acc)

    def steps(count):
        return lax.div(count + (UNROLL - 1), UNROLL)

    def pair_at(step):
        spots = [step * UNROLL + n for n in range(UNROLL)]
        return [(spot, lists_ref[GROUP + 1, spot], lists_ref[GROUP + 2, spot]) for spot in spots]

    last = pred.shape[0] - 1
    pairs, groups = lists_ref[GROUP + 3, 1], lists_ref[GROUP + 3, 0]

    def predict(step, unused):
        blocks = [
            (spot, jnp.dot(comp_tiles[i], targ_flip[j], preferred_element_type=jnp.float32))
            for spot, i, j in pair_at(step)
        ]
        for spot, block in blocks:
            spot = jnp.minimum(spot, last)
            pred[spot] = block.astype(pred.dtype)
            total[spot] = jnp.zeros(total.shape[1:], total.dtype)
        return unused

    lax.fori_loop(0, steps(pairs), predict, 0)

    one = degrees_free * noise_scale * noise_scale

    def weigh(step, unused):
        sums = []
        for n in range(UNROLL):
            group = step * UNROLL + n
            spot = lists_ref[GROUP, group]
            guess = pred[spot].astype(jnp.float32)
            whole = None
            for m in range(GROUP):
                slot = lists_ref[m, group]
                resid = values_ref[slot].astype(jnp.float32) - guess
                inverse = pl.reciprocal(one + resid * resid, approx=True)
                scaled = resid * weight_ref[slot].astype(jnp.float32) * inverse
                whole = scaled if whole is None else whole + scaled
            sums.append((spot, whole))
        for spot, whole in sums:
            total[spot] += whole
        return unused

    lax.fori_loop(0, steps(groups), weigh, 0)

    def gather(step, unused):
        parts = []
        for spot, i, j in pair_at(step):
            weights = total[jnp.minimum(spot, last)].astype(jnp.bfloat16)
            comp_part = jnp.dot(weights, targ_tiles[j], preferred_element_type=jnp.float32)
            targ_part = jnp.dot(comp_flip[i], weights, preferred_element_type=jnp.float32)
            parts.append((i, comp_part, j, targ_part))
        for i, comp_part, j, targ_part in parts:
            comp_acc[i] += comp_part
            targ_acc[j] += targ_part
        return unused

    lax.fori_loop(0, steps(pairs), gather, 0)

    gain = degrees_free + 1.0
    for n in range(cols):
        out = comp_send if n % 2 else comp_keep
        for i in range(comp_per):
            part = comp_acc[n * comp_per + i] * gain
            out[n // 2, i * side : (i + 1) * side] = part.astype(out.dtype)
    for n in range(rows):
        out = targ_outs[n]
        for i in range(targ_per):
            part = targ_acc[n * targ_per + i] * gain
            out[i * side : (i + 1) * side] = part.T.astype(out.dtype)


smem = pl.BlockSpec(memory_space=pltpu.SMEM)
vmem = pl.BlockSpec(memory_space=pltpu.VMEM)
hbm = pl.BlockSpec(memory_space=pltpu.HBM)


def load_tiles(pairs, live, targ_group, shape, values, weight):
    slots, side, width = values.shape
    chunks = slots // math.gcd(slots, 16)
    held = pltpu.VMEM((slots + 1, side, width), values.dtype)
    values, weight = (pltpu.with_memory_space_constraint(x, pltpu.HBM) for x in (values, weight))
    return pl.pallas_call(
        functools.partial(load_kernel, targ_group, shape),
        out_shape=[held, held, jax.ShapeDtypeStruct((GROUP + 4, slots), jnp.int32)],
        in_specs=[vmem, smem, hbm, hbm],
        out_specs=[vmem] * 3,
        scratch_shapes=[pltpu.SemaphoreType.DMA((2, chunks))],
        compiler_params=pltpu.CompilerParams(vmem_limit_bytes=24 * 2**20),
        name="tile_load",
    )(pairs, live, values, weight)


def local_grads(lists, comp_firsts, comp_seconds, targ_blocks, values, weight, pairs):
    cols, rows = 2 * len(comp_firsts), len(targ_blocks)
    comp_rows, rank = comp_firsts[0].shape
    targ_rows = targ_blocks[0].shape[0]
    side = values.shape[1]
    comp_tiles, targ_tiles = cols * comp_rows // side, rows * targ_rows // side
    comp_shape = jax.ShapeDtypeStruct((cols // 2, comp_rows, rank), jnp.bfloat16)
    targ_shape = jax.ShapeDtypeStruct((targ_rows, rank), jnp.bfloat16)
    held = (pairs + 1) * side * side * 6 + (comp_tiles + targ_tiles + 2) * side * rank * 8
    held += 4 * values.size
    outs = pl.pallas_call(
        functools.partial(force_kernel, cols, rows),
        out_shape=[comp_shape] * 2 + [targ_shape] * rows,
        in_specs=[smem] + [vmem] * (cols + rows + 2),
        out_specs=[vmem] * (2 + rows),
        scratch_shapes=[
            pltpu.VMEM((pairs + 1, side, side), jnp.bfloat16),
            pltpu.VMEM((pairs + 1, side, side), jnp.float32),
            pltpu.VMEM((comp_tiles + 1, side, rank), jnp.bfloat16),
            pltpu.VMEM((comp_tiles + 1, rank, side), jnp.bfloat16),
            pltpu.VMEM((targ_tiles + 1, side, rank), jnp.bfloat16),
            pltpu.VMEM((targ_tiles + 1, rank, side), jnp.bfloat16),
            pltpu.VMEM((comp_tiles + 1, side, rank), jnp.float32),
            pltpu.VMEM((targ_tiles + 1, rank, side), jnp.float32),
        ],
        compiler_params=pltpu.CompilerParams(vmem_limit_bytes=held + 4 * 2**20),
        name="tile_force",
    )(lists, *comp_firsts, *comp_seconds, *targ_blocks, values, weight)
    return outs[0], outs[1], outs[2:]


def swap(block, axis, offset):
    size = lax.axis_size(axis)
    return lax.ppermute(block, axis, [(i, i ^ offset) for i in range(size)])


def spread(block, axis):
    size = lax.axis_size(axis)
    seconds = [block] + [swap(block, axis, offset) for offset in range(2, size, 2)]
    return [each for second in seconds for each in (second, swap(second, axis, 1))]


def collect(blocks, axis):
    whole = blocks[0].astype(jnp.float32)
    for offset in range(2, len(blocks), 2):
        near = swap(blocks[offset + 1], axis, 1).astype(jnp.float32)
        far = (blocks[offset].astype(jnp.float32) + near).astype(blocks[offset].dtype)
        whole = whole + swap(far, axis, offset).astype(jnp.float32)
    return whole + swap(blocks[1], axis, 1).astype(jnp.float32)


def spread_pairs(block, axis):
    firsts = [block]
    firsts += [swap(block, axis, offset) for offset in range(2, lax.axis_size(axis), 2)]
    return firsts, [swap(block, axis, 1) for block in firsts]


def collect_pairs(keep, send, axis):
    got = swap(send, axis, 1)
    both = [
        keep[n].astype(jnp.float32) + got[n].astype(jnp.float32) for n in range(keep.shape[0])
    ]
    whole = both[0]
    for n, block in enumerate(both[1:]):
        whole = whole + swap(block.astype(keep.dtype), axis, 2 * n + 2).astype(jnp.float32)
    return whole


def body(
    compound_pos,
    compound_mom,
    target_pos,
    target_mom,
    tile_rows,
    tile_cols,
    tile_count,
    tile_values,
    tile_weight,
):
    side = tile_values.shape[2]
    comp_per = compound_pos.shape[0] // side
    targ_per = target_pos.shape[0] // side
    cols, rows = lax.axis_size("col"), lax.axis_size("row")
    col_index, row_index = lax.axis_index("col"), lax.axis_index("row")
    assert cols & (cols - 1) == 0 and rows & (rows - 1) == 0
    comp_local = tile_rows[0] - row_index * (cols * comp_per)
    comp_place = ((comp_local // comp_per) ^ col_index) * comp_per + comp_local % comp_per
    holder = tile_cols[0] // targ_per // cols
    targ_place = (holder ^ row_index) * targ_per + tile_cols[0] % targ_per
    targ_group = rows * targ_per
    alive = jnp.arange(tile_values.shape[1], dtype=jnp.int32) < tile_count[0]
    spare = cols * comp_per * targ_group
    slots = jnp.where(alive, comp_place * targ_group + targ_place, spare)

    shape = (min(spare, slots.shape[0]), cols * comp_per, targ_group)
    values, weight, lists = load_tiles(
        slots[None], tile_count, targ_group, shape, tile_values[0], tile_weight[0]
    )

    def forces(comp, targ):
        comp_keep, comp_send, targ_parts = local_grads(
            lists,
            *spread_pairs(comp.astype(jnp.bfloat16), "col"),
            spread(targ.astype(jnp.bfloat16), "row"),
            values,
            weight,
            shape[0],
        )
        comp_sum = collect_pairs(comp_keep, comp_send, "col")
        targ_sum = collect(targ_parts, "row")
        return comp_sum - prior_weight * comp, targ_sum - prior_weight * targ

    places = (compound_pos, target_pos)
    speeds = (compound_mom, target_mom)
    push = forces(*places)
    for leap in range(LEAPS):
        scale = (0.5 if leap == 0 else 1.0) * step_size
        speeds = tuple(p + scale * f for p, f in zip(speeds, push))
        places = tuple(q + step_size * p for q, p in zip(places, speeds))
        push = forces(*places)
    speeds = tuple(p + 0.5 * step_size * f for p, f in zip(speeds, push))
    return (places[0], speeds[0], places[1], speeds[1])


def solution(mesh):
    split = P(("row", "col"), None)
    tiles = P(("row", "col"), None, None, None)
    return jax.shard_map(
        body,
        mesh=mesh,
        in_specs=(split,) * 6 + (P(("row", "col")), tiles, tiles),
        out_specs=(split,) * 4,
        check_vma=False,
    )
```

```python
import functools
import math

import jax
import jax.numpy as jnp
from jax import lax
from jax.experimental import pallas as pl
from jax.experimental.pallas import tpu as pltpu
from jax.sharding import PartitionSpec as P

LEAPS = 2
GROUP = 4
UNROLL = 4


degrees_free = 4.0
noise_scale = 0.5
prior_weight = 1.0
step_size = 0.01


def load_kernel(targ_group, shape, pair_ref, live_ref, values_hbm, weight_hbm, *refs):
    values_out, weight_out, lists_ref, sems = refs
    pairs, comp_tiles, targ_tiles = shape
    slots = values_hbm.shape[0]
    chunks = sems.shape[1]
    chunk = slots // chunks

    def copies(index):
        part = pl.ds(index * chunk, chunk)
        return (
            pltpu.make_async_copy(values_hbm.at[part], values_out.at[part], sems.at[0, index]),
            pltpu.make_async_copy(weight_hbm.at[part], weight_out.at[part], sems.at[1, index]),
        )

    for index in range(chunks):

        @pl.when(index * chunk < live_ref[0])
        def _():
            for copy in copies(index):
                copy.start()

    values_out[slots] = jnp.zeros_like(values_out[slots])
    weight_out[slots] = jnp.zeros_like(weight_out[slots])

    across = jnp.broadcast_to(pair_ref[...].astype(jnp.float32), (slots, slots))
    down = across.T
    at = lax.broadcasted_iota(jnp.int32, (slots, slots), 1).astype(jnp.float32)
    mine = lax.broadcasted_iota(jnp.int32, (slots, slots), 0).astype(jnp.float32)
    spare = float(comp_tiles * targ_group)
    same = down == across

    def count(mask, axis):
        return jnp.sum(jnp.where(mask, 1.0, 0.0), axis=axis, keepdims=True)

    earlier = count(same & (mine < at), 0)
    groups = jnp.floor((count(same, 0) + (GROUP - 1.0)) * (1.0 / GROUP))
    opens = (earlier == 0.0) & (across[:1] < spare)
    before = across < down
    rank = jnp.sum(jnp.where(before & opens, 1.0, 0.0), axis=1, keepdims=True)
    first = jnp.sum(jnp.where(before & opens, groups, 0.0), axis=1, keepdims=True)
    pair = down[:, :1]
    earlier = count(same & (at < mine), 1)
    alive = pair < spare
    opens = (earlier == 0.0) & alive
    step = jnp.floor(earlier * (1.0 / GROUP))
    place = jnp.where(alive, first + step, -1.0)
    member = earlier - GROUP * step
    groups = jnp.floor((count(same, 1) + (GROUP - 1.0)) * (1.0 / GROUP))

    def pick(mask, value, rest):
        return jnp.sum(jnp.where(mask, value - rest, 0.0), axis=0, keepdims=True) + rest

    here = place == at
    comp_tile = jnp.floor((pair + 0.5) * (1.0 / targ_group))
    rows = [pick(here & (member == n), mine[:, :1], float(slots)) for n in range(GROUP)]
    rows.append(pick(here & (member == 0.0), rank, float(pairs)))
    here = (rank == at) & opens
    rows.append(pick(here, comp_tile, float(comp_tiles)))
    rows.append(pick(here, pair - targ_group * comp_tile, float(targ_tiles)))
    totals = [jnp.sum(jnp.where(opens, n, 0.0), axis=0, keepdims=True) for n in (groups, 1.0)]
    rows.append(jnp.where(at[:1] == 0.0, totals[0], totals[1]))
    lists_ref[...] = jnp.concatenate(rows, axis=0).astype(jnp.int32)

    for index in range(chunks):

        @pl.when(index * chunk < live_ref[0])
        def _():
            for copy in copies(index):
                copy.wait()


def force_kernel(cols, rows, lists_ref, *refs):
    comp_firsts, comp_seconds, refs = refs[0], refs[1], refs[2:]
    targ_blocks, refs = refs[:rows], refs[rows:]
    values_ref, weight_ref, refs = refs[0], refs[1], refs[2:]
    comp_keep, comp_send, refs = refs[0], refs[1], refs[2:]
    targ_outs, refs = refs[:rows], refs[rows:]
    pred, total, comp_tiles, comp_flip, targ_tiles, targ_flip, comp_acc, targ_acc = refs
    side = values_ref.shape[1]
    comp_rows, targ_rows = comp_firsts.shape[1], targ_blocks[0].shape[0]
    comp_per, targ_per = comp_rows // side, targ_rows // side

    def fill(spot, tile, tiles, flip, acc):
        tiles[spot] = tile
        flip[spot] = tile.T
        acc[spot] = jnp.zeros(acc.shape[1:], acc.dtype)

    for n in range(rows):
        for i in range(targ_per):
            tile = targ_blocks[n][i * side : (i + 1) * side]
            fill(n * targ_per + i, tile, targ_tiles, targ_flip, targ_acc)
    for n in range(cols):
        for i in range(comp_per):
            tile = (comp_seconds if n % 2 else comp_firsts)[n // 2, i * side : (i + 1) * side]
            fill(n * comp_per + i, tile, comp_tiles, comp_flip, comp_acc)

    def steps(count):
        return lax.div(count + (UNROLL - 1), UNROLL)

    def pair_at(step):
        spots = [step * UNROLL + n for n in range(UNROLL)]
        return [(spot, lists_ref[GROUP + 1, spot], lists_ref[GROUP + 2, spot]) for spot in spots]

    last = pred.shape[0] - 1
    pairs, groups = lists_ref[GROUP + 3, 1], lists_ref[GROUP + 3, 0]

    def predict(step, unused):
        blocks = [
            (spot, jnp.dot(comp_tiles[i], targ_flip[j], preferred_element_type=jnp.float32))
            for spot, i, j in pair_at(step)
        ]
        for spot, block in blocks:
            spot = jnp.minimum(spot, last)
            pred[spot] = block.astype(pred.dtype)
            total[spot] = jnp.zeros(total.shape[1:], total.dtype)
        return unused

    lax.fori_loop(0, steps(pairs), predict, 0)

    one = degrees_free * noise_scale * noise_scale

    def weigh(step, unused):
        for n in range(UNROLL):
            group = step * UNROLL + n
            spot = lists_ref[GROUP, group]
            guess = pred[spot].astype(jnp.float32)
            whole = None
            for m in range(GROUP):
                slot = lists_ref[m, group]
                resid = values_ref[slot].astype(jnp.float32) - guess
                inverse = pl.reciprocal(one + resid * resid, approx=True)
                scaled = resid * weight_ref[slot].astype(jnp.float32) * inverse
                whole = scaled if whole is None else whole + scaled
            total[spot] += whole
        return unused

    lax.fori_loop(0, steps(groups), weigh, 0)

    def gather(step, unused):
        parts = []
        for spot, i, j in pair_at(step):
            weights = total[jnp.minimum(spot, last)].astype(jnp.bfloat16)
            comp_part = jnp.dot(weights, targ_tiles[j], preferred_element_type=jnp.float32)
            targ_part = jnp.dot(comp_flip[i], weights, preferred_element_type=jnp.float32)
            parts.append((i, comp_part, j, targ_part))
        for i, comp_part, j, targ_part in parts:
            comp_acc[i] += comp_part
            targ_acc[j] += targ_part
        return unused

    lax.fori_loop(0, steps(pairs), gather, 0)

    gain = degrees_free + 1.0
    for n in range(cols):
        out = comp_send if n % 2 else comp_keep
        for i in range(comp_per):
            part = comp_acc[n * comp_per + i] * gain
            out[n // 2, i * side : (i + 1) * side] = part.astype(out.dtype)
    for n in range(rows):
        out = targ_outs[n]
        for i in range(targ_per):
            part = targ_acc[n * targ_per + i] * gain
            out[i * side : (i + 1) * side] = part.T.astype(out.dtype)


smem = pl.BlockSpec(memory_space=pltpu.SMEM)
vmem = pl.BlockSpec(memory_space=pltpu.VMEM)
hbm = pl.BlockSpec(memory_space=pltpu.HBM)


def load_tiles(pairs, live, targ_group, shape, values, weight):
    slots, side, width = values.shape
    chunks = slots // math.gcd(slots, 16)
    held = pltpu.VMEM((slots + 1, side, width), values.dtype)
    values, weight = (pltpu.with_memory_space_constraint(x, pltpu.HBM) for x in (values, weight))
    return pl.pallas_call(
        functools.partial(load_kernel, targ_group, shape),
        out_shape=[held, held, jax.ShapeDtypeStruct((GROUP + 4, slots), jnp.int32)],
        in_specs=[vmem, smem, hbm, hbm],
        out_specs=[vmem] * 3,
        scratch_shapes=[pltpu.SemaphoreType.DMA((2, chunks))],
        compiler_params=pltpu.CompilerParams(vmem_limit_bytes=24 * 2**20),
        name="tile_load",
    )(pairs, live, values, weight)


def local_grads(lists, comp_firsts, comp_seconds, targ_blocks, values, weight, pairs):
    cols, rows = 2 * comp_firsts.shape[0], len(targ_blocks)
    comp_rows, rank = comp_firsts.shape[1:]
    targ_rows = targ_blocks[0].shape[0]
    side = values.shape[1]
    comp_tiles, targ_tiles = cols * comp_rows // side, rows * targ_rows // side
    comp_shape = jax.ShapeDtypeStruct((cols // 2, comp_rows, rank), jnp.bfloat16)
    targ_shape = jax.ShapeDtypeStruct((targ_rows, rank), jnp.bfloat16)
    held = (pairs + 1) * side * side * 6 + (comp_tiles + targ_tiles + 2) * side * rank * 8
    held += 4 * values.size
    outs = pl.pallas_call(
        functools.partial(force_kernel, cols, rows),
        out_shape=[comp_shape] * 2 + [targ_shape] * rows,
        in_specs=[smem] + [vmem] * (rows + 4),
        out_specs=[vmem] * (2 + rows),
        scratch_shapes=[
            pltpu.VMEM((pairs + 1, side, side), jnp.bfloat16),
            pltpu.VMEM((pairs + 1, side, side), jnp.float32),
            pltpu.VMEM((comp_tiles + 1, side, rank), jnp.bfloat16),
            pltpu.VMEM((comp_tiles + 1, rank, side), jnp.bfloat16),
            pltpu.VMEM((targ_tiles + 1, side, rank), jnp.bfloat16),
            pltpu.VMEM((targ_tiles + 1, rank, side), jnp.bfloat16),
            pltpu.VMEM((comp_tiles + 1, side, rank), jnp.float32),
            pltpu.VMEM((targ_tiles + 1, rank, side), jnp.float32),
        ],
        compiler_params=pltpu.CompilerParams(vmem_limit_bytes=held + 4 * 2**20),
        name="tile_force",
    )(lists, comp_firsts, comp_seconds, *targ_blocks, values, weight)
    return outs[0], outs[1], outs[2:]


def swap(block, axis, offset):
    size = lax.axis_size(axis)
    return lax.ppermute(block, axis, [(i, i ^ offset) for i in range(size)])


def spread(block, axis):
    size = lax.axis_size(axis)
    seconds = [block] + [swap(block, axis, offset) for offset in range(2, size, 2)]
    return [each for second in seconds for each in (second, swap(second, axis, 1))]


def collect(blocks, axis):
    whole = blocks[0].astype(jnp.float32)
    for offset in range(2, len(blocks), 2):
        near = swap(blocks[offset + 1], axis, 1).astype(jnp.float32)
        far = (blocks[offset].astype(jnp.float32) + near).astype(blocks[offset].dtype)
        whole = whole + swap(far, axis, offset).astype(jnp.float32)
    return whole + swap(blocks[1], axis, 1).astype(jnp.float32)


def between_chips(blocks, axis):
    size = lax.axis_size(axis)
    groups = [list(range(first, size, 2)) for first in range(2)]
    return lax.all_to_all(blocks, axis, 0, 0, axis_index_groups=groups)


def spread_pairs(block, axis):
    copies = jnp.broadcast_to(block, (lax.axis_size(axis) // 2, *block.shape))
    firsts = between_chips(copies, axis)
    return firsts, swap(firsts, axis, 1)


def collect_pairs(keep, send, axis):
    both = keep.astype(jnp.float32) + swap(send, axis, 1).astype(jnp.float32)
    got = between_chips(both.astype(keep.dtype), axis)
    return jnp.sum(got.astype(jnp.float32), axis=0)


def body(
    compound_pos,
    compound_mom,
    target_pos,
    target_mom,
    tile_rows,
    tile_cols,
    tile_count,
    tile_values,
    tile_weight,
):
    side = tile_values.shape[2]
    comp_per = compound_pos.shape[0] // side
    targ_per = target_pos.shape[0] // side
    cols, rows = lax.axis_size("col"), lax.axis_size("row")
    col_index, row_index = lax.axis_index("col"), lax.axis_index("row")
    assert cols & (cols - 1) == 0 and rows & (rows - 1) == 0
    comp_local = tile_rows[0] - row_index * (cols * comp_per)
    comp_place = ((comp_local // comp_per) ^ (col_index & 1)) * comp_per + comp_local % comp_per
    holder = tile_cols[0] // targ_per // cols
    targ_place = (holder ^ row_index) * targ_per + tile_cols[0] % targ_per
    targ_group = rows * targ_per
    alive = jnp.arange(tile_values.shape[1], dtype=jnp.int32) < tile_count[0]
    spare = cols * comp_per * targ_group
    slots = jnp.where(alive, comp_place * targ_group + targ_place, spare)

    shape = (min(spare, slots.shape[0]), cols * comp_per, targ_group)
    values, weight, lists = load_tiles(
        slots[None], tile_count, targ_group, shape, tile_values[0], tile_weight[0]
    )

    def forces(comp, targ):
        comp_keep, comp_send, targ_parts = local_grads(
            lists,
            *spread_pairs(comp.astype(jnp.bfloat16), "col"),
            spread(targ.astype(jnp.bfloat16), "row"),
            values,
            weight,
            shape[0],
        )
        comp_sum = collect_pairs(comp_keep, comp_send, "col")
        targ_sum = collect(targ_parts, "row")
        return comp_sum - prior_weight * comp, targ_sum - prior_weight * targ

    places = (compound_pos, target_pos)
    speeds = (compound_mom, target_mom)
    push = forces(*places)
    for leap in range(LEAPS):
        scale = (0.5 if leap == 0 else 1.0) * step_size
        speeds = tuple(p + scale * f for p, f in zip(speeds, push))
        places = tuple(q + step_size * p for q, p in zip(places, speeds))
        push = forces(*places)
    speeds = tuple(p + 0.5 * step_size * f for p, f in zip(speeds, push))
    return (places[0], speeds[0], places[1], speeds[1])


def solution(mesh):
    split = P(("row", "col"), None)
    tiles = P(("row", "col"), None, None, None)
    return jax.shard_map(
        body,
        mesh=mesh,
        in_specs=(split,) * 6 + (P(("row", "col")), tiles, tiles),
        out_specs=(split,) * 4,
        check_vma=False,
    )
```

```python
import functools
import math

import jax
import jax.numpy as jnp
from jax import lax
from jax.experimental import pallas as pl
from jax.experimental.pallas import tpu as pltpu
from jax.sharding import PartitionSpec as P

LEAPS = 2
GROUP = 4
UNROLL = 4
PAIRS = 8


degrees_free = 4.0
noise_scale = 0.5
prior_weight = 1.0
step_size = 0.01


def load_kernel(targ_group, shape, pair_ref, live_ref, values_hbm, weight_hbm, *refs):
    values_out, weight_out, lists_ref, sems = refs
    pairs, comp_tiles, targ_tiles = shape
    slots = values_hbm.shape[0]
    chunks = sems.shape[1]
    chunk = slots // chunks

    def copies(index):
        part = pl.ds(index * chunk, chunk)
        return (
            pltpu.make_async_copy(values_hbm.at[part], values_out.at[part], sems.at[0, index]),
            pltpu.make_async_copy(weight_hbm.at[part], weight_out.at[part], sems.at[1, index]),
        )

    for index in range(chunks):

        @pl.when(index * chunk < live_ref[0])
        def _():
            for copy in copies(index):
                copy.start()

    values_out[slots] = jnp.zeros_like(values_out[slots])
    weight_out[slots] = jnp.zeros_like(weight_out[slots])

    across = jnp.broadcast_to(pair_ref[...].astype(jnp.float32), (slots, slots))
    down = across.T
    at = lax.broadcasted_iota(jnp.int32, (slots, slots), 1).astype(jnp.float32)
    mine = lax.broadcasted_iota(jnp.int32, (slots, slots), 0).astype(jnp.float32)
    spare = float(comp_tiles * targ_group)
    same = down == across

    def count(mask, axis):
        return jnp.sum(jnp.where(mask, 1.0, 0.0), axis=axis, keepdims=True)

    earlier = count(same & (mine < at), 0)
    groups = jnp.floor((count(same, 0) + (GROUP - 1.0)) * (1.0 / GROUP))
    opens = (earlier == 0.0) & (across[:1] < spare)
    before = across < down
    rank = jnp.sum(jnp.where(before & opens, 1.0, 0.0), axis=1, keepdims=True)
    first = jnp.sum(jnp.where(before & opens, groups, 0.0), axis=1, keepdims=True)
    pair = down[:, :1]
    earlier = count(same & (at < mine), 1)
    alive = pair < spare
    opens = (earlier == 0.0) & alive
    step = jnp.floor(earlier * (1.0 / GROUP))
    place = jnp.where(alive, first + step, -1.0)
    member = earlier - GROUP * step
    groups = jnp.floor((count(same, 1) + (GROUP - 1.0)) * (1.0 / GROUP))

    def pick(mask, value, rest):
        return jnp.sum(jnp.where(mask, value - rest, 0.0), axis=0, keepdims=True) + rest

    here = place == at
    comp_tile = jnp.floor((pair + 0.5) * (1.0 / targ_group))
    rows = [pick(here & (member == n), mine[:, :1], float(slots)) for n in range(GROUP)]
    rows.append(pick(here & (member == 0.0), rank, float(pairs)))
    here = (rank == at) & opens
    rows.append(pick(here, comp_tile, float(comp_tiles)))
    rows.append(pick(here, pair - targ_group * comp_tile, float(targ_tiles)))
    totals = [jnp.sum(jnp.where(opens, n, 0.0), axis=0, keepdims=True) for n in (groups, 1.0)]
    rows.append(jnp.where(at[:1] == 0.0, totals[0], totals[1]))
    lists_ref[...] = jnp.concatenate(rows, axis=0).astype(jnp.int32)

    for index in range(chunks):

        @pl.when(index * chunk < live_ref[0])
        def _():
            for copy in copies(index):
                copy.wait()


def force_kernel(cols, rows, lists_ref, *refs):
    comp_firsts, refs = refs[: cols // 2], refs[cols // 2 :]
    comp_seconds, refs = refs[: cols // 2], refs[cols // 2 :]
    targ_blocks, refs = refs[:rows], refs[rows:]
    values_ref, weight_ref, refs = refs[0], refs[1], refs[2:]
    comp_keep, comp_send, refs = refs[0], refs[1], refs[2:]
    targ_outs, refs = refs[:rows], refs[rows:]
    pred, total, comp_tiles, comp_flip, targ_tiles, targ_flip, comp_acc, targ_acc = refs
    side = values_ref.shape[1]
    comp_rows, targ_rows = comp_firsts[0].shape[0], targ_blocks[0].shape[0]
    comp_per, targ_per = comp_rows // side, targ_rows // side

    def fill(spot, tile, tiles, flip, acc):
        tiles[spot] = tile
        flip[spot] = tile.T
        acc[spot] = jnp.zeros(acc.shape[1:], acc.dtype)

    for n in range(rows):
        for i in range(targ_per):
            tile = targ_blocks[n][i * side : (i + 1) * side]
            fill(n * targ_per + i, tile, targ_tiles, targ_flip, targ_acc)
    for n in range(cols):
        for i in range(comp_per):
            tile = (comp_seconds if n % 2 else comp_firsts)[n // 2][i * side : (i + 1) * side]
            fill(n * comp_per + i, tile, comp_tiles, comp_flip, comp_acc)

    def steps(count, unroll):
        return lax.div(count + (unroll - 1), unroll)

    def pair_at(step):
        spots = [step * PAIRS + n for n in range(PAIRS)]
        return [(spot, lists_ref[GROUP + 1, spot], lists_ref[GROUP + 2, spot]) for spot in spots]

    last = pred.shape[0] - 1
    pairs, groups = lists_ref[GROUP + 3, 1], lists_ref[GROUP + 3, 0]

    def predict(step, unused):
        blocks = [
            (spot, jnp.dot(comp_tiles[i], targ_flip[j], preferred_element_type=jnp.float32))
            for spot, i, j in pair_at(step)
        ]
        for spot, block in blocks:
            spot = jnp.minimum(spot, last)
            pred[spot] = block.astype(pred.dtype)
            total[spot] = jnp.zeros(total.shape[1:], total.dtype)
        return unused

    lax.fori_loop(0, steps(pairs, PAIRS), predict, 0)

    one = degrees_free * noise_scale * noise_scale
    assert one == 1.0

    def weigh(step, unused):
        for n in range(UNROLL):
            group = step * UNROLL + n
            spot = lists_ref[GROUP, group]
            guess = pred[spot].astype(jnp.float32)
            whole = None
            for m in range(GROUP):
                slot = lists_ref[m, group]
                resid = values_ref[slot].astype(jnp.float32) - guess
                scaled = weight_ref[slot].astype(jnp.float32)
                if m % 2:
                    scaled *= pl.reciprocal(resid + pl.reciprocal(resid, approx=True), approx=True)
                else:
                    scaled *= resid * pl.reciprocal(one + resid * resid, approx=True)
                whole = scaled if whole is None else whole + scaled
            total[spot] += whole
        return unused

    lax.fori_loop(0, steps(groups, UNROLL), weigh, 0)

    def gather(step, unused):
        parts = []
        for spot, i, j in pair_at(step):
            weights = total[jnp.minimum(spot, last)].astype(jnp.bfloat16)
            comp_part = jnp.dot(weights, targ_tiles[j], preferred_element_type=jnp.float32)
            targ_part = jnp.dot(comp_flip[i], weights, preferred_element_type=jnp.float32)
            parts.append((i, comp_part, j, targ_part))
        for i, comp_part, j, targ_part in parts:
            comp_acc[i] += comp_part
            targ_acc[j] += targ_part
        return unused

    lax.fori_loop(0, steps(pairs, PAIRS), gather, 0)

    gain = degrees_free + 1.0
    for n in range(cols):
        out = comp_send if n % 2 else comp_keep
        for i in range(comp_per):
            part = comp_acc[n * comp_per + i] * gain
            out[n // 2, i * side : (i + 1) * side] = part.astype(out.dtype)
    for n in range(rows):
        out = targ_outs[n]
        for i in range(targ_per):
            part = targ_acc[n * targ_per + i] * gain
            out[i * side : (i + 1) * side] = part.T.astype(out.dtype)


smem = pl.BlockSpec(memory_space=pltpu.SMEM)
vmem = pl.BlockSpec(memory_space=pltpu.VMEM)
hbm = pl.BlockSpec(memory_space=pltpu.HBM)


def load_tiles(pairs, live, targ_group, shape, values, weight):
    slots, side, width = values.shape
    chunks = slots // math.gcd(slots, 16)
    held = pltpu.VMEM((slots + 1, side, width), values.dtype)
    values, weight = (pltpu.with_memory_space_constraint(x, pltpu.HBM) for x in (values, weight))
    return pl.pallas_call(
        functools.partial(load_kernel, targ_group, shape),
        out_shape=[held, held, jax.ShapeDtypeStruct((GROUP + 4, slots), jnp.int32)],
        in_specs=[vmem, smem, hbm, hbm],
        out_specs=[vmem] * 3,
        scratch_shapes=[pltpu.SemaphoreType.DMA((2, chunks))],
        compiler_params=pltpu.CompilerParams(vmem_limit_bytes=24 * 2**20),
        name="tile_load",
    )(pairs, live, values, weight)


def local_grads(lists, comp_firsts, comp_seconds, targ_blocks, values, weight, pairs):
    cols, rows = 2 * len(comp_firsts), len(targ_blocks)
    comp_rows, rank = comp_firsts[0].shape
    targ_rows = targ_blocks[0].shape[0]
    side = values.shape[1]
    comp_tiles, targ_tiles = cols * comp_rows // side, rows * targ_rows // side
    comp_shape = jax.ShapeDtypeStruct((cols // 2, comp_rows, rank), jnp.bfloat16)
    targ_shape = jax.ShapeDtypeStruct((targ_rows, rank), jnp.bfloat16)
    held = (pairs + 1) * side * side * 6 + (comp_tiles + targ_tiles + 2) * side * rank * 8
    held += 4 * values.size
    outs = pl.pallas_call(
        functools.partial(force_kernel, cols, rows),
        out_shape=[comp_shape] * 2 + [targ_shape] * rows,
        in_specs=[smem] + [vmem] * (cols + rows + 2),
        out_specs=[vmem] * (2 + rows),
        scratch_shapes=[
            pltpu.VMEM((pairs + 1, side, side), jnp.bfloat16),
            pltpu.VMEM((pairs + 1, side, side), jnp.float32),
            pltpu.VMEM((comp_tiles + 1, side, rank), jnp.bfloat16),
            pltpu.VMEM((comp_tiles + 1, rank, side), jnp.bfloat16),
            pltpu.VMEM((targ_tiles + 1, side, rank), jnp.bfloat16),
            pltpu.VMEM((targ_tiles + 1, rank, side), jnp.bfloat16),
            pltpu.VMEM((comp_tiles + 1, side, rank), jnp.float32),
            pltpu.VMEM((targ_tiles + 1, rank, side), jnp.float32),
        ],
        compiler_params=pltpu.CompilerParams(vmem_limit_bytes=held + 4 * 2**20),
        name="tile_force",
    )(lists, *comp_firsts, *comp_seconds, *targ_blocks, values, weight)
    return outs[0], outs[1], outs[2:]


def swap(block, axis, offset):
    size = lax.axis_size(axis)
    return lax.ppermute(block, axis, [(i, i ^ offset) for i in range(size)])


def spread(block, axis):
    size = lax.axis_size(axis)
    seconds = [block] + [swap(block, axis, offset) for offset in range(2, size, 2)]
    return [each for second in seconds for each in (second, swap(second, axis, 1))]


def collect(blocks, axis):
    whole = blocks[0].astype(jnp.float32)
    for offset in range(2, len(blocks), 2):
        near = swap(blocks[offset + 1], axis, 1).astype(jnp.float32)
        far = (blocks[offset].astype(jnp.float32) + near).astype(blocks[offset].dtype)
        whole = whole + swap(far, axis, offset).astype(jnp.float32)
    return whole + swap(blocks[1], axis, 1).astype(jnp.float32)


def spread_pairs(block, axis):
    firsts = [block]
    firsts += [swap(block, axis, offset) for offset in range(2, lax.axis_size(axis), 2)]
    return firsts, [swap(block, axis, 1) for block in firsts]


def collect_pairs(keep, send, axis):
    got = swap(send, axis, 1)
    both = [
        keep[n].astype(jnp.float32) + got[n].astype(jnp.float32) for n in range(keep.shape[0])
    ]
    whole = both[0]
    for n, block in enumerate(both[1:]):
        whole = whole + swap(block.astype(keep.dtype), axis, 2 * n + 2).astype(jnp.float32)
    return whole


def body(
    compound_pos,
    compound_mom,
    target_pos,
    target_mom,
    tile_rows,
    tile_cols,
    tile_count,
    tile_values,
    tile_weight,
):
    side = tile_values.shape[2]
    comp_per = compound_pos.shape[0] // side
    targ_per = target_pos.shape[0] // side
    cols, rows = lax.axis_size("col"), lax.axis_size("row")
    col_index, row_index = lax.axis_index("col"), lax.axis_index("row")
    assert cols & (cols - 1) == 0 and rows & (rows - 1) == 0
    comp_local = tile_rows[0] - row_index * (cols * comp_per)
    comp_place = ((comp_local // comp_per) ^ col_index) * comp_per + comp_local % comp_per
    holder = tile_cols[0] // targ_per // cols
    targ_place = (holder ^ row_index) * targ_per + tile_cols[0] % targ_per
    targ_group = rows * targ_per
    alive = jnp.arange(tile_values.shape[1], dtype=jnp.int32) < tile_count[0]
    spare = cols * comp_per * targ_group
    slots = jnp.where(alive, comp_place * targ_group + targ_place, spare)

    shape = (min(spare, slots.shape[0]), cols * comp_per, targ_group)
    values, weight, lists = load_tiles(
        slots[None], tile_count, targ_group, shape, tile_values[0], tile_weight[0]
    )

    def forces(comp, targ):
        comp_keep, comp_send, targ_parts = local_grads(
            lists,
            *spread_pairs(comp.astype(jnp.bfloat16), "col"),
            spread(targ.astype(jnp.bfloat16), "row"),
            values,
            weight,
            shape[0],
        )
        comp_sum = collect_pairs(comp_keep, comp_send, "col")
        targ_sum = collect(targ_parts, "row")
        return comp_sum - prior_weight * comp, targ_sum - prior_weight * targ

    places = (compound_pos, target_pos)
    speeds = (compound_mom, target_mom)
    push = forces(*places)
    for leap in range(LEAPS):
        scale = (0.5 if leap == 0 else 1.0) * step_size
        speeds = tuple(p + scale * f for p, f in zip(speeds, push))
        places = tuple(q + step_size * p for q, p in zip(places, speeds))
        push = forces(*places)
    speeds = tuple(p + 0.5 * step_size * f for p, f in zip(speeds, push))
    return (places[0], speeds[0], places[1], speeds[1])


def solution(mesh):
    split = P(("row", "col"), None)
    tiles = P(("row", "col"), None, None, None)
    return jax.shard_map(
        body,
        mesh=mesh,
        in_specs=(split,) * 6 + (P(("row", "col")), tiles, tiles),
        out_specs=(split,) * 4,
        check_vma=False,
    )
```

```python
import functools
import math

import jax
import jax.numpy as jnp
from jax import lax
from jax.experimental import pallas as pl
from jax.experimental.pallas import tpu as pltpu
from jax.sharding import PartitionSpec as P

LEAPS = 2
GROUP = 4
UNROLL = 4
PAIRS = 8


degrees_free = 4.0
noise_scale = 0.5
prior_weight = 1.0
step_size = 0.01


def tile_copies(values_hbm, weight_hbm, values_ref, weight_ref, sems):
    chunks = sems.shape[1]
    chunk = values_hbm.shape[0] // chunks
    for index in range(chunks):
        part = pl.ds(index * chunk, chunk)
        yield index * chunk, [
            pltpu.make_async_copy(values_hbm.at[part], values_ref.at[part], sems.at[0, index]),
            pltpu.make_async_copy(weight_hbm.at[part], weight_ref.at[part], sems.at[1, index]),
        ]


def list_slots(pair, comp_tiles, targ_tiles, pairs):
    slots = pair.shape[1]
    across = jnp.broadcast_to(pair.astype(jnp.float32), (slots, slots))
    down = across.T
    at = lax.broadcasted_iota(jnp.int32, (slots, slots), 1).astype(jnp.float32)
    mine = lax.broadcasted_iota(jnp.int32, (slots, slots), 0).astype(jnp.float32)
    spare = float(comp_tiles * targ_tiles)
    same = down == across

    def count(mask, axis):
        return jnp.sum(jnp.where(mask, 1.0, 0.0), axis=axis, keepdims=True)

    earlier = count(same & (mine < at), 0)
    groups = jnp.floor((count(same, 0) + (GROUP - 1.0)) * (1.0 / GROUP))
    opens = (earlier == 0.0) & (across[:1] < spare)
    before = across < down
    rank = jnp.sum(jnp.where(before & opens, 1.0, 0.0), axis=1, keepdims=True)
    first = jnp.sum(jnp.where(before & opens, groups, 0.0), axis=1, keepdims=True)
    pair = down[:, :1]
    earlier = count(same & (at < mine), 1)
    alive = pair < spare
    opens = (earlier == 0.0) & alive
    step = jnp.floor(earlier * (1.0 / GROUP))
    place = jnp.where(alive, first + step, -1.0)
    member = earlier - GROUP * step
    groups = jnp.floor((count(same, 1) + (GROUP - 1.0)) * (1.0 / GROUP))

    def pick(mask, value, rest):
        return jnp.sum(jnp.where(mask, value - rest, 0.0), axis=0, keepdims=True) + rest

    here = place == at
    comp_tile = jnp.floor((pair + 0.5) * (1.0 / targ_tiles))
    rows = [pick(here & (member == n), mine[:, :1], float(slots)) for n in range(GROUP)]
    rows.append(pick(here & (member == 0.0), rank, float(pairs)))
    here = (rank == at) & opens
    rows.append(pick(here, comp_tile, float(comp_tiles)))
    rows.append(pick(here, pair - targ_tiles * comp_tile, float(targ_tiles)))
    totals = [jnp.sum(jnp.where(opens, n, 0.0), axis=0, keepdims=True) for n in (groups, 1.0)]
    rows.append(jnp.where(at[:1] == 0.0, totals[0], totals[1]))
    return jnp.concatenate(rows, axis=0).astype(jnp.int32)


def force_kernel(cols, rows, first, *refs):
    if first:
        live_ref, row_ref, col_ref, refs = *refs[:3], refs[3:]
    else:
        lists_ref, refs = refs[0], refs[1:]
    comp_firsts, refs = refs[: cols // 2], refs[cols // 2 :]
    comp_seconds, refs = refs[: cols // 2], refs[cols // 2 :]
    targ_blocks, refs = refs[:rows], refs[rows:]
    values_ref, weight_ref, refs = refs[0], refs[1], refs[2:]
    comp_keep, comp_send, refs = refs[0], refs[1], refs[2:]
    targ_outs, refs = refs[:rows], refs[rows:]
    if first:
        values_hbm, weight_hbm = values_ref, weight_ref
        values_ref, weight_ref, lists_out, refs = *refs[:3], refs[3:]
        lists_ref, list_sem, sems, refs = *refs[:3], refs[3:]
    pred, total, comp_tiles, comp_flip, targ_tiles, targ_flip, comp_acc, targ_acc = refs
    side = values_ref.shape[1]
    comp_rows, targ_rows = comp_firsts[0].shape[0], targ_blocks[0].shape[0]
    comp_per, targ_per = comp_rows // side, targ_rows // side

    if first:
        copies = tile_copies(values_hbm, weight_hbm, values_ref, weight_ref, sems)
        copies = list(copies)
        for start, both in copies:

            @pl.when(start < live_ref[0])
            def _():
                for copy in both:
                    copy.start()

        slots = values_hbm.shape[0]
        values_ref[slots] = jnp.zeros_like(values_ref[slots])
        weight_ref[slots] = jnp.zeros_like(weight_ref[slots])
        row_index, col_index = lax.axis_index("row"), lax.axis_index("col")
        local = row_ref[...] - row_index * (cols * comp_per)
        comp_place = (lax.div(local, comp_per) ^ col_index) * comp_per + lax.rem(local, comp_per)
        holder = lax.div(col_ref[...], targ_per * cols)
        targ_place = (holder ^ row_index) * targ_per + lax.rem(col_ref[...], targ_per)
        alive = lax.broadcasted_iota(jnp.int32, (1, slots), 1) < live_ref[0]
        spare = cols * comp_per * rows * targ_per
        pair = jnp.where(alive, comp_place * (rows * targ_per) + targ_place, spare)
        lists_out[...] = list_slots(pair, cols * comp_per, rows * targ_per, pred.shape[0] - 1)
        to_scalars = pltpu.make_async_copy(lists_out, lists_ref, list_sem)
        to_scalars.start()

    def fill(spot, tile, tiles, flip, acc):
        tiles[spot] = tile
        flip[spot] = tile.T
        acc[spot] = jnp.zeros(acc.shape[1:], acc.dtype)

    for n in range(rows):
        for i in range(targ_per):
            tile = targ_blocks[n][i * side : (i + 1) * side]
            fill(n * targ_per + i, tile, targ_tiles, targ_flip, targ_acc)
    for n in range(cols):
        for i in range(comp_per):
            tile = (comp_seconds if n % 2 else comp_firsts)[n // 2][i * side : (i + 1) * side]
            fill(n * comp_per + i, tile, comp_tiles, comp_flip, comp_acc)

    if first:
        to_scalars.wait()

    def steps(count, unroll):
        return lax.div(count + (unroll - 1), unroll)

    def pair_at(step):
        spots = [step * PAIRS + n for n in range(PAIRS)]
        return [(spot, lists_ref[GROUP + 1, spot], lists_ref[GROUP + 2, spot]) for spot in spots]

    last = pred.shape[0] - 1
    pairs, groups = lists_ref[GROUP + 3, 1], lists_ref[GROUP + 3, 0]

    def predict(step, unused):
        blocks = [
            (spot, jnp.dot(comp_tiles[i], targ_flip[j], preferred_element_type=jnp.float32))
            for spot, i, j in pair_at(step)
        ]
        for spot, block in blocks:
            spot = jnp.minimum(spot, last)
            pred[spot] = block.astype(pred.dtype)
            total[spot] = jnp.zeros(total.shape[1:], total.dtype)
        return unused

    lax.fori_loop(0, steps(pairs, PAIRS), predict, 0)

    if first:
        for start, both in copies:

            @pl.when(start < live_ref[0])
            def _():
                for copy in both:
                    copy.wait()

    one = degrees_free * noise_scale * noise_scale
    assert one == 1.0

    def weigh(step, unused):
        for n in range(UNROLL):
            group = step * UNROLL + n
            spot = lists_ref[GROUP, group]
            guess = pred[spot].astype(jnp.float32)
            whole = None
            for m in range(GROUP):
                slot = lists_ref[m, group]
                resid = values_ref[slot].astype(jnp.float32) - guess
                scaled = weight_ref[slot].astype(jnp.float32)
                if m % 2:
                    scaled *= pl.reciprocal(resid + pl.reciprocal(resid, approx=True), approx=True)
                else:
                    scaled *= resid * pl.reciprocal(one + resid * resid, approx=True)
                whole = scaled if whole is None else whole + scaled
            total[spot] += whole
        return unused

    lax.fori_loop(0, steps(groups, UNROLL), weigh, 0)

    def gather(step, unused):
        parts = []
        for spot, i, j in pair_at(step):
            weights = total[jnp.minimum(spot, last)].astype(jnp.bfloat16)
            comp_part = jnp.dot(weights, targ_tiles[j], preferred_element_type=jnp.float32)
            targ_part = jnp.dot(comp_flip[i], weights, preferred_element_type=jnp.float32)
            parts.append((i, comp_part, j, targ_part))
        for i, comp_part, j, targ_part in parts:
            comp_acc[i] += comp_part
            targ_acc[j] += targ_part
        return unused

    lax.fori_loop(0, steps(pairs, PAIRS), gather, 0)

    gain = degrees_free + 1.0
    for n in range(cols):
        out = comp_send if n % 2 else comp_keep
        for i in range(comp_per):
            part = comp_acc[n * comp_per + i] * gain
            out[n // 2, i * side : (i + 1) * side] = part.astype(out.dtype)
    for n in range(rows):
        out = targ_outs[n]
        for i in range(targ_per):
            part = targ_acc[n * targ_per + i] * gain
            out[i * side : (i + 1) * side] = part.T.astype(out.dtype)


smem = pl.BlockSpec(memory_space=pltpu.SMEM)
vmem = pl.BlockSpec(memory_space=pltpu.VMEM)
hbm = pl.BlockSpec(memory_space=pltpu.HBM)


def local_grads(slots_at, comp_firsts, comp_seconds, targ_blocks, values, weight):
    first = len(slots_at) > 1
    cols, rows = 2 * len(comp_firsts), len(targ_blocks)
    comp_rows, rank = comp_firsts[0].shape
    targ_rows = targ_blocks[0].shape[0]
    side = values.shape[1]
    comp_tiles, targ_tiles = cols * comp_rows // side, rows * targ_rows // side
    slots = values.shape[0] if first else values.shape[0] - 1
    pairs = min(comp_tiles * targ_tiles, slots)
    held = (pairs + 1) * side * side * 6 + (comp_tiles + targ_tiles + 2) * side * rank * 8
    held += 4 * 2**20 if first else 4 * values.size
    comp_shape = jax.ShapeDtypeStruct((cols // 2, comp_rows, rank), jnp.bfloat16)
    targ_shape = jax.ShapeDtypeStruct((targ_rows, rank), jnp.bfloat16)
    outs = [comp_shape] * 2 + [targ_shape] * rows
    scratch = []
    ins = [smem, vmem, vmem] if first else [smem]
    if first:
        lists = (GROUP + 4, slots)
        outs += [pltpu.VMEM((slots + 1, side, side), x.dtype) for x in (values, weight)]
        outs += [jax.ShapeDtypeStruct(lists, jnp.int32)]
        scratch = [pltpu.SMEM(lists, jnp.int32), pltpu.SemaphoreType.DMA]
        scratch += [pltpu.SemaphoreType.DMA((2, slots // math.gcd(slots, 16)))]
        values, weight = (pltpu.with_memory_space_constraint(x, pltpu.HBM) for x in (values, weight))
    ins += [vmem] * (cols + rows) + [hbm if first else vmem] * 2
    outs = pl.pallas_call(
        functools.partial(force_kernel, cols, rows, first),
        out_shape=outs,
        in_specs=ins,
        out_specs=[vmem] * len(outs),
        scratch_shapes=[
            *scratch,
            pltpu.VMEM((pairs + 1, side, side), jnp.bfloat16),
            pltpu.VMEM((pairs + 1, side, side), jnp.float32),
            pltpu.VMEM((comp_tiles + 1, side, rank), jnp.bfloat16),
            pltpu.VMEM((comp_tiles + 1, rank, side), jnp.bfloat16),
            pltpu.VMEM((targ_tiles + 1, side, rank), jnp.bfloat16),
            pltpu.VMEM((targ_tiles + 1, rank, side), jnp.bfloat16),
            pltpu.VMEM((comp_tiles + 1, side, rank), jnp.float32),
            pltpu.VMEM((targ_tiles + 1, rank, side), jnp.float32),
        ],
        compiler_params=pltpu.CompilerParams(vmem_limit_bytes=held + 4 * 2**20),
        name="tile_force",
    )(*slots_at, *comp_firsts, *comp_seconds, *targ_blocks, values, weight)
    return outs[0], outs[1], outs[2 : 2 + rows], outs[2 + rows :]


def swap(block, axis, offset):
    size = lax.axis_size(axis)
    return lax.ppermute(block, axis, [(i, i ^ offset) for i in range(size)])


def spread(block, axis):
    size = lax.axis_size(axis)
    seconds = [block] + [swap(block, axis, offset) for offset in range(2, size, 2)]
    return [each for second in seconds for each in (second, swap(second, axis, 1))]


def collect(blocks, axis):
    whole = blocks[0].astype(jnp.float32)
    for offset in range(2, len(blocks), 2):
        near = swap(blocks[offset + 1], axis, 1).astype(jnp.float32)
        far = (blocks[offset].astype(jnp.float32) + near).astype(blocks[offset].dtype)
        whole = whole + swap(far, axis, offset).astype(jnp.float32)
    return whole + swap(blocks[1], axis, 1).astype(jnp.float32)


def spread_pairs(block, axis):
    firsts = [block]
    firsts += [swap(block, axis, offset) for offset in range(2, lax.axis_size(axis), 2)]
    return firsts, [swap(block, axis, 1) for block in firsts]


def collect_pairs(keep, send, axis):
    got = swap(send, axis, 1)
    both = [
        keep[n].astype(jnp.float32) + got[n].astype(jnp.float32) for n in range(keep.shape[0])
    ]
    whole = both[0]
    for n, block in enumerate(both[1:]):
        whole = whole + swap(block.astype(keep.dtype), axis, 2 * n + 2).astype(jnp.float32)
    return whole


def body(
    compound_pos,
    compound_mom,
    target_pos,
    target_mom,
    tile_rows,
    tile_cols,
    tile_count,
    tile_values,
    tile_weight,
):
    cols, rows = lax.axis_size("col"), lax.axis_size("row")
    assert cols & (cols - 1) == 0 and rows & (rows - 1) == 0
    held = (tile_values[0], tile_weight[0], tile_count, tile_rows, tile_cols)

    def forces(comp, targ):
        nonlocal held
        comp_keep, comp_send, targ_parts, kept = local_grads(
            held[2:],
            *spread_pairs(comp.astype(jnp.bfloat16), "col"),
            spread(targ.astype(jnp.bfloat16), "row"),
            *held[:2],
        )
        held = kept or held
        comp_sum = collect_pairs(comp_keep, comp_send, "col")
        targ_sum = collect(targ_parts, "row")
        return comp_sum - prior_weight * comp, targ_sum - prior_weight * targ

    places = (compound_pos, target_pos)
    speeds = (compound_mom, target_mom)
    push = forces(*places)
    for leap in range(LEAPS):
        scale = (0.5 if leap == 0 else 1.0) * step_size
        speeds = tuple(p + scale * f for p, f in zip(speeds, push))
        places = tuple(q + step_size * p for q, p in zip(places, speeds))
        push = forces(*places)
    speeds = tuple(p + 0.5 * step_size * f for p, f in zip(speeds, push))
    return (places[0], speeds[0], places[1], speeds[1])


def solution(mesh):
    split = P(("row", "col"), None)
    tiles = P(("row", "col"), None, None, None)
    return jax.shard_map(
        body,
        mesh=mesh,
        in_specs=(split,) * 6 + (P(("row", "col")), tiles, tiles),
        out_specs=(split,) * 4,
        check_vma=False,
    )
```

```python
import functools
import math

import jax
import jax.numpy as jnp
from jax import lax
from jax.experimental import pallas as pl
from jax.experimental.pallas import tpu as pltpu
from jax.sharding import PartitionSpec as P

LEAPS = 2
GROUP = 4
UNROLL = 4
PAIRS = 8
PARTS = 2


degrees_free = 4.0
noise_scale = 0.5
prior_weight = 1.0
step_size = 0.01


def tile_copies(values_hbm, weight_hbm, values_ref, weight_ref, sems):
    chunks = sems.shape[1]
    chunk = values_hbm.shape[0] // chunks
    for index in range(chunks):
        part = pl.ds(index * chunk, chunk)
        yield index * chunk, [
            pltpu.make_async_copy(values_hbm.at[part], values_ref.at[part], sems.at[0, index]),
            pltpu.make_async_copy(weight_hbm.at[part], weight_ref.at[part], sems.at[1, index]),
        ]


def list_slots(pair, comp_tiles, targ_tiles, pairs, parts):
    slots = pair.shape[1]
    across = jnp.broadcast_to(pair.astype(jnp.float32), (slots, slots))
    down = across.T
    at = lax.broadcasted_iota(jnp.int32, (slots, slots), 1).astype(jnp.float32)
    mine = lax.broadcasted_iota(jnp.int32, (slots, slots), 0).astype(jnp.float32)
    spare = float(comp_tiles * targ_tiles)
    span = slots // parts
    part_across, part_down = jnp.floor(at * (1.0 / span)), jnp.floor(mine * (1.0 / span))
    key_across, key_down = (
        pair + part * (spare + 1.0)
        for pair, part in ((across, part_across), (down, part_down))
    )
    same = key_down == key_across

    def count(mask, axis):
        return jnp.sum(jnp.where(mask, 1.0, 0.0), axis=axis, keepdims=True)

    earlier = count(same & (mine < at), 0)
    groups = jnp.floor((count(same, 0) + (GROUP - 1.0)) * (1.0 / GROUP))
    opens = (earlier == 0.0) & (across[:1] < spare)
    leads = (count((down == across) & (mine < at), 0) == 0.0) & (across[:1] < spare)
    rank = count((across < down) & leads, 1)
    before = (key_across < key_down) & opens
    first = jnp.sum(jnp.where(before, groups, 0.0), axis=1, keepdims=True)
    pair = down[:, :1]
    earlier = count(same & (at < mine), 1)
    alive = pair < spare
    opens = (earlier == 0.0) & alive
    leads = (count((down == across) & (at < mine), 1) == 0.0) & alive
    step = jnp.floor(earlier * (1.0 / GROUP))
    place = jnp.where(alive, first + step, -1.0)
    member = earlier - GROUP * step
    groups = jnp.floor((count(same, 1) + (GROUP - 1.0)) * (1.0 / GROUP))

    def pick(mask, value, rest):
        return jnp.sum(jnp.where(mask, value - rest, 0.0), axis=0, keepdims=True) + rest

    here = place == at
    comp_tile = jnp.floor((pair + 0.5) * (1.0 / targ_tiles))
    rows = [pick(here & (member == n), mine[:, :1], float(slots)) for n in range(GROUP)]
    rows.append(pick(here & (member == 0.0), rank, float(pairs)))
    here = (rank == at) & leads
    rows.append(pick(here, comp_tile, float(comp_tiles)))
    rows.append(pick(here, pair - targ_tiles * comp_tile, float(targ_tiles)))
    early = jnp.where(part_down[:, :1] == 0.0, groups, 0.0)
    totals = [
        jnp.sum(jnp.where(mask, value, 0.0), axis=0, keepdims=True)
        for mask, value in ((opens, groups), (leads, 1.0), (opens, early))
    ]
    whole = jnp.where(at[:1] == 1.0, totals[1], totals[2])
    rows.append(jnp.where(at[:1] == 0.0, totals[0], whole))
    return jnp.concatenate(rows, axis=0).astype(jnp.int32)


def force_kernel(cols, rows, first, *refs):
    if first:
        live_ref, row_ref, col_ref, refs = *refs[:3], refs[3:]
    else:
        lists_ref, refs = refs[0], refs[1:]
    comp_firsts, refs = refs[: cols // 2], refs[cols // 2 :]
    comp_seconds, refs = refs[: cols // 2], refs[cols // 2 :]
    targ_blocks, refs = refs[:rows], refs[rows:]
    values_ref, weight_ref, refs = refs[0], refs[1], refs[2:]
    comp_keep, comp_send, refs = refs[0], refs[1], refs[2:]
    targ_outs, refs = refs[:rows], refs[rows:]
    if first:
        values_hbm, weight_hbm = values_ref, weight_ref
        values_ref, weight_ref, lists_out, refs = *refs[:3], refs[3:]
        lists_ref, lists_buf, place_buf, place_sems, sems, refs = *refs[:5], refs[5:]
    pred, total, comp_tiles, comp_flip, targ_tiles, targ_flip, comp_acc, targ_acc = refs
    side = values_ref.shape[1]
    comp_rows, targ_rows = comp_firsts[0].shape[0], targ_blocks[0].shape[0]
    comp_per, targ_per = comp_rows // side, targ_rows // side

    if first:
        places = [
            pltpu.make_async_copy(source, place_buf.at[n], place_sems.at[n])
            for n, source in enumerate((row_ref, col_ref))
        ]
        for copy in places:
            copy.start()
        copies = tile_copies(values_hbm, weight_hbm, values_ref, weight_ref, sems)
        copies = list(copies)
        for start, both in copies:

            @pl.when(start < live_ref[0])
            def _():
                for copy in both:
                    copy.start()

        slots = values_hbm.shape[0]
        values_ref[slots] = jnp.zeros_like(values_ref[slots])
        weight_ref[slots] = jnp.zeros_like(weight_ref[slots])
        for copy in places:
            copy.wait()
        row_index, col_index = lax.axis_index("row"), lax.axis_index("col")
        local = place_buf[0] - row_index * (cols * comp_per)
        comp_place = (lax.div(local, comp_per) ^ col_index) * comp_per + lax.rem(local, comp_per)
        holder = lax.div(place_buf[1], targ_per * cols)
        targ_place = (holder ^ row_index) * targ_per + lax.rem(place_buf[1], targ_per)
        alive = lax.broadcasted_iota(jnp.int32, (1, slots), 1) < live_ref[0]
        spare = cols * comp_per * rows * targ_per
        pair = jnp.where(alive, comp_place * (rows * targ_per) + targ_place, spare)
        sizes = cols * comp_per, rows * targ_per, pred.shape[0] - 1
        lists_buf[...] = list_slots(pair, *sizes, PARTS)
        to_scalars = pltpu.make_async_copy(lists_buf, lists_ref, place_sems.at[2])
        to_scalars.start()
        lists_out[...] = list_slots(pair, *sizes, 1)

    def fill(spot, tile, tiles, flip, acc):
        tiles[spot] = tile
        flip[spot] = tile.T
        acc[spot] = jnp.zeros(acc.shape[1:], acc.dtype)

    for n in range(rows):
        for i in range(targ_per):
            tile = targ_blocks[n][i * side : (i + 1) * side]
            fill(n * targ_per + i, tile, targ_tiles, targ_flip, targ_acc)
    for n in range(cols):
        for i in range(comp_per):
            tile = (comp_seconds if n % 2 else comp_firsts)[n // 2][i * side : (i + 1) * side]
            fill(n * comp_per + i, tile, comp_tiles, comp_flip, comp_acc)

    if first:
        to_scalars.wait()

    def steps(count, unroll):
        return lax.div(count + (unroll - 1), unroll)

    def pair_at(step):
        spots = [step * PAIRS + n for n in range(PAIRS)]
        return [(spot, lists_ref[GROUP + 1, spot], lists_ref[GROUP + 2, spot]) for spot in spots]

    last = pred.shape[0] - 1
    pairs, groups = lists_ref[GROUP + 3, 1], lists_ref[GROUP + 3, 0]

    def predict(step, unused):
        blocks = [
            (spot, jnp.dot(comp_tiles[i], targ_flip[j], preferred_element_type=jnp.float32))
            for spot, i, j in pair_at(step)
        ]
        for spot, block in blocks:
            spot = jnp.minimum(spot, last)
            pred[spot] = block.astype(pred.dtype)
            total[spot] = jnp.zeros(total.shape[1:], total.dtype)
        return unused

    lax.fori_loop(0, steps(pairs, PAIRS), predict, 0)

    one = degrees_free * noise_scale * noise_scale
    assert one == 1.0

    def weigh(step, unused):
        for n in range(UNROLL):
            group = step * UNROLL + n
            spot = lists_ref[GROUP, group]
            guess = pred[spot].astype(jnp.float32)
            whole = None
            for m in range(GROUP):
                slot = lists_ref[m, group]
                resid = values_ref[slot].astype(jnp.float32) - guess
                scaled = weight_ref[slot].astype(jnp.float32)
                if m % 2:
                    scaled *= pl.reciprocal(resid + pl.reciprocal(resid, approx=True), approx=True)
                else:
                    scaled *= resid * pl.reciprocal(one + resid * resid, approx=True)
                whole = scaled if whole is None else whole + scaled
            total[spot] += whole
        return unused

    done = 0
    if first:
        span = values_hbm.shape[0] // PARTS
        early = lax.div(lists_ref[GROUP + 3, 2], UNROLL)
        for low, high in ((0, span), (span, values_hbm.shape[0])):
            for start, both in copies:
                if low <= start < high:

                    @pl.when(start < live_ref[0])
                    def _():
                        for copy in both:
                            copy.wait()

            if low == 0:
                lax.fori_loop(0, early, weigh, 0)
        done = early
    lax.fori_loop(done, steps(groups, UNROLL), weigh, 0)

    def gather(step, unused):
        parts = []
        for spot, i, j in pair_at(step):
            weights = total[jnp.minimum(spot, last)].astype(jnp.bfloat16)
            comp_part = jnp.dot(weights, targ_tiles[j], preferred_element_type=jnp.float32)
            targ_part = jnp.dot(comp_flip[i], weights, preferred_element_type=jnp.float32)
            parts.append((i, comp_part, j, targ_part))
        for i, comp_part, j, targ_part in parts:
            comp_acc[i] += comp_part
            targ_acc[j] += targ_part
        return unused

    lax.fori_loop(0, steps(pairs, PAIRS), gather, 0)

    gain = degrees_free + 1.0
    for n in range(cols):
        out = comp_send if n % 2 else comp_keep
        for i in range(comp_per):
            part = comp_acc[n * comp_per + i] * gain
            out[n // 2, i * side : (i + 1) * side] = part.astype(out.dtype)
    for n in range(rows):
        out = targ_outs[n]
        for i in range(targ_per):
            part = targ_acc[n * targ_per + i] * gain
            out[i * side : (i + 1) * side] = part.T.astype(out.dtype)


smem = pl.BlockSpec(memory_space=pltpu.SMEM)
vmem = pl.BlockSpec(memory_space=pltpu.VMEM)
hbm = pl.BlockSpec(memory_space=pltpu.HBM)


def local_grads(slots_at, comp_firsts, comp_seconds, targ_blocks, values, weight):
    first = len(slots_at) > 1
    cols, rows = 2 * len(comp_firsts), len(targ_blocks)
    comp_rows, rank = comp_firsts[0].shape
    targ_rows = targ_blocks[0].shape[0]
    side = values.shape[1]
    comp_tiles, targ_tiles = cols * comp_rows // side, rows * targ_rows // side
    slots = values.shape[0] if first else values.shape[0] - 1
    pairs = min(comp_tiles * targ_tiles, slots)
    held = (pairs + 1) * side * side * 6 + (comp_tiles + targ_tiles + 2) * side * rank * 8
    held += 4 * 2**20 if first else 4 * values.size
    comp_shape = jax.ShapeDtypeStruct((cols // 2, comp_rows, rank), jnp.bfloat16)
    targ_shape = jax.ShapeDtypeStruct((targ_rows, rank), jnp.bfloat16)
    outs = [comp_shape] * 2 + [targ_shape] * rows
    scratch = []
    ins = [smem, hbm, hbm] if first else [smem]
    if first:
        lists = (GROUP + 4, slots)
        outs += [pltpu.VMEM((slots + 1, side, side), x.dtype) for x in (values, weight)]
        outs += [jax.ShapeDtypeStruct(lists, jnp.int32)]
        scratch = [pltpu.SMEM(lists, jnp.int32), pltpu.VMEM(lists, jnp.int32)]
        scratch += [pltpu.VMEM((2, 1, slots), jnp.int32), pltpu.SemaphoreType.DMA((3,))]
        scratch += [pltpu.SemaphoreType.DMA((2, slots // math.gcd(slots, 16)))]
        values, weight, *places = (
            pltpu.with_memory_space_constraint(x, pltpu.HBM) for x in (values, weight, *slots_at[1:])
        )
        slots_at = (slots_at[0], *places)
    ins += [vmem] * (cols + rows) + [hbm if first else vmem] * 2
    outs = pl.pallas_call(
        functools.partial(force_kernel, cols, rows, first),
        out_shape=outs,
        in_specs=ins,
        out_specs=[vmem] * len(outs),
        scratch_shapes=[
            *scratch,
            pltpu.VMEM((pairs + 1, side, side), jnp.bfloat16),
            pltpu.VMEM((pairs + 1, side, side), jnp.float32),
            pltpu.VMEM((comp_tiles + 1, side, rank), jnp.bfloat16),
            pltpu.VMEM((comp_tiles + 1, rank, side), jnp.bfloat16),
            pltpu.VMEM((targ_tiles + 1, side, rank), jnp.bfloat16),
            pltpu.VMEM((targ_tiles + 1, rank, side), jnp.bfloat16),
            pltpu.VMEM((comp_tiles + 1, side, rank), jnp.float32),
            pltpu.VMEM((targ_tiles + 1, rank, side), jnp.float32),
        ],
        compiler_params=pltpu.CompilerParams(vmem_limit_bytes=held + 4 * 2**20),
        name="tile_force",
    )(*slots_at, *comp_firsts, *comp_seconds, *targ_blocks, values, weight)
    return outs[0], outs[1], outs[2 : 2 + rows], outs[2 + rows :]


def round_kernel(comp_ref, targ_ref, comp_out, targ_out):
    comp_out[...] = comp_ref[...].astype(comp_out.dtype)
    targ_out[...] = targ_ref[...].astype(targ_out.dtype)


def rounded(*blocks):
    blocks = [pltpu.with_memory_space_constraint(x, pltpu.HBM) for x in blocks]
    return pl.pallas_call(
        round_kernel,
        out_shape=[jax.ShapeDtypeStruct(x.shape, jnp.bfloat16) for x in blocks],
        in_specs=[vmem] * 2,
        out_specs=[vmem] * 2,
        name="round_factors",
    )(*blocks)


def swap(block, axis, offset):
    size = lax.axis_size(axis)
    return lax.ppermute(block, axis, [(i, i ^ offset) for i in range(size)])


def spread(block, axis):
    size = lax.axis_size(axis)
    seconds = [block] + [swap(block, axis, offset) for offset in range(2, size, 2)]
    return [each for second in seconds for each in (second, swap(second, axis, 1))]


def collect(blocks, axis):
    whole = blocks[0].astype(jnp.float32)
    for offset in range(2, len(blocks), 2):
        near = swap(blocks[offset + 1], axis, 1).astype(jnp.float32)
        far = (blocks[offset].astype(jnp.float32) + near).astype(blocks[offset].dtype)
        whole = whole + swap(far, axis, offset).astype(jnp.float32)
    return whole + swap(blocks[1], axis, 1).astype(jnp.float32)


def spread_pairs(block, axis):
    firsts = [block]
    firsts += [swap(block, axis, offset) for offset in range(2, lax.axis_size(axis), 2)]
    return firsts, [swap(block, axis, 1) for block in firsts]


def collect_pairs(keep, send, axis):
    got = swap(send, axis, 1)
    both = [
        keep[n].astype(jnp.float32) + got[n].astype(jnp.float32) for n in range(keep.shape[0])
    ]
    whole = both[0]
    for n, block in enumerate(both[1:]):
        whole = whole + swap(block.astype(keep.dtype), axis, 2 * n + 2).astype(jnp.float32)
    return whole


def body(
    compound_pos,
    compound_mom,
    target_pos,
    target_mom,
    tile_rows,
    tile_cols,
    tile_count,
    tile_values,
    tile_weight,
):
    cols, rows = lax.axis_size("col"), lax.axis_size("row")
    assert cols & (cols - 1) == 0 and rows & (rows - 1) == 0
    held = (tile_values[0], tile_weight[0], tile_count, tile_rows, tile_cols)

    def forces(comp, targ):
        nonlocal held
        low = (comp.astype(jnp.bfloat16), targ.astype(jnp.bfloat16))
        if comp is compound_pos:
            low = rounded(comp, targ)
        comp_keep, comp_send, targ_parts, kept = local_grads(
            held[2:],
            *spread_pairs(low[0], "col"),
            spread(low[1], "row"),
            *held[:2],
        )
        held = kept or held
        comp_sum = collect_pairs(comp_keep, comp_send, "col")
        targ_sum = collect(targ_parts, "row")
        return comp_sum - prior_weight * comp, targ_sum - prior_weight * targ

    places = (compound_pos, target_pos)
    speeds = (compound_mom, target_mom)
    push = forces(*places)
    for leap in range(LEAPS):
        scale = (0.5 if leap == 0 else 1.0) * step_size
        speeds = tuple(p + scale * f for p, f in zip(speeds, push))
        places = tuple(q + step_size * p for q, p in zip(places, speeds))
        push = forces(*places)
    speeds = tuple(p + 0.5 * step_size * f for p, f in zip(speeds, push))
    return (places[0], speeds[0], places[1], speeds[1])


def solution(mesh):
    split = P(("row", "col"), None)
    tiles = P(("row", "col"), None, None, None)
    return jax.shard_map(
        body,
        mesh=mesh,
        in_specs=(split,) * 6 + (P(("row", "col")), tiles, tiles),
        out_specs=(split,) * 4,
        check_vma=False,
    )
```

```python
import functools
import math

import jax
import jax.numpy as jnp
from jax import lax
from jax.experimental import pallas as pl
from jax.experimental.pallas import tpu as pltpu
from jax.sharding import PartitionSpec as P

LEAPS = 2
GROUP = 4
UNROLL = 4
PAIRS = 8
PARTS = 2


degrees_free = 4.0
noise_scale = 0.5
prior_weight = 1.0
step_size = 0.01


def tile_copies(values_hbm, weight_hbm, values_ref, weight_ref, sems):
    chunks = sems.shape[1]
    chunk = values_hbm.shape[0] // chunks
    for index in range(chunks):
        part = pl.ds(index * chunk, chunk)
        yield index * chunk, [
            pltpu.make_async_copy(values_hbm.at[part], values_ref.at[part], sems.at[0, index]),
            pltpu.make_async_copy(weight_hbm.at[part], weight_ref.at[part], sems.at[1, index]),
        ]


def list_slots(pair, comp_tiles, targ_tiles, pairs, parts):
    slots = pair.shape[1]
    across = jnp.broadcast_to(pair.astype(jnp.float32), (slots, slots))
    down = across.T
    at = lax.broadcasted_iota(jnp.int32, (slots, slots), 1).astype(jnp.float32)
    mine = lax.broadcasted_iota(jnp.int32, (slots, slots), 0).astype(jnp.float32)
    spare = float(comp_tiles * targ_tiles)
    span = slots // parts
    part_across, part_down = jnp.floor(at * (1.0 / span)), jnp.floor(mine * (1.0 / span))
    key_across, key_down = (
        pair + part * (spare + 1.0)
        for pair, part in ((across, part_across), (down, part_down))
    )
    same = key_down == key_across

    def count(mask, axis):
        return jnp.sum(jnp.where(mask, 1.0, 0.0), axis=axis, keepdims=True)

    earlier = count(same & (mine < at), 0)
    groups = jnp.floor((count(same, 0) + (GROUP - 1.0)) * (1.0 / GROUP))
    opens = (earlier == 0.0) & (across[:1] < spare)
    leads = (count((down == across) & (mine < at), 0) == 0.0) & (across[:1] < spare)
    rank = count((across < down) & leads, 1)
    before = (key_across < key_down) & opens
    first = jnp.sum(jnp.where(before, groups, 0.0), axis=1, keepdims=True)
    pair = down[:, :1]
    earlier = count(same & (at < mine), 1)
    alive = pair < spare
    opens = (earlier == 0.0) & alive
    leads = (count((down == across) & (at < mine), 1) == 0.0) & alive
    step = jnp.floor(earlier * (1.0 / GROUP))
    place = jnp.where(alive, first + step, -1.0)
    member = earlier - GROUP * step
    groups = jnp.floor((count(same, 1) + (GROUP - 1.0)) * (1.0 / GROUP))

    def pick(mask, value, rest):
        return jnp.sum(jnp.where(mask, value - rest, 0.0), axis=0, keepdims=True) + rest

    here = place == at
    comp_tile = jnp.floor((pair + 0.5) * (1.0 / targ_tiles))
    rows = [pick(here & (member == n), mine[:, :1], float(slots)) for n in range(GROUP)]
    rows.append(pick(here & (member == 0.0), rank, float(pairs)))
    here = (rank == at) & leads
    rows.append(pick(here, comp_tile, float(comp_tiles)))
    rows.append(pick(here, pair - targ_tiles * comp_tile, float(targ_tiles)))
    early = jnp.where(part_down[:, :1] == 0.0, groups, 0.0)
    totals = [
        jnp.sum(jnp.where(mask, value, 0.0), axis=0, keepdims=True)
        for mask, value in ((opens, groups), (leads, 1.0), (opens, early))
    ]
    whole = jnp.where(at[:1] == 1.0, totals[1], totals[2])
    rows.append(jnp.where(at[:1] == 0.0, totals[0], whole))
    return jnp.concatenate(rows, axis=0).astype(jnp.int32)


def force_kernel(cols, rows, first, *refs):
    if first:
        live_ref, row_ref, col_ref, refs = *refs[:3], refs[3:]
    else:
        lists_ref, refs = refs[0], refs[1:]
    comp_firsts, refs = refs[: cols // 2], refs[cols // 2 :]
    comp_seconds, refs = refs[: cols // 2], refs[cols // 2 :]
    targ_blocks, refs = refs[:rows], refs[rows:]
    values_ref, weight_ref, refs = refs[0], refs[1], refs[2:]
    comp_keep, comp_send, refs = refs[0], refs[1], refs[2:]
    targ_outs, refs = refs[:rows], refs[rows:]
    if first:
        values_hbm, weight_hbm = values_ref, weight_ref
        values_ref, weight_ref, lists_out, refs = *refs[:3], refs[3:]
        lists_ref, place_buf, place_sems, sems, refs = *refs[:4], refs[4:]
    pred, total, comp_tiles, comp_flip, targ_tiles, targ_flip, comp_acc, targ_acc = refs
    side = values_ref.shape[1]
    comp_rows, targ_rows = comp_firsts[0].shape[0], targ_blocks[0].shape[0]
    comp_per, targ_per = comp_rows // side, targ_rows // side

    if first:
        places = [
            pltpu.make_async_copy(source, place_buf.at[n], place_sems.at[n])
            for n, source in enumerate((row_ref, col_ref))
        ]
        for copy in places:
            copy.start()
        copies = tile_copies(values_hbm, weight_hbm, values_ref, weight_ref, sems)
        copies = list(copies)
        for start, both in copies:

            @pl.when(start < live_ref[0])
            def _():
                for copy in both:
                    copy.start()

        slots = values_hbm.shape[0]
        values_ref[slots] = jnp.zeros_like(values_ref[slots])
        weight_ref[slots] = jnp.zeros_like(weight_ref[slots])
        for copy in places:
            copy.wait()
        row_index, col_index = lax.axis_index("row"), lax.axis_index("col")
        local = place_buf[0] - row_index * (cols * comp_per)
        comp_place = (lax.div(local, comp_per) ^ col_index) * comp_per + lax.rem(local, comp_per)
        holder = lax.div(place_buf[1], targ_per * cols)
        targ_place = (holder ^ row_index) * targ_per + lax.rem(place_buf[1], targ_per)
        alive = lax.broadcasted_iota(jnp.int32, (1, slots), 1) < live_ref[0]
        spare = cols * comp_per * rows * targ_per
        pair = jnp.where(alive, comp_place * (rows * targ_per) + targ_place, spare)
        sizes = cols * comp_per, rows * targ_per, pred.shape[0] - 1
        lists_out[...] = list_slots(pair, *sizes, PARTS)
        to_scalars = pltpu.make_async_copy(lists_out, lists_ref, place_sems.at[2])
        to_scalars.start()

    def fill(spot, tile, tiles, flip, acc):
        tiles[spot] = tile
        flip[spot] = tile.T
        acc[spot] = jnp.zeros(acc.shape[1:], acc.dtype)

    for n in range(rows):
        for i in range(targ_per):
            tile = targ_blocks[n][i * side : (i + 1) * side]
            fill(n * targ_per + i, tile, targ_tiles, targ_flip, targ_acc)
    for n in range(cols):
        for i in range(comp_per):
            tile = (comp_seconds if n % 2 else comp_firsts)[n // 2][i * side : (i + 1) * side]
            fill(n * comp_per + i, tile, comp_tiles, comp_flip, comp_acc)

    if first:
        to_scalars.wait()

    def steps(count, unroll):
        return lax.div(count + (unroll - 1), unroll)

    def pair_at(step):
        spots = [step * PAIRS + n for n in range(PAIRS)]
        return [(spot, lists_ref[GROUP + 1, spot], lists_ref[GROUP + 2, spot]) for spot in spots]

    last = pred.shape[0] - 1
    pairs, groups = lists_ref[GROUP + 3, 1], lists_ref[GROUP + 3, 0]

    def predict(step, unused):
        blocks = [
            (spot, jnp.dot(comp_tiles[i], targ_flip[j], preferred_element_type=jnp.float32))
            for spot, i, j in pair_at(step)
        ]
        for spot, block in blocks:
            spot = jnp.minimum(spot, last)
            pred[spot] = block.astype(pred.dtype)
            total[spot] = jnp.zeros(total.shape[1:], total.dtype)
        return unused

    lax.fori_loop(0, steps(pairs, PAIRS), predict, 0)

    one = degrees_free * noise_scale * noise_scale
    assert one == 1.0

    def weigh(step, unused):
        for n in range(UNROLL):
            group = step * UNROLL + n
            spot = lists_ref[GROUP, group]
            guess = pred[spot].astype(jnp.float32)
            whole = None
            for m in range(GROUP):
                slot = lists_ref[m, group]
                resid = values_ref[slot].astype(jnp.float32) - guess
                scaled = weight_ref[slot].astype(jnp.float32)
                if m % 2:
                    scaled *= pl.reciprocal(resid + pl.reciprocal(resid, approx=True), approx=True)
                else:
                    scaled *= resid * pl.reciprocal(one + resid * resid, approx=True)
                whole = scaled if whole is None else whole + scaled
            total[spot] += whole
        return unused

    done = 0
    if first:
        span = values_hbm.shape[0] // PARTS
        early = lax.div(lists_ref[GROUP + 3, 2], UNROLL)
        for low, high in ((0, span), (span, values_hbm.shape[0])):
            for start, both in copies:
                if low <= start < high:

                    @pl.when(start < live_ref[0])
                    def _():
                        for copy in both:
                            copy.wait()

            if low == 0:
                lax.fori_loop(0, early, weigh, 0)
        done = early
    lax.fori_loop(done, steps(groups, UNROLL), weigh, 0)

    def gather(step, unused):
        parts = []
        for spot, i, j in pair_at(step):
            weights = total[jnp.minimum(spot, last)].astype(jnp.bfloat16)
            comp_part = jnp.dot(weights, targ_tiles[j], preferred_element_type=jnp.float32)
            targ_part = jnp.dot(comp_flip[i], weights, preferred_element_type=jnp.float32)
            parts.append((i, comp_part, j, targ_part))
        for i, comp_part, j, targ_part in parts:
            comp_acc[i] += comp_part
            targ_acc[j] += targ_part
        return unused

    lax.fori_loop(0, steps(pairs, PAIRS), gather, 0)

    gain = degrees_free + 1.0
    for n in range(cols):
        out = comp_send if n % 2 else comp_keep
        for i in range(comp_per):
            part = comp_acc[n * comp_per + i] * gain
            out[n // 2, i * side : (i + 1) * side] = part.astype(out.dtype)
    for n in range(rows):
        out = targ_outs[n]
        for i in range(targ_per):
            part = targ_acc[n * targ_per + i] * gain
            out[i * side : (i + 1) * side] = part.T.astype(out.dtype)


smem = pl.BlockSpec(memory_space=pltpu.SMEM)
vmem = pl.BlockSpec(memory_space=pltpu.VMEM)
hbm = pl.BlockSpec(memory_space=pltpu.HBM)


def local_grads(slots_at, comp_firsts, comp_seconds, targ_blocks, values, weight):
    first = len(slots_at) > 1
    cols, rows = 2 * len(comp_firsts), len(targ_blocks)
    comp_rows, rank = comp_firsts[0].shape
    targ_rows = targ_blocks[0].shape[0]
    side = values.shape[1]
    comp_tiles, targ_tiles = cols * comp_rows // side, rows * targ_rows // side
    slots = values.shape[0] if first else values.shape[0] - 1
    pairs = min(comp_tiles * targ_tiles, slots)
    held = (pairs + 1) * side * side * 6 + (comp_tiles + targ_tiles + 2) * side * rank * 8
    held += 4 * 2**20 if first else 4 * values.size
    comp_shape = jax.ShapeDtypeStruct((cols // 2, comp_rows, rank), jnp.bfloat16)
    targ_shape = jax.ShapeDtypeStruct((targ_rows, rank), jnp.bfloat16)
    outs = [comp_shape] * 2 + [targ_shape] * rows
    scratch = []
    ins = [smem, hbm, hbm] if first else [smem]
    if first:
        lists = (GROUP + 4, slots)
        outs += [pltpu.VMEM((slots + 1, side, side), x.dtype) for x in (values, weight)]
        outs += [jax.ShapeDtypeStruct(lists, jnp.int32)]
        scratch = [pltpu.SMEM(lists, jnp.int32)]
        scratch += [pltpu.VMEM((2, 1, slots), jnp.int32), pltpu.SemaphoreType.DMA((3,))]
        scratch += [pltpu.SemaphoreType.DMA((2, slots // math.gcd(slots, 16)))]
        values, weight, *places = (
            pltpu.with_memory_space_constraint(x, pltpu.HBM) for x in (values, weight, *slots_at[1:])
        )
        slots_at = (slots_at[0], *places)
    ins += [vmem] * (cols + rows) + [hbm if first else vmem] * 2
    outs = pl.pallas_call(
        functools.partial(force_kernel, cols, rows, first),
        out_shape=outs,
        in_specs=ins,
        out_specs=[vmem] * len(outs),
        scratch_shapes=[
            *scratch,
            pltpu.VMEM((pairs + 1, side, side), jnp.bfloat16),
            pltpu.VMEM((pairs + 1, side, side), jnp.float32),
            pltpu.VMEM((comp_tiles + 1, side, rank), jnp.bfloat16),
            pltpu.VMEM((comp_tiles + 1, rank, side), jnp.bfloat16),
            pltpu.VMEM((targ_tiles + 1, side, rank), jnp.bfloat16),
            pltpu.VMEM((targ_tiles + 1, rank, side), jnp.bfloat16),
            pltpu.VMEM((comp_tiles + 1, side, rank), jnp.float32),
            pltpu.VMEM((targ_tiles + 1, rank, side), jnp.float32),
        ],
        compiler_params=pltpu.CompilerParams(vmem_limit_bytes=held + 4 * 2**20),
        name="tile_force",
    )(*slots_at, *comp_firsts, *comp_seconds, *targ_blocks, values, weight)
    return outs[0], outs[1], outs[2 : 2 + rows], outs[2 + rows :]


def swap(block, axis, offset):
    size = lax.axis_size(axis)
    return lax.ppermute(block, axis, [(i, i ^ offset) for i in range(size)])


def spread(block, axis):
    size = lax.axis_size(axis)
    seconds = [block] + [swap(block, axis, offset) for offset in range(2, size, 2)]
    return [each for second in seconds for each in (second, swap(second, axis, 1))]


def collect(blocks, axis):
    whole = blocks[0].astype(jnp.float32)
    for offset in range(2, len(blocks), 2):
        near = swap(blocks[offset + 1], axis, 1).astype(jnp.float32)
        far = (blocks[offset].astype(jnp.float32) + near).astype(blocks[offset].dtype)
        whole = whole + swap(far, axis, offset).astype(jnp.float32)
    return whole + swap(blocks[1], axis, 1).astype(jnp.float32)


def spread_pairs(block, axis):
    firsts = [block]
    firsts += [swap(block, axis, offset) for offset in range(2, lax.axis_size(axis), 2)]
    return firsts, [swap(block, axis, 1) for block in firsts]


def collect_pairs(keep, send, axis):
    got = swap(send, axis, 1)
    both = [
        keep[n].astype(jnp.float32) + got[n].astype(jnp.float32) for n in range(keep.shape[0])
    ]
    whole = both[0]
    for n, block in enumerate(both[1:]):
        whole = whole + swap(block.astype(keep.dtype), axis, 2 * n + 2).astype(jnp.float32)
    return whole


def body(
    compound_pos,
    compound_mom,
    target_pos,
    target_mom,
    tile_rows,
    tile_cols,
    tile_count,
    tile_values,
    tile_weight,
):
    cols, rows = lax.axis_size("col"), lax.axis_size("row")
    assert cols & (cols - 1) == 0 and rows & (rows - 1) == 0
    held = (tile_values[0], tile_weight[0], tile_count, tile_rows, tile_cols)

    def forces(comp, targ):
        nonlocal held
        comp_keep, comp_send, targ_parts, kept = local_grads(
            held[2:],
            *spread_pairs(comp.astype(jnp.bfloat16), "col"),
            spread(targ.astype(jnp.bfloat16), "row"),
            *held[:2],
        )
        held = kept or held
        comp_sum = collect_pairs(comp_keep, comp_send, "col")
        targ_sum = collect(targ_parts, "row")
        return comp_sum - prior_weight * comp, targ_sum - prior_weight * targ

    places = (compound_pos, target_pos)
    speeds = (compound_mom, target_mom)
    push = forces(*places)
    for leap in range(LEAPS):
        scale = (0.5 if leap == 0 else 1.0) * step_size
        speeds = tuple(p + scale * f for p, f in zip(speeds, push))
        places = tuple(q + step_size * p for q, p in zip(places, speeds))
        push = forces(*places)
    speeds = tuple(p + 0.5 * step_size * f for p, f in zip(speeds, push))
    return (places[0], speeds[0], places[1], speeds[1])


def solution(mesh):
    split = P(("row", "col"), None)
    tiles = P(("row", "col"), None, None, None)
    return jax.shard_map(
        body,
        mesh=mesh,
        in_specs=(split,) * 6 + (P(("row", "col")), tiles, tiles),
        out_specs=(split,) * 4,
        check_vma=False,
    )
```

```python
import functools
import math

import jax
import jax.numpy as jnp
from jax import lax
from jax.experimental import pallas as pl
from jax.experimental.pallas import tpu as pltpu
from jax.sharding import PartitionSpec as P

LEAPS = 2
GROUP = 4
UNROLL = 4
PAIRS = 8


degrees_free = 4.0
noise_scale = 0.5
prior_weight = 1.0
step_size = 0.01


def tile_copies(values_hbm, weight_hbm, values_ref, weight_ref, sems):
    chunks = sems.shape[1]
    chunk = values_hbm.shape[0] // chunks
    for index in range(chunks):
        part = pl.ds(index * chunk, chunk)
        yield index * chunk, [
            pltpu.make_async_copy(values_hbm.at[part], values_ref.at[part], sems.at[0, index]),
            pltpu.make_async_copy(weight_hbm.at[part], weight_ref.at[part], sems.at[1, index]),
        ]


def list_slots(pair, comp_tiles, targ_tiles, pairs):
    slots = pair.shape[1]
    across = jnp.broadcast_to(pair.astype(jnp.float32), (slots, slots))
    down = across.T
    at = lax.broadcasted_iota(jnp.int32, (slots, slots), 1).astype(jnp.float32)
    mine = lax.broadcasted_iota(jnp.int32, (slots, slots), 0).astype(jnp.float32)
    spare = float(comp_tiles * targ_tiles)
    same = down == across

    def count(mask, axis):
        return jnp.sum(jnp.where(mask, 1.0, 0.0), axis=axis, keepdims=True)

    earlier = count(same & (mine < at), 0)
    groups = jnp.floor((count(same, 0) + (GROUP - 1.0)) * (1.0 / GROUP))
    opens = (earlier == 0.0) & (across[:1] < spare)
    before = across < down
    rank = jnp.sum(jnp.where(before & opens, 1.0, 0.0), axis=1, keepdims=True)
    first = jnp.sum(jnp.where(before & opens, groups, 0.0), axis=1, keepdims=True)
    pair = down[:, :1]
    earlier = count(same & (at < mine), 1)
    alive = pair < spare
    opens = (earlier == 0.0) & alive
    step = jnp.floor(earlier * (1.0 / GROUP))
    place = jnp.where(alive, first + step, -1.0)
    member = earlier - GROUP * step
    groups = jnp.floor((count(same, 1) + (GROUP - 1.0)) * (1.0 / GROUP))

    def pick(mask, value, rest):
        return jnp.sum(jnp.where(mask, value - rest, 0.0), axis=0, keepdims=True) + rest

    here = place == at
    comp_tile = jnp.floor((pair + 0.5) * (1.0 / targ_tiles))
    rows = [pick(here & (member == n), mine[:, :1], float(slots)) for n in range(GROUP)]
    rows.append(pick(here & (member == 0.0), rank, float(pairs)))
    here = (rank == at) & opens
    rows.append(pick(here, comp_tile, float(comp_tiles)))
    rows.append(pick(here, pair - targ_tiles * comp_tile, float(targ_tiles)))
    totals = [jnp.sum(jnp.where(opens, n, 0.0), axis=0, keepdims=True) for n in (groups, 1.0)]
    rows.append(jnp.where(at[:1] == 0.0, totals[0], totals[1]))
    return jnp.concatenate(rows, axis=0).astype(jnp.int32)


def force_kernel(cols, rows, first, *refs):
    if first:
        live_ref, row_ref, col_ref, refs = *refs[:3], refs[3:]
    else:
        lists_ref, refs = refs[0], refs[1:]
    comp_firsts, refs = refs[: cols // 2], refs[cols // 2 :]
    comp_seconds, refs = refs[: cols // 2], refs[cols // 2 :]
    targ_blocks, refs = refs[:rows], refs[rows:]
    values_ref, weight_ref, refs = refs[0], refs[1], refs[2:]
    comp_keep, comp_send, refs = refs[0], refs[1], refs[2:]
    targ_outs, refs = refs[:rows], refs[rows:]
    if first:
        values_hbm, weight_hbm = values_ref, weight_ref
        values_ref, weight_ref, lists_out, refs = *refs[:3], refs[3:]
        lists_ref, place_buf, place_sems, sems, refs = *refs[:4], refs[4:]
    pred, total, comp_tiles, comp_flip, targ_tiles, targ_flip, comp_acc, targ_acc = refs
    side = values_ref.shape[1]
    comp_rows, targ_rows = comp_firsts[0].shape[0], targ_blocks[0].shape[0]
    comp_per, targ_per = comp_rows // side, targ_rows // side

    if first:
        places = [
            pltpu.make_async_copy(source, place_buf.at[n], place_sems.at[n])
            for n, source in enumerate((row_ref, col_ref))
        ]
        for copy in places:
            copy.start()
        copies = tile_copies(values_hbm, weight_hbm, values_ref, weight_ref, sems)
        copies = list(copies)
        for start, both in copies:

            @pl.when(start < live_ref[0])
            def _():
                for copy in both:
                    copy.start()

        slots = values_hbm.shape[0]
        values_ref[slots] = jnp.zeros_like(values_ref[slots])
        weight_ref[slots] = jnp.zeros_like(weight_ref[slots])
        for copy in places:
            copy.wait()
        row_index, col_index = lax.axis_index("row"), lax.axis_index("col")
        local = place_buf[0] - row_index * (cols * comp_per)
        comp_place = (lax.div(local, comp_per) ^ col_index) * comp_per + lax.rem(local, comp_per)
        holder = lax.div(place_buf[1], targ_per * cols)
        targ_place = (holder ^ row_index) * targ_per + lax.rem(place_buf[1], targ_per)
        alive = lax.broadcasted_iota(jnp.int32, (1, slots), 1) < live_ref[0]
        spare = cols * comp_per * rows * targ_per
        pair = jnp.where(alive, comp_place * (rows * targ_per) + targ_place, spare)
        lists_out[...] = list_slots(pair, cols * comp_per, rows * targ_per, pred.shape[0] - 1)
        to_scalars = pltpu.make_async_copy(lists_out, lists_ref, place_sems.at[2])
        to_scalars.start()

    def fill(spot, tile, tiles, flip, acc):
        tiles[spot] = tile
        flip[spot] = tile.T
        acc[spot] = jnp.zeros(acc.shape[1:], acc.dtype)

    for n in range(rows):
        for i in range(targ_per):
            tile = targ_blocks[n][i * side : (i + 1) * side]
            fill(n * targ_per + i, tile, targ_tiles, targ_flip, targ_acc)
    for n in range(cols):
        for i in range(comp_per):
            tile = (comp_seconds if n % 2 else comp_firsts)[n // 2][i * side : (i + 1) * side]
            fill(n * comp_per + i, tile, comp_tiles, comp_flip, comp_acc)

    if first:
        to_scalars.wait()

    def steps(count, unroll):
        return lax.div(count + (unroll - 1), unroll)

    def pair_at(step):
        spots = [step * PAIRS + n for n in range(PAIRS)]
        return [(spot, lists_ref[GROUP + 1, spot], lists_ref[GROUP + 2, spot]) for spot in spots]

    last = pred.shape[0] - 1
    pairs, groups = lists_ref[GROUP + 3, 1], lists_ref[GROUP + 3, 0]

    def predict(step, unused):
        blocks = [
            (spot, jnp.dot(comp_tiles[i], targ_flip[j], preferred_element_type=jnp.float32))
            for spot, i, j in pair_at(step)
        ]
        for spot, block in blocks:
            spot = jnp.minimum(spot, last)
            pred[spot] = block.astype(pred.dtype)
            total[spot] = jnp.zeros(total.shape[1:], total.dtype)
        return unused

    lax.fori_loop(0, steps(pairs, PAIRS), predict, 0)

    if first:
        for start, both in copies:

            @pl.when(start < live_ref[0])
            def _():
                for copy in both:
                    copy.wait()

    one = degrees_free * noise_scale * noise_scale
    assert one == 1.0

    def weigh(step, unused):
        for n in range(UNROLL):
            group = step * UNROLL + n
            spot = lists_ref[GROUP, group]
            guess = pred[spot].astype(jnp.float32)
            whole = None
            for m in range(GROUP):
                slot = lists_ref[m, group]
                resid = values_ref[slot].astype(jnp.float32) - guess
                scaled = weight_ref[slot].astype(jnp.float32)
                if m % 2:
                    scaled *= pl.reciprocal(resid + pl.reciprocal(resid, approx=True), approx=True)
                else:
                    scaled *= resid * pl.reciprocal(one + resid * resid, approx=True)
                whole = scaled if whole is None else whole + scaled
            total[spot] += whole
        return unused

    lax.fori_loop(0, steps(groups, UNROLL), weigh, 0)

    def gather(step, unused):
        parts = []
        for spot, i, j in pair_at(step):
            weights = total[jnp.minimum(spot, last)].astype(jnp.bfloat16)
            comp_part = jnp.dot(weights, targ_tiles[j], preferred_element_type=jnp.float32)
            targ_part = jnp.dot(comp_flip[i], weights, preferred_element_type=jnp.float32)
            parts.append((i, comp_part, j, targ_part))
        for i, comp_part, j, targ_part in parts:
            comp_acc[i] += comp_part
            targ_acc[j] += targ_part
        return unused

    lax.fori_loop(0, steps(pairs, PAIRS), gather, 0)

    gain = degrees_free + 1.0
    for n in range(cols):
        out = comp_send if n % 2 else comp_keep
        for i in range(comp_per):
            part = comp_acc[n * comp_per + i] * gain
            out[n // 2, i * side : (i + 1) * side] = part.astype(out.dtype)
    for n in range(rows):
        out = targ_outs[n]
        for i in range(targ_per):
            part = targ_acc[n * targ_per + i] * gain
            out[i * side : (i + 1) * side] = part.T.astype(out.dtype)


smem = pl.BlockSpec(memory_space=pltpu.SMEM)
vmem = pl.BlockSpec(memory_space=pltpu.VMEM)
hbm = pl.BlockSpec(memory_space=pltpu.HBM)


def local_grads(slots_at, comp_firsts, comp_seconds, targ_blocks, values, weight):
    first = len(slots_at) > 1
    cols, rows = 2 * len(comp_firsts), len(targ_blocks)
    comp_rows, rank = comp_firsts[0].shape
    targ_rows = targ_blocks[0].shape[0]
    side = values.shape[1]
    comp_tiles, targ_tiles = cols * comp_rows // side, rows * targ_rows // side
    slots = values.shape[0] if first else values.shape[0] - 1
    pairs = min(comp_tiles * targ_tiles, slots)
    held = (pairs + 1) * side * side * 6 + (comp_tiles + targ_tiles + 2) * side * rank * 8
    held += 4 * 2**20 if first else 4 * values.size
    comp_shape = jax.ShapeDtypeStruct((cols // 2, comp_rows, rank), jnp.bfloat16)
    targ_shape = jax.ShapeDtypeStruct((targ_rows, rank), jnp.bfloat16)
    outs = [comp_shape] * 2 + [targ_shape] * rows
    scratch = []
    ins = [smem, hbm, hbm] if first else [smem]
    if first:
        lists = (GROUP + 4, slots)
        outs += [pltpu.VMEM((slots + 1, side, side), x.dtype) for x in (values, weight)]
        outs += [jax.ShapeDtypeStruct(lists, jnp.int32)]
        scratch = [pltpu.SMEM(lists, jnp.int32), pltpu.VMEM((2, 1, slots), jnp.int32)]
        scratch += [pltpu.SemaphoreType.DMA((3,))]
        scratch += [pltpu.SemaphoreType.DMA((2, slots // math.gcd(slots, 16)))]
        values, weight, *places = (
            pltpu.with_memory_space_constraint(x, pltpu.HBM) for x in (values, weight, *slots_at[1:])
        )
        slots_at = (slots_at[0], *places)
    ins += [vmem] * (cols + rows) + [hbm if first else vmem] * 2
    outs = pl.pallas_call(
        functools.partial(force_kernel, cols, rows, first),
        out_shape=outs,
        in_specs=ins,
        out_specs=[vmem] * len(outs),
        scratch_shapes=[
            *scratch,
            pltpu.VMEM((pairs + 1, side, side), jnp.bfloat16),
            pltpu.VMEM((pairs + 1, side, side), jnp.float32),
            pltpu.VMEM((comp_tiles + 1, side, rank), jnp.bfloat16),
            pltpu.VMEM((comp_tiles + 1, rank, side), jnp.bfloat16),
            pltpu.VMEM((targ_tiles + 1, side, rank), jnp.bfloat16),
            pltpu.VMEM((targ_tiles + 1, rank, side), jnp.bfloat16),
            pltpu.VMEM((comp_tiles + 1, side, rank), jnp.float32),
            pltpu.VMEM((targ_tiles + 1, rank, side), jnp.float32),
        ],
        compiler_params=pltpu.CompilerParams(vmem_limit_bytes=held + 4 * 2**20),
        name="tile_force",
    )(*slots_at, *comp_firsts, *comp_seconds, *targ_blocks, values, weight)
    return outs[0], outs[1], outs[2 : 2 + rows], outs[2 + rows :]


def swap(block, axis, offset):
    size = lax.axis_size(axis)
    return lax.ppermute(block, axis, [(i, i ^ offset) for i in range(size)])


def spread(block, axis):
    size = lax.axis_size(axis)
    seconds = [block] + [swap(block, axis, offset) for offset in range(2, size, 2)]
    return [each for second in seconds for each in (second, swap(second, axis, 1))]


def collect(blocks, axis):
    whole = blocks[0].astype(jnp.float32)
    for offset in range(2, len(blocks), 2):
        near = swap(blocks[offset + 1], axis, 1).astype(jnp.float32)
        far = (blocks[offset].astype(jnp.float32) + near).astype(blocks[offset].dtype)
        whole = whole + swap(far, axis, offset).astype(jnp.float32)
    return whole + swap(blocks[1], axis, 1).astype(jnp.float32)


def spread_pairs(block, axis):
    firsts = [block]
    firsts += [swap(block, axis, offset) for offset in range(2, lax.axis_size(axis), 2)]
    return firsts, [swap(block, axis, 1) for block in firsts]


def collect_pairs(keep, send, axis):
    got = swap(send, axis, 1)
    both = [
        keep[n].astype(jnp.float32) + got[n].astype(jnp.float32) for n in range(keep.shape[0])
    ]
    whole = both[0]
    for n, block in enumerate(both[1:]):
        whole = whole + swap(block.astype(keep.dtype), axis, 2 * n + 2).astype(jnp.float32)
    return whole


def body(
    compound_pos,
    compound_mom,
    target_pos,
    target_mom,
    tile_rows,
    tile_cols,
    tile_count,
    tile_values,
    tile_weight,
):
    cols, rows = lax.axis_size("col"), lax.axis_size("row")
    assert cols & (cols - 1) == 0 and rows & (rows - 1) == 0
    held = (tile_values[0], tile_weight[0], tile_count, tile_rows, tile_cols)

    def forces(comp, targ):
        nonlocal held
        comp_keep, comp_send, targ_parts, kept = local_grads(
            held[2:],
            *spread_pairs(comp.astype(jnp.bfloat16), "col"),
            spread(targ.astype(jnp.bfloat16), "row"),
            *held[:2],
        )
        held = kept or held
        comp_sum = collect_pairs(comp_keep, comp_send, "col")
        targ_sum = collect(targ_parts, "row")
        return comp_sum - prior_weight * comp, targ_sum - prior_weight * targ

    places = (compound_pos, target_pos)
    speeds = (compound_mom, target_mom)
    push = forces(*places)
    for leap in range(LEAPS):
        scale = (0.5 if leap == 0 else 1.0) * step_size
        speeds = tuple(p + scale * f for p, f in zip(speeds, push))
        places = tuple(q + step_size * p for q, p in zip(places, speeds))
        push = forces(*places)
    speeds = tuple(p + 0.5 * step_size * f for p, f in zip(speeds, push))
    return (places[0], speeds[0], places[1], speeds[1])


def solution(mesh):
    split = P(("row", "col"), None)
    tiles = P(("row", "col"), None, None, None)
    return jax.shard_map(
        body,
        mesh=mesh,
        in_specs=(split,) * 6 + (P(("row", "col")), tiles, tiles),
        out_specs=(split,) * 4,
        check_vma=False,
    )
```

```python
import functools
import math

import jax
import jax.numpy as jnp
from jax import lax
from jax.experimental import pallas as pl
from jax.experimental.pallas import tpu as pltpu
from jax.sharding import PartitionSpec as P

LEAPS = 2
GROUP = 4
UNROLL = 4
PAIRS = 8


degrees_free = 4.0
noise_scale = 0.5
prior_weight = 1.0
step_size = 0.01


def tile_copies(values_hbm, weight_hbm, values_ref, weight_ref, sems):
    chunks = sems.shape[1]
    chunk = values_hbm.shape[0] // chunks
    for index in range(chunks):
        part = pl.ds(index * chunk, chunk)
        yield index * chunk, [
            pltpu.make_async_copy(values_hbm.at[part], values_ref.at[part], sems.at[0, index]),
            pltpu.make_async_copy(weight_hbm.at[part], weight_ref.at[part], sems.at[1, index]),
        ]


def list_slots(pair, comp_tiles, targ_tiles, pairs):
    slots = pair.shape[1]
    across = jnp.broadcast_to(pair.astype(jnp.float32), (slots, slots))
    down = across.T
    at = lax.broadcasted_iota(jnp.int32, (slots, slots), 1).astype(jnp.float32)
    mine = lax.broadcasted_iota(jnp.int32, (slots, slots), 0).astype(jnp.float32)
    spare = float(comp_tiles * targ_tiles)
    same = down == across

    def count(mask, axis):
        return jnp.sum(jnp.where(mask, 1.0, 0.0), axis=axis, keepdims=True)

    earlier = count(same & (mine < at), 0)
    groups = jnp.floor((count(same, 0) + (GROUP - 1.0)) * (1.0 / GROUP))
    opens = (earlier == 0.0) & (across[:1] < spare)
    before = across < down
    rank = jnp.sum(jnp.where(before & opens, 1.0, 0.0), axis=1, keepdims=True)
    first = jnp.sum(jnp.where(before & opens, groups, 0.0), axis=1, keepdims=True)
    pair = down[:, :1]
    earlier = count(same & (at < mine), 1)
    alive = pair < spare
    opens = (earlier == 0.0) & alive
    step = jnp.floor(earlier * (1.0 / GROUP))
    place = jnp.where(alive, first + step, -1.0)
    member = earlier - GROUP * step
    groups = jnp.floor((count(same, 1) + (GROUP - 1.0)) * (1.0 / GROUP))

    def pick(mask, value, rest):
        return jnp.sum(jnp.where(mask, value - rest, 0.0), axis=0, keepdims=True) + rest

    here = place == at
    comp_tile = jnp.floor((pair + 0.5) * (1.0 / targ_tiles))
    rows = [pick(here & (member == n), mine[:, :1], float(slots)) for n in range(GROUP)]
    rows.append(pick(here & (member == 0.0), rank, float(pairs)))
    here = (rank == at) & opens
    rows.append(pick(here, comp_tile, float(comp_tiles)))
    rows.append(pick(here, pair - targ_tiles * comp_tile, float(targ_tiles)))
    totals = [jnp.sum(jnp.where(opens, n, 0.0), axis=0, keepdims=True) for n in (groups, 1.0)]
    rows.append(jnp.where(at[:1] == 0.0, totals[0], totals[1]))
    return jnp.concatenate(rows, axis=0).astype(jnp.int32)


def force_kernel(cols, rows, first, *refs):
    if first:
        live_ref, pair_ref, refs = *refs[:2], refs[2:]
    else:
        lists_ref, refs = refs[0], refs[1:]
    comp_firsts, refs = refs[: cols // 2], refs[cols // 2 :]
    comp_seconds, refs = refs[: cols // 2], refs[cols // 2 :]
    targ_blocks, refs = refs[:rows], refs[rows:]
    values_ref, weight_ref, refs = refs[0], refs[1], refs[2:]
    comp_keep, comp_send, refs = refs[0], refs[1], refs[2:]
    targ_outs, refs = refs[:rows], refs[rows:]
    if first:
        values_hbm, weight_hbm = values_ref, weight_ref
        values_ref, weight_ref, lists_out, refs = *refs[:3], refs[3:]
        lists_ref, list_sem, sems, refs = *refs[:3], refs[3:]
    pred, total, comp_tiles, comp_flip, targ_tiles, targ_flip, comp_acc, targ_acc = refs
    side = values_ref.shape[1]
    comp_rows, targ_rows = comp_firsts[0].shape[0], targ_blocks[0].shape[0]
    comp_per, targ_per = comp_rows // side, targ_rows // side

    if first:
        copies = tile_copies(values_hbm, weight_hbm, values_ref, weight_ref, sems)
        copies = list(copies)
        for start, both in copies:

            @pl.when(start < live_ref[0])
            def _():
                for copy in both:
                    copy.start()

        slots = values_hbm.shape[0]
        values_ref[slots] = jnp.zeros_like(values_ref[slots])
        weight_ref[slots] = jnp.zeros_like(weight_ref[slots])
        sizes = cols * comp_per, rows * targ_per, pred.shape[0] - 1
        lists_out[...] = list_slots(pair_ref[...], *sizes)
        to_scalars = pltpu.make_async_copy(lists_out, lists_ref, list_sem)
        to_scalars.start()

    def fill(spot, tile, tiles, flip, acc):
        tiles[spot] = tile
        flip[spot] = tile.T
        acc[spot] = jnp.zeros(acc.shape[1:], acc.dtype)

    for n in range(rows):
        for i in range(targ_per):
            tile = targ_blocks[n][i * side : (i + 1) * side]
            fill(n * targ_per + i, tile, targ_tiles, targ_flip, targ_acc)
    for n in range(cols):
        for i in range(comp_per):
            tile = (comp_seconds if n % 2 else comp_firsts)[n // 2][i * side : (i + 1) * side]
            fill(n * comp_per + i, tile, comp_tiles, comp_flip, comp_acc)

    if first:
        to_scalars.wait()

    def steps(count, unroll):
        return lax.div(count + (unroll - 1), unroll)

    def pair_at(step):
        spots = [step * PAIRS + n for n in range(PAIRS)]
        return [(spot, lists_ref[GROUP + 1, spot], lists_ref[GROUP + 2, spot]) for spot in spots]

    last = pred.shape[0] - 1
    pairs, groups = lists_ref[GROUP + 3, 1], lists_ref[GROUP + 3, 0]

    def predict(step, unused):
        blocks = [
            (spot, jnp.dot(comp_tiles[i], targ_flip[j], preferred_element_type=jnp.float32))
            for spot, i, j in pair_at(step)
        ]
        for spot, block in blocks:
            spot = jnp.minimum(spot, last)
            pred[spot] = block.astype(pred.dtype)
            total[spot] = jnp.zeros(total.shape[1:], total.dtype)
        return unused

    lax.fori_loop(0, steps(pairs, PAIRS), predict, 0)

    if first:
        for start, both in copies:

            @pl.when(start < live_ref[0])
            def _():
                for copy in both:
                    copy.wait()

    one = degrees_free * noise_scale * noise_scale
    assert one == 1.0

    def weigh(step, unused):
        for n in range(UNROLL):
            group = step * UNROLL + n
            spot = lists_ref[GROUP, group]
            guess = pred[spot].astype(jnp.float32)
            whole = None
            for m in range(GROUP):
                slot = lists_ref[m, group]
                resid = values_ref[slot].astype(jnp.float32) - guess
                scaled = weight_ref[slot].astype(jnp.float32)
                if m % 2:
                    scaled *= pl.reciprocal(resid + pl.reciprocal(resid, approx=True), approx=True)
                else:
                    scaled *= resid * pl.reciprocal(one + resid * resid, approx=True)
                whole = scaled if whole is None else whole + scaled
            total[spot] += whole
        return unused

    lax.fori_loop(0, steps(groups, UNROLL), weigh, 0)

    def gather(step, unused):
        parts = []
        for spot, i, j in pair_at(step):
            weights = total[jnp.minimum(spot, last)].astype(jnp.bfloat16)
            comp_part = jnp.dot(weights, targ_tiles[j], preferred_element_type=jnp.float32)
            targ_part = jnp.dot(comp_flip[i], weights, preferred_element_type=jnp.float32)
            parts.append((i, comp_part, j, targ_part))
        for i, comp_part, j, targ_part in parts:
            comp_acc[i] += comp_part
            targ_acc[j] += targ_part
        return unused

    lax.fori_loop(0, steps(pairs, PAIRS), gather, 0)

    gain = degrees_free + 1.0
    for n in range(cols):
        out = comp_send if n % 2 else comp_keep
        for i in range(comp_per):
            part = comp_acc[n * comp_per + i] * gain
            out[n // 2, i * side : (i + 1) * side] = part.astype(out.dtype)
    for n in range(rows):
        out = targ_outs[n]
        for i in range(targ_per):
            part = targ_acc[n * targ_per + i] * gain
            out[i * side : (i + 1) * side] = part.T.astype(out.dtype)


smem = pl.BlockSpec(memory_space=pltpu.SMEM)
vmem = pl.BlockSpec(memory_space=pltpu.VMEM)
hbm = pl.BlockSpec(memory_space=pltpu.HBM)


def local_grads(slots_at, comp_firsts, comp_seconds, targ_blocks, values, weight):
    first = len(slots_at) > 1
    cols, rows = 2 * len(comp_firsts), len(targ_blocks)
    comp_rows, rank = comp_firsts[0].shape
    targ_rows = targ_blocks[0].shape[0]
    side = values.shape[1]
    comp_tiles, targ_tiles = cols * comp_rows // side, rows * targ_rows // side
    slots = values.shape[0] if first else values.shape[0] - 1
    pairs = min(comp_tiles * targ_tiles, slots)
    held = (pairs + 1) * side * side * 6 + (comp_tiles + targ_tiles + 2) * side * rank * 8
    held += 4 * 2**20 if first else 4 * values.size
    comp_shape = jax.ShapeDtypeStruct((cols // 2, comp_rows, rank), jnp.bfloat16)
    targ_shape = jax.ShapeDtypeStruct((targ_rows, rank), jnp.bfloat16)
    outs = [comp_shape] * 2 + [targ_shape] * rows
    scratch = []
    ins = [smem, vmem] if first else [smem]
    if first:
        lists = (GROUP + 4, slots)
        outs += [pltpu.VMEM((slots + 1, side, side), x.dtype) for x in (values, weight)]
        outs += [jax.ShapeDtypeStruct(lists, jnp.int32)]
        scratch = [pltpu.SMEM(lists, jnp.int32), pltpu.SemaphoreType.DMA]
        scratch += [pltpu.SemaphoreType.DMA((2, slots // math.gcd(slots, 16)))]
        values, weight = (pltpu.with_memory_space_constraint(x, pltpu.HBM) for x in (values, weight))
    ins += [vmem] * (cols + rows) + [hbm if first else vmem] * 2
    outs = pl.pallas_call(
        functools.partial(force_kernel, cols, rows, first),
        out_shape=outs,
        in_specs=ins,
        out_specs=[vmem] * len(outs),
        scratch_shapes=[
            *scratch,
            pltpu.VMEM((pairs + 1, side, side), jnp.bfloat16),
            pltpu.VMEM((pairs + 1, side, side), jnp.float32),
            pltpu.VMEM((comp_tiles + 1, side, rank), jnp.bfloat16),
            pltpu.VMEM((comp_tiles + 1, rank, side), jnp.bfloat16),
            pltpu.VMEM((targ_tiles + 1, side, rank), jnp.bfloat16),
            pltpu.VMEM((targ_tiles + 1, rank, side), jnp.bfloat16),
            pltpu.VMEM((comp_tiles + 1, side, rank), jnp.float32),
            pltpu.VMEM((targ_tiles + 1, rank, side), jnp.float32),
        ],
        compiler_params=pltpu.CompilerParams(vmem_limit_bytes=held + 4 * 2**20),
        name="tile_force",
    )(*slots_at, *comp_firsts, *comp_seconds, *targ_blocks, values, weight)
    return outs[0], outs[1], outs[2 : 2 + rows], outs[2 + rows :]


def swap(block, axis, offset):
    size = lax.axis_size(axis)
    return lax.ppermute(block, axis, [(i, i ^ offset) for i in range(size)])


def spread(block, axis):
    size = lax.axis_size(axis)
    seconds = [block] + [swap(block, axis, offset) for offset in range(2, size, 2)]
    return [each for second in seconds for each in (second, swap(second, axis, 1))]


def collect(blocks, axis):
    whole = blocks[0].astype(jnp.float32)
    for offset in range(2, len(blocks), 2):
        near = swap(blocks[offset + 1], axis, 1).astype(jnp.float32)
        far = (blocks[offset].astype(jnp.float32) + near).astype(blocks[offset].dtype)
        whole = whole + swap(far, axis, offset).astype(jnp.float32)
    return whole + swap(blocks[1], axis, 1).astype(jnp.float32)


def spread_pairs(block, axis):
    firsts = [block]
    firsts += [swap(block, axis, offset) for offset in range(2, lax.axis_size(axis), 2)]
    return firsts, [swap(block, axis, 1) for block in firsts]


def collect_pairs(keep, send, axis):
    got = swap(send, axis, 1)
    both = [
        keep[n].astype(jnp.float32) + got[n].astype(jnp.float32) for n in range(keep.shape[0])
    ]
    whole = both[0]
    for n, block in enumerate(both[1:]):
        whole = whole + swap(block.astype(keep.dtype), axis, 2 * n + 2).astype(jnp.float32)
    return whole


def body(
    compound_pos,
    compound_mom,
    target_pos,
    target_mom,
    tile_rows,
    tile_cols,
    tile_count,
    tile_values,
    tile_weight,
):
    cols, rows = lax.axis_size("col"), lax.axis_size("row")
    assert cols & (cols - 1) == 0 and rows & (rows - 1) == 0
    side = tile_values.shape[2]
    comp_per = compound_pos.shape[0] // side
    targ_per = target_pos.shape[0] // side
    col_index, row_index = lax.axis_index("col"), lax.axis_index("row")
    comp_local = tile_rows - row_index * (cols * comp_per)
    comp_place = (lax.div(comp_local, comp_per) ^ col_index) * comp_per
    comp_place += lax.rem(comp_local, comp_per)
    targ_place = (lax.div(tile_cols, targ_per * cols) ^ row_index) * targ_per
    targ_place += lax.rem(tile_cols, targ_per)
    alive = jnp.arange(tile_values.shape[1], dtype=jnp.int32)[None] < tile_count[0]
    spare = cols * comp_per * rows * targ_per
    pair = jnp.where(alive, comp_place * (rows * targ_per) + targ_place, spare)
    held = (tile_values[0], tile_weight[0], tile_count, pair)

    def forces(comp, targ):
        nonlocal held
        comp_keep, comp_send, targ_parts, kept = local_grads(
            held[2:],
            *spread_pairs(comp.astype(jnp.bfloat16), "col"),
            spread(targ.astype(jnp.bfloat16), "row"),
            *held[:2],
        )
        held = kept or held
        comp_sum = collect_pairs(comp_keep, comp_send, "col")
        targ_sum = collect(targ_parts, "row")
        return comp_sum - prior_weight * comp, targ_sum - prior_weight * targ

    places = (compound_pos, target_pos)
    speeds = (compound_mom, target_mom)
    push = forces(*places)
    for leap in range(LEAPS):
        scale = (0.5 if leap == 0 else 1.0) * step_size
        speeds = tuple(p + scale * f for p, f in zip(speeds, push))
        places = tuple(q + step_size * p for q, p in zip(places, speeds))
        push = forces(*places)
    speeds = tuple(p + 0.5 * step_size * f for p, f in zip(speeds, push))
    return (places[0], speeds[0], places[1], speeds[1])


def solution(mesh):
    split = P(("row", "col"), None)
    tiles = P(("row", "col"), None, None, None)
    return jax.shard_map(
        body,
        mesh=mesh,
        in_specs=(split,) * 6 + (P(("row", "col")), tiles, tiles),
        out_specs=(split,) * 4,
        check_vma=False,
    )
```
